512 devices in a mesh: vocab: 32 (over x, z), tok: 16 (over y, core).
Axes of the slice: x: 4, y: 8, z: 8, core: 2. Of those that a mesh axis runs over, the one named last changes fastest.
Arguments:
- embeddings: bfloat16 [131072, 4096], P('tok', 'vocab'), may hold values from -40 to 40
- norm_gain: bfloat16 [4096], P('vocab'), may hold values from 0.5 to 1.5
- query_key_value_weight: bfloat16 [4096, 32, 384], P('tok', 'vocab'), may hold values from -0.09375 to 0.09375
- out_weight: bfloat16 [4096, 4096], P('tok', 'vocab'), may hold values from -0.09375 to 0.09375
- dense_weight: bfloat16 [4096, 4096], P('tok', 'vocab'), may hold values from -2 to 2
- head_weight: bfloat16 [4096], P('vocab'), may hold values from -1 to 1
- token_ids: int32 [16, 128], P('tok'), may hold values from 0 to 131071, as said below
- replace_ids: int32 [16, 128], P('tok'), may hold values from 0 to 131071, as said below
- masked: int32 [16, 128], P('tok'), may hold values 0 or 1
- labels: int32 [16, 128], P('tok'), may hold values 0 or 1
- segments: int32 [16, 128], P('tok'), may hold values from 0 to 7, never falling along the last dimension, each value on 1 to 32 neighbouring positions
Outputs:
- table_grads: bfloat16 [131072, 4096], P('tok', 'vocab')
The draws below stay inside these ranges and needn't reach their ends.
Inputs may be any that keep to these rules, and one draw needn't show every extreme that they name: Ids are split into blocks of 8192 consecutive ids. At every position, token_ids and replace_ids lie in the same block. In each sequence at most 16 positions lie in any one block, and one block holds exactly 16 of them. `replace_ids`: see token_ids.
All inputs are finite; a program needn't handle non-finite values. No bound on the sum of `masked` or of `labels` on one device may be relied on, other than what follows from the above.
Results may differ from the reference program's by a relative error of at most 0.034.
Values may be sent and summed in bfloat16 or wider, within the bound.
A program may use at most 64 MiB of HBM per device.

```python
import math
import jax
import jax.numpy as jnp
import numpy as np
from jax import lax

D = 4096
HEADS = 32
HEAD_WIDTH = 128
VROWS = 8192
TOK_DEV = 128
SEQS = 16
VOCAB = 131072
CAP = 16
N_VOCAB = 32


def owner_blocks(key):
    key = jax.random.fold_in(key, 5)
    first_key, second_key = jax.random.split(key)
    hottest = jax.random.randint(first_key, (SEQS, 1), 0, SEQS)
    position = jnp.arange(TOK_DEV, dtype=jnp.int32)[None, :]
    spread_out = (hottest + 1 + (position - CAP) % (SEQS - 1)) % SEQS
    owner_tokens = jnp.where(position < CAP, hottest, spread_out)
    shuffle = jax.vmap(lambda row_key: jax.random.permutation(row_key, TOK_DEV))(jax.random.split(second_key, SEQS))
    return jnp.take_along_axis(owner_tokens, shuffle, axis=1)


def draw_token_ids(key, part):
    owner_tokens = owner_blocks(key)
    key = jax.random.fold_in(key, 7)
    offsets = jax.random.randint(key, (SEQS, TOK_DEV), 0, VROWS)
    return (owner_tokens * VROWS + offsets).astype(jnp.int32)


def draw_replace_ids(key, part):
    owner_tokens = owner_blocks(key)
    key = jax.random.fold_in(key, 9)
    offsets = jax.random.randint(key, (SEQS, TOK_DEV), 0, VROWS)
    return (owner_tokens * VROWS + offsets).astype(jnp.int32)


def draw_embeddings(key, part):
    key = jax.random.fold_in(key, 11)
    first_key, second_key = jax.random.split(key)
    column = jnp.arange(D, dtype=jnp.float32)[None, :] / D
    column_scale = jnp.exp(2.302585 * (column - 0.5))
    row_scale = jnp.exp(jax.random.uniform(second_key, (VOCAB, 1), jnp.float32, -0.7, 0.7))
    base_values = jnp.clip(jax.random.normal(first_key, (VOCAB, D), jnp.float32), -6.0, 6.0)
    return (base_values * column_scale * row_scale).astype(jnp.bfloat16)


def draw_dense_weight(key, part):
    key = jax.random.fold_in(key, 13)
    column = jnp.arange(D, dtype=jnp.float32)[None, :] / D
    rising = jnp.exp(1.3862944 * (column - 0.5))
    base_values = jnp.clip(jax.random.normal(key, (D, D), jnp.float32), -6.0, 6.0)
    return (base_values * rising / jnp.sqrt(jnp.float32(D))).astype(jnp.bfloat16)


def draw_head_weight(key, part):
    key = jax.random.fold_in(key, 17)
    column = jnp.arange(D, dtype=jnp.float32) / D
    rising = jnp.exp(1.3862944 * (column - 0.5))
    base_values = jax.random.uniform(key, (D,), jnp.float32, -0.4, 1.6)
    return (base_values * rising / jnp.sqrt(jnp.float32(D))).astype(jnp.bfloat16)


def set_ends(drawn, own_key, least, top_value):
    longest = drawn.shape.index(max(drawn.shape))
    spots = []
    for shift in (0, 1):
        where = [jax.random.randint(jax.random.fold_in(own_key, axis), (), 0, length) for axis, length in enumerate(drawn.shape)]
        where[longest] = (where[longest] + shift) % drawn.shape[longest]
        spots.append(tuple(where))
    return drawn.at[spots[0]].set(least).at[spots[1]].set(top_value)


def steps_of(own_key, dims, cuts, least, largest):
    level = 1.0
    for dim, blocks in cuts:
        draws = jax.random.uniform(jax.random.fold_in(jax.random.fold_in(own_key, 6), dim), (blocks,), jnp.float32, least / len(cuts), largest / len(cuts))
        level = level * jnp.repeat(jnp.exp(draws), dims[dim] // blocks).reshape((-1,) + (1,) * (len(dims) - 1 - dim))
    return level


def profile(amount, total, bound, slope):
    loads = [(1 << 20) // math.isqrt(rank ** slope) + 1 for rank in range(2, amount + 1)]
    rest, holding = total - bound - (amount - 1), [1] * (amount - 1)
    while rest > 0:
        candidates = [i for i in range(amount - 1) if holding[i] < bound]
        mass, budget = sum([loads[i] for i in candidates]), rest
        for i in candidates:
            extra = min(bound - holding[i], max(1, budget * loads[i] // mass), rest)
            holding[i] = holding[i] + extra
            rest = rest - extra
    return np.array([bound] + holding)


def uneven(key, number_of, total, limit, skew):
    if number_of == 2:
        one = jax.random.randint(key, (), max(1, total - limit), min(limit, total - 1) + 1)
        return jnp.stack([one, total - one])
    tallies = jnp.asarray(profile(number_of, total, limit, skew), jnp.int32)
    twos = (number_of - 1) // 2
    donor, sink = tallies[1:1 + 2 * twos:2], tallies[2:2 + 2 * twos:2]
    margin = jnp.minimum(donor - 1, limit - sink)
    passed = jax.random.randint(jax.random.fold_in(key, 1), (twos,), 0, 1 << 20) % (margin + 1)
    tallies = tallies.at[1:1 + 2 * twos:2].set(donor - passed).at[2:2 + 2 * twos:2].set(sink + passed)
    return tallies[jax.random.permutation(jax.random.fold_in(key, 2), number_of)]


def gaussian(key, dims, deviation, reach, cuts=(), held_as=jnp.bfloat16):
    loudness = steps_of(key, dims, cuts, -0.22, 0.18) if cuts else 1.0
    array = jax.random.normal(key, dims, jnp.float32) * deviation * loudness
    return jnp.minimum(jnp.maximum(array, -reach), reach).astype(held_as)


def setup_inputs(seed: int = 0) -> dict:
    key_of = jax.random.split(jax.random.key(seed), 12)
    embeddings = draw_embeddings(jax.random.fold_in(key_of[11], 71), 0)
    norm_gain = jnp.clip(1.0 + 0.1 * jax.random.normal(key_of[1], (D,), jnp.float32), 0.5, 1.5).astype(jnp.bfloat16)
    query_key_value_weight = gaussian(key_of[2], (D, HEADS, 3 * HEAD_WIDTH), D ** -0.5, 0.09375, ((0, 16), (1, 32)))
    out_weight = gaussian(key_of[3], (D, D), D ** -0.5, 0.09375, ((0, 16), (1, 32)))
    dense_weight = draw_dense_weight(jax.random.fold_in(key_of[11], 71), 0)
    head_weight = draw_head_weight(jax.random.fold_in(key_of[11], 71), 0)
    token_ids = draw_token_ids(jax.random.fold_in(key_of[11], 71), 0)
    replace_ids = draw_replace_ids(jax.random.fold_in(key_of[11], 71), 0)
    masked = set_ends((jax.random.randint(key_of[8], (SEQS, TOK_DEV), 0, 100) < 15).astype(jnp.int32), jax.random.fold_in(key_of[8], 1), 0, 1)
    labels = set_ends((jax.random.randint(key_of[9], (SEQS, TOK_DEV), 0, 2) < 1).astype(jnp.int32), jax.random.fold_in(key_of[9], 1), 0, 1)
    segments = jax.vmap(lambda own: jnp.searchsorted(jnp.cumsum(uneven(own, 8, TOK_DEV, TOK_DEV // 4, 0)), jnp.arange(TOK_DEV), side="right"))(jax.random.split(key_of[10], SEQS)).reshape((SEQS, TOK_DEV)).astype(jnp.int32)
    return dict(embeddings=embeddings, norm_gain=norm_gain, query_key_value_weight=query_key_value_weight, out_weight=out_weight, dense_weight=dense_weight, head_weight=head_weight, token_ids=token_ids, replace_ids=replace_ids, masked=masked, labels=labels, segments=segments)


soft_limit = 50.0
loss_scale = 64.0
epsilon = 1e-05
inv_root_two = 0.7071067811865476
inv_root_tau = 0.3989422804014327

def rounded(value):
    return lax.optimization_barrier(value.astype(jnp.bfloat16)).astype(jnp.float32)

def attend(queries, key_rows, same_segment):
    raw_scores = jnp.einsum('qhd,khd->hqk', queries.astype(jnp.float32), key_rows.astype(jnp.float32)) / math.sqrt(HEAD_WIDTH)
    capped = soft_limit * jnp.tanh(raw_scores / soft_limit)
    exps = jnp.where(same_segment[None], jnp.exp(capped), 0.0)
    probabilities = exps / lax.optimization_barrier(jnp.sum(exps, axis=-1, keepdims=True))
    return (capped, probabilities)

def split_parts(query_key_value_rows):
    return (query_key_value_rows[:, :, :HEAD_WIDTH], query_key_value_rows[:, :, HEAD_WIDTH:2 * HEAD_WIDTH], query_key_value_rows[:, :, 2 * HEAD_WIDTH:])

def forward_heads(packed):
    query_key_value_rows, segment_row = packed
    queries, key_rows, value_rows = split_parts(query_key_value_rows)
    same_segment = segment_row[:, None] == segment_row[None, :]
    capped, probabilities = attend(queries, key_rows, same_segment)
    prob_rounded = probabilities.astype(jnp.bfloat16)
    return jnp.einsum('hqk,khd->qhd', prob_rounded.astype(jnp.float32), value_rows.astype(jnp.float32)).astype(jnp.bfloat16)

def backward_heads(packed):
    query_key_value_rows, segment_row, out_rows = packed
    queries, key_rows, value_rows = split_parts(query_key_value_rows)
    same_segment = segment_row[:, None] == segment_row[None, :]
    capped, probabilities = attend(queries, key_rows, same_segment)
    prob_rounded = probabilities.astype(jnp.bfloat16).astype(jnp.float32)
    out_float = out_rows.astype(jnp.float32)
    prob_grads = jnp.einsum('qhd,khd->hqk', out_float, value_rows.astype(jnp.float32))
    value_grads = jnp.einsum('hqk,qhd->khd', prob_rounded, out_float)
    capped_grads = probabilities * (prob_grads - lax.optimization_barrier(jnp.sum(probabilities * prob_grads, axis=-1, keepdims=True)))
    ratio = capped / soft_limit
    score_grads = capped_grads * (1.0 - ratio * ratio) / math.sqrt(HEAD_WIDTH)
    score_rounded = score_grads.astype(jnp.bfloat16).astype(jnp.float32)
    query_grads = jnp.einsum('hqk,khd->qhd', score_rounded, key_rows.astype(jnp.float32))
    key_grads = jnp.einsum('hqk,qhd->khd', score_rounded, queries.astype(jnp.float32))
    return jnp.concatenate([query_grads, key_grads, value_grads], axis=-1).astype(jnp.bfloat16)

def reference(embeddings, norm_gain, query_key_value_weight, out_weight, dense_weight, head_weight, token_ids, replace_ids, masked, labels, segments):
    chosen = jnp.where(masked == 1, replace_ids, token_ids).astype(jnp.int32)
    inputs = jnp.take(embeddings, chosen, axis=0)
    features = inputs.astype(jnp.float32)
    row_mean = lax.optimization_barrier(jnp.mean(features, axis=-1, keepdims=True))
    variance = lax.optimization_barrier(jnp.mean(features * features, axis=-1, keepdims=True)) - row_mean * row_mean
    inv_std = lax.rsqrt(variance + epsilon)
    centered = (features - row_mean) * inv_std
    gain = norm_gain.astype(jnp.float32)
    norm_output = (centered * gain).astype(jnp.bfloat16)
    query_key_value = jnp.einsum('ykz,zbi->ykbi', norm_output.astype(jnp.float32), query_key_value_weight.astype(jnp.float32)).astype(jnp.bfloat16)
    head_values = lax.map(forward_heads, (query_key_value, segments))
    positions = SEQS * TOK_DEV
    head_flat = head_values.reshape(positions, D)
    hidden = features.reshape(positions, D) + jnp.dot(head_flat, out_weight, preferred_element_type=jnp.float32)
    hidden_narrow = hidden.astype(jnp.bfloat16)
    dense_linear = jnp.dot(hidden_narrow, dense_weight, preferred_element_type=jnp.float32)
    activated = jax.nn.gelu(dense_linear, approximate=False)
    head_mean = lax.optimization_barrier(jnp.mean(activated, axis=-1, keepdims=True))
    head_variance = lax.optimization_barrier(jnp.mean(activated * activated, axis=-1, keepdims=True)) - head_mean * head_mean
    head_scale = lax.rsqrt(head_variance + epsilon)
    head_centered = (activated - head_mean) * head_scale
    head_vector = head_weight.astype(jnp.float32)
    logits = lax.optimization_barrier(jnp.sum(head_centered * head_vector[None, :], axis=-1))
    logit_grads = loss_scale * (jax.nn.sigmoid(logits) - labels.reshape(positions).astype(jnp.float32))
    centered_grads = logit_grads[:, None] * head_vector[None, :]
    mean_grads = lax.optimization_barrier(jnp.mean(centered_grads, axis=-1, keepdims=True))
    mean_product = lax.optimization_barrier(jnp.mean(centered_grads * head_centered, axis=-1, keepdims=True))
    activated_grads = head_scale * (centered_grads - mean_grads - head_centered * mean_product)
    gelu_slope = 0.5 * (1.0 + lax.erf(dense_linear * inv_root_two)) + dense_linear * jnp.exp(-0.5 * dense_linear * dense_linear) * inv_root_tau
    pre_grads = (activated_grads * gelu_slope).astype(jnp.bfloat16)
    block_width = D // N_VOCAB
    hidden_grads = jnp.zeros((positions, D), jnp.float32)
    for block_index in range(N_VOCAB):
        begin_at = block_index * block_width
        end_at = begin_at + block_width
        partial_value = jnp.dot(pre_grads[:, begin_at:end_at], dense_weight[:, begin_at:end_at].T, preferred_element_type=jnp.float32)
        hidden_grads = hidden_grads + rounded(partial_value)
    hidden_rounded = hidden_grads.astype(jnp.bfloat16)
    total_sum = jnp.zeros((positions, D), jnp.float32)
    for block_index in range(N_VOCAB):
        begin_at = block_index * block_width
        end_at = begin_at + block_width
        partial_value = jnp.dot(hidden_rounded[:, begin_at:end_at], out_weight[:, begin_at:end_at].T, preferred_element_type=jnp.float32)
        total_sum = total_sum + rounded(partial_value)
    out_grads = total_sum.astype(jnp.bfloat16).reshape(SEQS, TOK_DEV, HEADS, HEAD_WIDTH)
    qkv_grads = lax.map(backward_heads, (query_key_value, segments, out_grads))
    grads_flat = qkv_grads.reshape(positions, HEADS, 3 * HEAD_WIDTH)
    heads_block = HEADS // N_VOCAB
    norm_grads = jnp.zeros((positions, D), jnp.float32)
    for block_index in range(N_VOCAB):
        begin_at = block_index * heads_block
        end_at = begin_at + heads_block
        partial_value = jnp.einsum('nhe,dhe->nd', grads_flat[:, begin_at:end_at].astype(jnp.float32), query_key_value_weight[:, begin_at:end_at].astype(jnp.float32))
        norm_grads = norm_grads + rounded(partial_value)
    centered_flat = centered.reshape(positions, D)
    scaled = norm_grads * gain[None, :]
    mean_scaled = lax.optimization_barrier(jnp.mean(scaled, axis=-1, keepdims=True))
    mean_weighted = lax.optimization_barrier(jnp.mean(scaled * centered_flat, axis=-1, keepdims=True))
    input_grads = hidden_grads + inv_std.reshape(positions, 1) * (scaled - mean_scaled - centered_flat * mean_weighted)
    chosen_flat = chosen.reshape(positions)

    def owner_rows(owner_index):
        local_rows = chosen_flat - owner_index * VROWS
        inside = (local_rows >= 0) & (local_rows < VROWS)
        row_index = jnp.where(inside, local_rows, 0).astype(jnp.int32)
        contrib = jnp.where(inside[:, None], input_grads, 0.0)
        return jnp.zeros((VROWS, D), jnp.float32).at[row_index].add(contrib).astype(jnp.bfloat16)
    table_grads = lax.map(owner_rows, jnp.arange(SEQS, dtype=jnp.int32))
    return table_grads.reshape(VOCAB, D)
```

```python
import functools
import math

import jax
import jax.numpy as jnp
from jax import lax
from jax.experimental import pallas as pl
from jax.experimental.pallas import tpu as pltpu
from jax.sharding import PartitionSpec as P

MESH = pl.DeviceIdType.MESH
BF = jnp.bfloat16
F32 = jnp.float32
B = 128

soft_limit = 50.0
loss_scale = 64.0
epsilon = 1e-05
inv_root_two = 0.7071067811865476
inv_root_tau = 0.3989422804014327


def dot(a, b):
    return jnp.dot(a, b, preferred_element_type=F32)


def dot_nt(a, b):
    return lax.dot_general(a, b, (((1,), (1,)), ((), ())), preferred_element_type=F32)


def dot_tn(a, b):
    return lax.dot_general(a, b, (((0,), (0,)), ((), ())), preferred_element_type=F32)


def iota(shape, dim):
    return lax.broadcasted_iota(jnp.int32, shape, dim)


def columns_to_rows(columns):
    lane = iota((B, B), 1)
    total = jnp.zeros((B, B), F32)
    for i, column in enumerate(columns):
        total = jnp.where(lane == i, column, total)
    return total.T[:8]


def rows_to_square(rows):
    return jnp.concatenate([rows, jnp.zeros((B - 8, B), F32)], axis=0).T


def row_to_square(row):
    return jnp.broadcast_to(row, (B, B)).T


def main_kernel(
    X, Z, Y, C, vocab_rows,
    emb_hbm, gain_ref, wq_ref, wo_ref, wd_ref, hw_ref,
    tok_ref, rep_ref, mask_ref, lab_ref, seg_ref,
    grad_out, req_out,
    emb, wod_src, Wq, Wod,
    ids_src, ids_buf, row_src, row_buf, gslot_src, gslot_buf,
    x_src, x_buf, h_src, h_buf, d_src, d_buf,
    pq, pq_buf, po, po_buf, pd, pd_buf,
    pre_buf, b1, b1_buf, hr_buf, b2, b2_buf, g_buf, b3, b3_buf,
    nrm, ar_src, ar_buf,
    emb_sem, w1q_sem, w1o_sem, w1_send, w2_recv, w2_send, sib_recv, sib_send,
    t_recv, t_send, e_recv, e_send, e0_send, rx_recv, rx_send, ax_recv, ax_send,
    r_recv, r_send, s_recv, s_send,
):
    V, T = X * Z, Y * C
    Xc = X // C
    D = V * B
    K = Z * B
    v, t = lax.axis_index("vocab"), lax.axis_index("tok")
    x, z = v // Z, v % Z
    y, c = t // C, t % C
    cap = 2 * B // T
    R = T * cap

    def dev(xx, zz, yy, cc):
        return (xx * Z + zz, yy * C + cc)

    def remote(src, dst, send, recv, device):
        return pltpu.make_async_remote_copy(
            src_ref=src, dst_ref=dst, send_sem=send, recv_sem=recv,
            device_id=device, device_id_type=MESH,
        )

    def wait_bytes(ref, sem):
        pltpu.make_async_copy(ref, ref, sem).wait()

    emb_copy = pltpu.make_async_copy(emb_hbm, emb, emb_sem)
    emb_copy.start()
    barrier = pltpu.get_barrier_semaphore()

    def greet_vocab(d, carry):
        pl.semaphore_signal(barrier, inc=1, device_id=((v + d) % V, t), device_id_type=MESH)
        return carry

    def greet_tok(d, carry):
        pl.semaphore_signal(barrier, inc=1, device_id=(v, (t + d) % T), device_id_type=MESH)
        return carry

    lax.fori_loop(1, V, greet_vocab, 0)
    lax.fori_loop(1, T, greet_tok, 0)
    same_core = (x // Xc) == c

    @pl.when(jnp.logical_not(same_core))
    def _():
        for i in range(Xc):
            pl.semaphore_signal(
                barrier, inc=1, device_id=dev(Xc * c + i, z, y, x // Xc), device_id_type=MESH
            )

    wod_src[:, 0:B] = wo_ref[...]
    wod_src[:, B : 2 * B] = wd_ref[...]
    chosen = jnp.where(mask_ref[...] == 1, rep_ref[...], tok_ref[...])
    owner = chosen // vocab_rows
    offset = (chosen - owner * vocab_rows).astype(F32)
    owner_f = owner.astype(F32)
    earlier = iota((B, B), 0) < iota((B, B), 1)
    same_owner = row_to_square(owner_f) == owner_f
    slot = jnp.sum(jnp.where(same_owner & earlier, 1.0, 0.0), axis=0, keepdims=True)
    place = owner_f * float(cap) + slot
    place_hot = iota((R, B), 0).astype(F32) == place
    wanted = jnp.sum(jnp.where(place_hot, offset, 0.0), axis=1, keepdims=True)
    ids_src[...] = jnp.broadcast_to(wanted, (R, B)).reshape(T, cap, B)
    put_hot = jnp.where(place_hot, 1.0, 0.0).astype(BF)

    peers = V - 1 + T - 1

    @pl.when(same_core)
    def _():
        pl.semaphore_wait(barrier, peers)

    @pl.when(jnp.logical_not(same_core))
    def _():
        pl.semaphore_wait(barrier, peers + Xc)

    def tok_start(src, buf, n):
        buf[t] = src[t]

        def send(d, carry):
            to = (t + d) % T
            remote(src.at[to], buf.at[t], t_send.at[n], t_recv.at[n], (v, to)).start()
            return carry

        lax.fori_loop(1, T, send, 0)

    def tok_wait(src, buf, n):
        wait_bytes(buf.at[pl.ds(0, T - 1)], t_recv.at[n])

    def tok_done(src, buf, n):
        wait_bytes(src.at[pl.ds(0, T - 1)], t_send.at[n])

    tok_start(ids_src, ids_buf, 0)

    def w1_each(act):
        for i in range(Xc):
            xd, cd = Xc * c + i, x // Xc
            mine = (xd == x) & same_core
            rows = pl.ds(i * B, B)
            dst_rows = pl.ds(pl.multiple_of(y * B, B), B)
            q = (wq_ref.at[rows], Wq.at[x, dst_rows], w1q_sem)
            o = (wod_src.at[rows], Wod.at[x, dst_rows], w1o_sem)
            for a, (src, dst, sem) in enumerate((q, o)):
                act(mine, src, dst, sem, w1_send.at[i, a], dev(xd, z, y, cd))

    def w1_go(mine, src, dst, sem, send, device):
        @pl.when(mine)
        def _():
            pltpu.make_async_copy(src, dst, sem).start()

        @pl.when(jnp.logical_not(mine))
        def _():
            remote(src, dst, send, sem, device).start()

    def w1_end(mine, src, dst, sem, send, device):
        @pl.when(jnp.logical_not(mine))
        def _():
            wait_bytes(src, send)

    w1_each(w1_go)

    arrays = (Wq, Wod)
    right_hops, left_hops = Y // 2, Y - 1 - Y // 2

    def slab(a, k):
        return arrays[a].at[pl.ds(Xc * c, Xc), pl.ds(pl.multiple_of(k * B, B), B)]

    def hop(a, h, way):
        step = 1 if way == 0 else Y - 1
        k = (y + (Y - step) * (h - 1)) % Y
        ref = slab(a, k)
        return remote(
            ref, ref, w2_send.at[a, way, h - 1], w2_recv.at[a, way, h - 1],
            dev(x, z, (y + step) % Y, c),
        )

    def sibling(a, k, n):
        ref = slab(a, k)
        return remote(ref, ref, sib_send.at[a, n], sib_recv.at[a, n], dev(x, z, y, (c + 1) % C))

    def hops_of(way):
        return right_hops if way == 0 else left_hops

    def arrived(h, way):
        step = 1 if way == 0 else Y - 1
        return (y + (Y - step) * h) % Y

    def w2_begin(a):
        wait_bytes(arrays[a].at[pl.ds(0, Xc), pl.ds(0, B)], (w1q_sem, w1o_sem)[a])
        for way in (0, 1):
            if hops_of(way) >= 1:
                hop(a, 1, way).start()
        sibling(a, y, 0).start()

    def sib_slot(h, way):
        return h if way == 0 else right_hops + h

    def w2_forward(a, h):
        for way in (0, 1):
            if h <= hops_of(way):
                hop(a, h, way).wait_recv()
                if h + 1 <= hops_of(way):
                    hop(a, h + 1, way).start()
                sibling(a, arrived(h, way), sib_slot(h, way)).start()

    def w2_ready(a):
        for n in range(Y):
            wait_bytes(arrays[a].at[pl.ds(0, Xc), pl.ds(0, B)], sib_recv.at[a, n])

    def w2_done(a):
        for way in (0, 1):
            for h in range(1, hops_of(way) + 1):
                hop(a, h, way).wait_send()
        for n in range(Y):
            wait_bytes(arrays[a].at[pl.ds(0, Xc), pl.ds(0, B)], sib_send.at[a, n])

    row = z % X
    at_home = x == row

    def row_start(src, buf, n):
        k = v // X
        for j in list(range(1, Z)):
            remote(src, buf.at[k], e_send.at[n], e_recv.at[n], dev(row, (z + j) % Z, y, c)).start()

        @pl.when(at_home)
        def _():
            pltpu.make_async_copy(src, buf.at[k], e_recv.at[n]).start()

        @pl.when(jnp.logical_not(at_home))
        def _():
            remote(src, buf.at[k], e0_send.at[n], e_recv.at[n], dev(row, z, y, c)).start()

    def row_wait(src, buf, n):
        wait_bytes(buf, e_recv.at[n])

    def row_done(src, buf, n):
        wait_bytes(buf.at[pl.ds(0, Z - 1)], e_send.at[n])

        @pl.when(jnp.logical_not(at_home))
        def _():
            wait_bytes(src, e0_send.at[n])

    def rx_start(part, buf, n):
        for d in range(1, X):
            to = (x + d) % X
            remote(
                part.at[to], buf.at[d - 1], rx_send.at[n], rx_recv.at[n], dev(to, z, y, c)
            ).start()

    def rx_sum(part, buf, n):
        wait_bytes(buf, rx_recv.at[n])
        total = part[x].astype(F32)
        for d in range(1, X):
            total = total + buf[d - 1].astype(F32)
        return total

    def ax_start(buf, n):
        for d in range(1, X):
            remote(
                buf.at[x], buf.at[x], ax_send.at[n], ax_recv.at[n], dev((x + d) % X, z, y, c)
            ).start()

    def ax_wait(buf, n):
        wait_bytes(buf.at[pl.ds(0, X - 1)], ax_recv.at[n])

    def own_start(part, buf, k, n):
        to = X * k + x
        mine = to == v

        @pl.when(mine)
        def _():
            pltpu.make_async_copy(part.at[k], buf.at[z], r_recv.at[n]).start()

        @pl.when(jnp.logical_not(mine))
        def _():
            remote(part.at[k], buf.at[z], r_send.at[n, k], r_recv.at[n], (to, t)).start()

    def own_sum(buf, n):
        wait_bytes(buf, r_recv.at[n])
        total = buf[0].astype(F32)
        for k in range(1, Z):
            total = total + buf[k].astype(F32)
        return total

    def own_done(part, n):
        for k in range(Z):
            @pl.when(X * k + x != v)
            def _():
                wait_bytes(part.at[k], r_send.at[n, k])

    def spread_back(left, weights, part, buf, n):
        step = 2
        for first in range(0, Z, step):
            total = None
            for xx in range(X):
                term = dot_nt(left(xx), weights(xx, pl.ds(first * B, step * B)))
                total = term if total is None else total + term
            for k in range(first, first + step):
                part[k] = total[:, (k - first) * B : (k - first + 1) * B].astype(BF)
                own_start(part, buf, k, n)

    def ar_start(rows, n):
        ar_src[n] = rows
        ar_buf[n, 0] = rows

        def send(d, carry):
            remote(
                ar_src.at[n], ar_buf.at[n, d], s_send.at[n], s_recv.at[n], ((v + d) % V, t)
            ).start()
            return carry

        lax.fori_loop(1, V, send, 0)

    def ar_sum(n):
        wait_bytes(ar_buf.at[n, pl.ds(1, V - 1)], s_recv.at[n])
        return rows_to_square(jnp.sum(ar_buf[n], axis=0))

    def ar_done(n):
        wait_bytes(ar_buf.at[n, pl.ds(1, V - 1)], s_send.at[n])

    place_square = row_to_square(place)
    take_hot = jnp.concatenate(
        [
            jnp.where(place_square == (iota((B, B), 1) + first).astype(F32), 1.0, 0.0)
            for first in range(0, R, B)
        ],
        axis=1,
    ).astype(BF)
    emb_copy.wait()
    tok_wait(ids_src, ids_buf, 0)
    requested = ids_buf[...].reshape(R, B)
    chunk = 512

    def fetch(i, total):
        base = i * chunk
        hot = jnp.concatenate(
            [
                jnp.where(
                    requested == (iota((R, B), 1) + (base + first)).astype(F32), 1.0, 0.0
                ).astype(BF)
                for first in range(0, chunk, B)
            ],
            axis=1,
        )
        return total + dot(hot, emb[pl.ds(pl.multiple_of(base, chunk), chunk), :])

    fetched = lax.fori_loop(0, vocab_rows // chunk, fetch, jnp.zeros((R, B), F32))
    row_src[...] = fetched.astype(BF).reshape(T, cap, B)
    tok_start(row_src, row_buf, 1)
    w2_begin(0)
    for first in range(0, R, B):
        req_out[:, first : first + B] = requested[first : first + B].T[:8]
    w2_forward(0, 1)
    tok_wait(row_src, row_buf, 1)
    inputs = dot(take_hot, row_buf[...].reshape(R, B))
    features = inputs
    gain = gain_ref[...].astype(F32)
    x_src[0:B, :] = inputs.astype(BF)
    x_src[B : B + 16, :] = jnp.broadcast_to(gain_ref[...].astype(F32), (16, B)).astype(BF)
    row_start(x_src, x_buf, 0)
    ar_start(
        columns_to_rows(
            [
                jnp.sum(features, axis=1, keepdims=True),
                jnp.sum(features * features, axis=1, keepdims=True),
            ]
        ),
        0,
    )
    w2_forward(0, 2)
    stats = ar_sum(0)
    row_mean = stats[:, 0:1] / D
    variance = stats[:, 1:2] / D - row_mean * row_mean
    inv_std = lax.rsqrt(variance + epsilon)
    centered = (features - row_mean) * inv_std
    w2_forward(0, 3)
    row_wait(x_src, x_buf, 0)
    for k in range(Z):
        block = x_buf[k, 0:B, :].astype(F32)
        block_gain = x_buf[k, B : B + 16, :].astype(F32)[0:1]
        nrm[:, k * B : (k + 1) * B] = (((block - row_mean) * inv_std) * block_gain).astype(BF)
    w2_forward(0, 4)
    w2_begin(1)
    w2_ready(0)

    for xx in range(X):
        pq[xx] = dot(nrm[...], Wq[xx]).astype(BF)
    rx_start(pq, pq_buf, 0)
    w2_forward(1, 1)
    qkv = rx_sum(pq, pq_buf, 0).astype(BF)
    queries, keys, values = qkv[:, :B], qkv[:, B : 2 * B], qkv[:, 2 * B :]
    segment_f = seg_ref[...].astype(F32)
    same_segment = row_to_square(segment_f) == segment_f
    raw = dot_nt(queries, keys) / math.sqrt(B)
    capped = soft_limit * jnp.tanh(raw / soft_limit)
    exps = jnp.where(same_segment, jnp.exp(capped), 0.0)
    probabilities = exps / jnp.sum(exps, axis=-1, keepdims=True)
    prob_rounded = probabilities.astype(BF)
    h_src[...] = dot(prob_rounded, values).astype(BF)
    row_start(h_src, h_buf, 1)
    w2_forward(1, 2)
    w2_forward(1, 3)
    w2_forward(1, 4)
    row_wait(h_src, h_buf, 1)
    w2_ready(1)

    heads_row = jnp.concatenate([h_buf[k] for k in range(Z)], axis=1)
    for xx in range(X):
        po[xx] = dot(heads_row, Wod[xx, :, 0:B]).astype(po.dtype)
    rx_start(po, po_buf, 1)
    hidden = features + rx_sum(po, po_buf, 1)
    d_src[...] = hidden.astype(BF)
    row_start(d_src, d_buf, 2)
    row_wait(d_src, d_buf, 2)

    dense_row = jnp.concatenate([d_buf[k] for k in range(Z)], axis=1)
    for xx in range(X):
        pd[xx] = dot(dense_row, Wod[xx, :, B : 2 * B]).astype(pd.dtype)
    rx_start(pd, pd_buf, 2)
    dense_linear = rx_sum(pd, pd_buf, 2)
    phi = 0.5 * (1.0 + lax.erf(dense_linear * inv_root_two))
    activated = dense_linear * phi
    head_vector = hw_ref[...].astype(F32)
    ar_start(
        columns_to_rows(
            [
                jnp.sum(activated, axis=1, keepdims=True),
                jnp.sum(activated * activated, axis=1, keepdims=True),
                jnp.sum(activated * head_vector, axis=1, keepdims=True),
                jnp.broadcast_to(jnp.sum(head_vector, axis=1, keepdims=True), (B, 1)),
            ]
        ),
        1,
    )
    gelu_slope = phi + dense_linear * jnp.exp(-0.5 * dense_linear * dense_linear) * inv_root_tau
    labels = row_to_square(lab_ref[...].astype(F32))[:, 0:1]
    stats = ar_sum(1)
    head_mean = stats[:, 0:1] / D
    head_scale = lax.rsqrt(stats[:, 1:2] / D - head_mean * head_mean + epsilon)
    weight_sum = stats[:, 3:4]
    logits = head_scale * (stats[:, 2:3] - head_mean * weight_sum)
    logit_grads = loss_scale * (jax.nn.sigmoid(logits) - labels)
    head_centered = (activated - head_mean) * head_scale
    mean_grads = logit_grads * weight_sum / D
    mean_product = logit_grads * logits / D
    activated_grads = head_scale * (
        logit_grads * head_vector - mean_grads - head_centered * mean_product
    )
    pre_buf[x] = (activated_grads * gelu_slope).astype(BF)
    ax_start(pre_buf, 0)
    ax_wait(pre_buf, 0)
    spread_back(
        lambda xx: pre_buf[xx], lambda xx, rows: Wod[xx, rows, B : 2 * B], b1, b1_buf, 0
    )
    hidden_grads = own_sum(b1_buf, 0)
    hr_buf[x] = hidden_grads.astype(BF)
    ax_start(hr_buf, 1)
    ax_wait(hr_buf, 1)
    spread_back(lambda xx: hr_buf[xx], lambda xx, rows: Wod[xx, rows, 0:B], b2, b2_buf, 1)
    out_rounded = own_sum(b2_buf, 1).astype(BF)

    prob_grads = dot_nt(out_rounded, values)
    value_grads = dot_tn(prob_rounded, out_rounded)
    capped_grads = probabilities * (
        prob_grads - jnp.sum(probabilities * prob_grads, axis=-1, keepdims=True)
    )
    ratio = capped / soft_limit
    score_rounded = (capped_grads * (1.0 - ratio * ratio) / math.sqrt(B)).astype(BF)
    query_grads = dot(score_rounded, keys)
    key_grads = dot_tn(score_rounded, queries)
    g_buf[x] = jnp.concatenate([query_grads, key_grads, value_grads], axis=1).astype(BF)
    ax_start(g_buf, 2)
    ax_wait(g_buf, 2)
    spread_back(lambda xx: g_buf[xx], lambda xx, rows: Wq[xx, rows, :], b3, b3_buf, 2)
    scaled = own_sum(b3_buf, 2) * gain
    ar_start(
        columns_to_rows(
            [
                jnp.sum(scaled, axis=1, keepdims=True),
                jnp.sum(scaled * centered, axis=1, keepdims=True),
            ]
        ),
        2,
    )
    stats = ar_sum(2)
    input_grads = hidden_grads + inv_std * (
        scaled - stats[:, 0:1] / D - centered * (stats[:, 1:2] / D)
    )

    gslot_src[...] = dot(put_hot, input_grads.astype(BF)).astype(BF).reshape(T, cap, B)
    tok_start(gslot_src, gslot_buf, 2)
    tok_wait(gslot_src, gslot_buf, 2)
    grad_out[...] = gslot_buf[...].reshape(R, B)

    tok_done(ids_src, ids_buf, 0)
    tok_done(row_src, row_buf, 1)
    tok_done(gslot_src, gslot_buf, 2)
    w1_each(w1_end)
    w2_done(0)
    w2_done(1)
    row_done(x_src, x_buf, 0)
    row_done(h_src, h_buf, 1)
    row_done(d_src, d_buf, 2)
    for n, buf in enumerate((pq_buf, po_buf, pd_buf)):
        wait_bytes(buf, rx_send.at[n])
    for n, buf in enumerate((pre_buf, hr_buf, g_buf)):
        wait_bytes(buf.at[pl.ds(0, X - 1)], ax_send.at[n])
    for n, part in enumerate((b1, b2, b3)):
        own_done(part, n)
    for n in range(3):
        ar_done(n)


def table_kernel(tile, grad_ref, req_ref, out_ref):
    base = pl.program_id(0) * tile
    hot = jnp.where(
        (iota((tile, req_ref.shape[1]), 0) + base).astype(F32) == req_ref[0:1, :], 1.0, 0.0
    ).astype(BF)
    out_ref[...] = dot(hot, grad_ref[...]).astype(BF)


def local(
    X, Z, Y, C,
    embeddings, norm_gain, query_key_value_weight, out_weight, dense_weight, head_weight,
    token_ids, replace_ids, masked, labels, segments,
):
    vocab_rows = embeddings.shape[0]
    V, T = X * Z, Y * C
    cap = 2 * B // T
    R = T * cap
    vm = pl.BlockSpec(memory_space=pltpu.VMEM)
    dma = pltpu.SemaphoreType.DMA
    rows = query_key_value_weight.shape[0]
    VM = pltpu.VMEM
    right = Y // 2
    grads, requests = pl.pallas_call(
        functools.partial(main_kernel, X, Z, Y, C, vocab_rows),
        out_shape=(
            jax.ShapeDtypeStruct((R, B), BF),
            jax.ShapeDtypeStruct((8, R), F32),
        ),
        in_specs=[pl.BlockSpec(memory_space=pl.ANY)] + [vm] * 10,
        out_specs=(vm, vm),
        scratch_shapes=[
            VM((vocab_rows, B), BF),
            VM((rows, 2 * B), BF),
            VM((X, Z * B, 3 * B), BF),
            VM((X, Z * B, 2 * B), BF),
            VM((T, cap, B), F32), VM((T, cap, B), F32),
            VM((T, cap, B), BF), VM((T, cap, B), BF),
            VM((T, cap, B), BF), VM((T, cap, B), BF),
            VM((B + 16, B), BF), VM((Z, B + 16, B), BF),
            VM((B, B), BF), VM((Z, B, B), BF),
            VM((B, B), BF), VM((Z, B, B), BF),
            VM((X, B, 3 * B), BF), VM((X - 1, B, 3 * B), BF),
            VM((X, B, B), F32), VM((X - 1, B, B), F32),
            VM((X, B, B), F32), VM((X - 1, B, B), F32),
            VM((X, B, B), BF), VM((Z, B, B), BF), VM((Z, B, B), BF),
            VM((X, B, B), BF), VM((Z, B, B), BF), VM((Z, B, B), BF),
            VM((X, B, 3 * B), BF), VM((Z, B, B), BF), VM((Z, B, B), BF),
            VM((B, Z * B), BF),
            VM((3, 8, B), F32), VM((3, V, 8, B), F32),
            dma(()), dma(()), dma(()), dma((X // C, 2)),
            dma((2, 2, right)), dma((2, 2, right)), dma((2, Y)), dma((2, Y)),
            dma((3,)), dma((3,)), dma((3,)), dma((3,)), dma((3,)),
            dma((3,)), dma((3,)), dma((3,)), dma((3,)),
            dma((3,)), dma((3, Z)), dma((3,)), dma((3,)),
        ],
        compiler_params=pltpu.CompilerParams(
            collective_id=0, has_side_effects=True, vmem_limit_bytes=40 * 1024 * 1024
        ),
    )(
        embeddings,
        norm_gain.reshape(1, B),
        query_key_value_weight.reshape(rows, 3 * B),
        out_weight,
        dense_weight,
        head_weight.reshape(1, B),
        token_ids, replace_ids, masked, labels, segments,
    )
    tile = min(1024, vocab_rows)
    return pl.pallas_call(
        functools.partial(table_kernel, tile),
        grid=(vocab_rows // tile,),
        out_shape=jax.ShapeDtypeStruct((vocab_rows, B), BF),
        in_specs=[
            pl.BlockSpec((R, B), lambda i: (0, 0)),
            pl.BlockSpec((8, R), lambda i: (0, 0)),
        ],
        out_specs=pl.BlockSpec((tile, B), lambda i: (i, 0)),
    )(grads, requests)


def solution(mesh):
    V, T = mesh.shape["vocab"], mesh.shape["tok"]
    X = 4 if V == 32 else 2
    C = 2
    placed = (
        P("tok", "vocab"),
        P("vocab"),
        P("tok", "vocab", None),
        P("tok", "vocab"),
        P("tok", "vocab"),
        P("vocab"),
        P("tok", None),
        P("tok", None),
        P("tok", None),
        P("tok", None),
        P("tok", None),
    )
    return jax.shard_map(
        functools.partial(local, X, V // X, T // C, C),
        mesh=mesh, in_specs=placed, out_specs=P("tok", "vocab"), check_vma=False,
    )
```

```python
import functools
import math

import jax
import jax.numpy as jnp
from jax import lax
from jax.experimental import pallas as pl
from jax.experimental.pallas import tpu as pltpu
from jax.sharding import PartitionSpec as P

MESH = pl.DeviceIdType.MESH
BF = jnp.bfloat16
F32 = jnp.float32
B = 128

soft_limit = 50.0
loss_scale = 64.0
epsilon = 1e-05
inv_root_two = 0.7071067811865476
inv_root_tau = 0.3989422804014327


def dot(a, b):
    return jnp.dot(a, b, preferred_element_type=F32)


def dot_nt(a, b):
    return lax.dot_general(a, b, (((1,), (1,)), ((), ())), preferred_element_type=F32)


def dot_tn(a, b):
    return lax.dot_general(a, b, (((0,), (0,)), ((), ())), preferred_element_type=F32)


def iota(shape, dim):
    return lax.broadcasted_iota(jnp.int32, shape, dim)


def columns_to_rows(columns):
    lane = iota((B, B), 1)
    total = jnp.zeros((B, B), F32)
    for i, column in enumerate(columns):
        total = jnp.where(lane == i, column, total)
    return total.T[:8]


def rows_to_square(rows):
    return jnp.concatenate([rows, jnp.zeros((B - 8, B), F32)], axis=0).T


def row_to_square(row):
    return jnp.broadcast_to(row, (B, B)).T


def main_kernel(
    X, Z, Y, C, vocab_rows,
    emb_hbm, gain_hbm, wq_hbm, wo_hbm, wd_hbm, hw_hbm,
    tok_hbm, rep_hbm, mask_hbm, lab_hbm, seg_hbm,
    grad_out, req_out,
    emb, wq_ref, wod_src, Wq, Wod,
    tok_ref, rep_ref, mask_ref, gain_ref, hw_ref, lab_ref, seg_ref,
    ids_src, ids_buf, row_src, row_buf, gslot_src, gslot_buf,
    x_src, x_buf, h_src, h_buf, d_src, d_buf,
    pq, pq_buf, po, po_buf, pd, pd_buf,
    b1, b1_buf, hr_buf, b2, b2_buf, g_buf, b3, b3_buf,
    nrm, cgain, gains, dl_buf, pre, hw_buf, ar_src, ar_buf,
    in_sem, w1q_sem, w1o_sem, w1_send, w2_recv, w2_send, sib_recv, sib_send,
    t_recv, t_send, e_recv, e_send, e0_send, rx_recv, rx_send, ax_recv, ax_send,
    r_recv, r_send, s_recv, s_send,
):
    V, T = X * Z, Y * C
    Xc = X // C
    D = V * B
    K = Z * B
    v, t = lax.axis_index("vocab"), lax.axis_index("tok")
    x, z = v // Z, v % Z
    y, c = t // C, t % C
    cap = 2 * B // T
    R = T * cap

    def dev(xx, zz, yy, cc):
        return (xx * Z + zz, yy * C + cc)

    def remote(src, dst, send, recv, device):
        return pltpu.make_async_remote_copy(
            src_ref=src, dst_ref=dst, send_sem=send, recv_sem=recv,
            device_id=device, device_id_type=MESH,
        )

    pending = []

    def finish():
        for done in pending:
            done()

    def wait_bytes(ref, sem):
        pltpu.make_async_copy(ref, ref, sem).wait()

    wanted_here = (
        (tok_hbm, tok_ref), (rep_hbm, rep_ref), (mask_hbm, mask_ref),
        (wq_hbm, wq_ref), (wo_hbm, wod_src.at[:, pl.ds(0, B)]),
        (wd_hbm, wod_src.at[:, pl.ds(B, B)]), (emb_hbm, emb),
        (gain_hbm, gain_ref), (hw_hbm, hw_ref), (lab_hbm, lab_ref), (seg_hbm, seg_ref),
    )
    copies = [
        pltpu.make_async_copy(src, dst, in_sem.at[i]) for i, (src, dst) in enumerate(wanted_here)
    ]
    for copy in copies:
        copy.start()
    barrier = pltpu.get_barrier_semaphore()

    def greet_vocab(d, carry):
        pl.semaphore_signal(barrier, inc=1, device_id=((v + d) % V, t), device_id_type=MESH)
        return carry

    def greet_tok(d, carry):
        pl.semaphore_signal(barrier, inc=1, device_id=(v, (t + d) % T), device_id_type=MESH)
        return carry

    lax.fori_loop(1, V, greet_vocab, 0)
    lax.fori_loop(1, T, greet_tok, 0)
    same_core = (x // Xc) == c

    @pl.when(jnp.logical_not(same_core))
    def _():
        for i in range(Xc):
            pl.semaphore_signal(
                barrier, inc=1, device_id=dev(Xc * c + i, z, y, x // Xc), device_id_type=MESH
            )

    for copy in copies[:3]:
        copy.wait()
    chosen = jnp.where(mask_ref[...] == 1, rep_ref[...], tok_ref[...])
    owner = chosen // vocab_rows
    offset = (chosen - owner * vocab_rows).astype(F32)
    owner_f = owner.astype(F32)
    earlier = iota((B, B), 0) < iota((B, B), 1)
    same_owner = row_to_square(owner_f) == owner_f
    slot = jnp.sum(jnp.where(same_owner & earlier, 1.0, 0.0), axis=0, keepdims=True)
    place = owner_f * float(cap) + slot
    place_hot = iota((R, B), 0).astype(F32) == place
    wanted = jnp.sum(jnp.where(place_hot, offset, 0.0), axis=1, keepdims=True)
    ids_src[...] = jnp.broadcast_to(wanted, (R, B)).reshape(T, cap, B)
    for copy in copies[3:6]:
        copy.wait()

    peers = V - 1 + T - 1

    @pl.when(same_core)
    def _():
        pl.semaphore_wait(barrier, peers)

    @pl.when(jnp.logical_not(same_core))
    def _():
        pl.semaphore_wait(barrier, peers + Xc)

    def tok_start(src, buf, n):
        buf[t] = src[t]

        def send(d, carry):
            to = (t + d) % T
            remote(src.at[to], buf.at[t], t_send.at[n], t_recv.at[n], (v, to)).start()
            return carry

        lax.fori_loop(1, T, send, 0)
        pending.append(lambda: wait_bytes(src.at[pl.ds(0, T - 1)], t_send.at[n]))

    def tok_wait(src, buf, n):
        wait_bytes(buf.at[pl.ds(0, T - 1)], t_recv.at[n])

    tok_start(ids_src, ids_buf, 0)

    def w1_each(act):
        for i in range(Xc):
            xd, cd = Xc * c + i, x // Xc
            mine = (xd == x) & same_core
            rows = pl.ds(i * B, B)
            dst_rows = pl.ds(pl.multiple_of(y * B, B), B)
            q = (wq_ref.at[rows], Wq.at[x, dst_rows], w1q_sem)
            o = (wod_src.at[rows], Wod.at[x, dst_rows], w1o_sem)
            for a, (src, dst, sem) in enumerate((q, o)):
                act(mine, src, dst, sem, w1_send.at[i, a], dev(xd, z, y, cd))

    def w1_go(mine, src, dst, sem, send, device):
        @pl.when(mine)
        def _():
            pltpu.make_async_copy(src, dst, sem).start()

        @pl.when(jnp.logical_not(mine))
        def _():
            remote(src, dst, send, sem, device).start()

    def w1_end(mine, src, dst, sem, send, device):
        @pl.when(jnp.logical_not(mine))
        def _():
            wait_bytes(src, send)

    w1_each(w1_go)
    pending.append(lambda: w1_each(w1_end))
    pending.append(lambda: w2_done())

    arrays = (Wq, Wod)
    half_up, half_down = Y // 2, Y - 1 - Y // 2

    def block_of(a, i, k):
        return arrays[a].at[Xc * c + i, pl.ds(pl.multiple_of(k * B, B), B)]

    def hops_of(i, way):
        return half_up if way == i % 2 else half_down

    def hop(a, i, h, way):
        step = 1 if way == 0 else Y - 1
        ref = block_of(a, i, (y + (Y - step) * (h - 1)) % Y)
        return remote(
            ref, ref, w2_send.at[a, i, way, h - 1], w2_recv.at[a, i, way, h - 1],
            dev(x, z, (y + step) % Y, c),
        )

    def sibling(a, i, k, n):
        ref = block_of(a, i, k)
        return remote(
            ref, ref, sib_send.at[a, i, n], sib_recv.at[a, i, n], dev(x, z, y, (c + 1) % C)
        )

    def w2_begin(a):
        wait_bytes(arrays[a].at[pl.ds(0, Xc), pl.ds(0, B)], (w1q_sem, w1o_sem)[a])
        for i in range(Xc):
            for way in (0, 1):
                if hops_of(i, way) >= 1:
                    hop(a, i, 1, way).start()
        for i in range(Xc):
            sibling(a, i, y, 0).start()

    def w2_forward(a, i, h):
        if i >= Xc:
            return
        for way in (0, 1):
            if h <= hops_of(i, way):
                hop(a, i, h, way).wait_recv()
                if h + 1 <= hops_of(i, way):
                    hop(a, i, h + 1, way).start()
        for way in (0, 1):
            if h <= hops_of(i, way):
                step = 1 if way == 0 else Y - 1
                n = h if way == 0 else hops_of(i, 0) + h
                sibling(a, i, (y + (Y - step) * h) % Y, n).start()

    def w2_ready(a):
        for i in range(Xc):
            for n in range(Y):
                wait_bytes(arrays[a].at[0, pl.ds(0, B)], sib_recv.at[a, i, n])

    def w2_done():
        for a in (0, 1):
            for i in range(Xc):
                for way in (0, 1):
                    for h in range(1, hops_of(i, way) + 1):
                        hop(a, i, h, way).wait_send()
                for n in range(Y):
                    wait_bytes(arrays[a].at[0, pl.ds(0, B)], sib_send.at[a, i, n])

    row = z % X
    at_home = x == row

    def row_start(src, buf, n):
        k = v // X
        for j in list(range(1, Z)):
            remote(src, buf.at[k], e_send.at[n], e_recv.at[n], dev(row, (z + j) % Z, y, c)).start()

        @pl.when(at_home)
        def _():
            pltpu.make_async_copy(src, buf.at[k], e_recv.at[n]).start()

        @pl.when(jnp.logical_not(at_home))
        def _():
            remote(src, buf.at[k], e0_send.at[n], e_recv.at[n], dev(row, z, y, c)).start()

        pending.append(lambda: row_done(src, buf, n))

    def row_wait(src, buf, n):
        wait_bytes(buf, e_recv.at[n])

    def row_done(src, buf, n):
        wait_bytes(buf.at[pl.ds(0, Z - 1)], e_send.at[n])

        @pl.when(jnp.logical_not(at_home))
        def _():
            wait_bytes(src, e0_send.at[n])

    def rx_start(part, buf, n):
        for d in range(1, X):
            to = (x + d) % X
            remote(
                part.at[to], buf.at[d - 1], rx_send.at[n], rx_recv.at[n], dev(to, z, y, c)
            ).start()
        pending.append(lambda: wait_bytes(buf, rx_send.at[n]))

    def rx_sum(part, buf, n):
        wait_bytes(buf, rx_recv.at[n])
        total = part[x].astype(F32)
        for d in range(1, X):
            total = total + buf[d - 1].astype(F32)
        return total

    def ax_start(buf, n):
        for d in range(1, X):
            remote(
                buf.at[x], buf.at[x], ax_send.at[n], ax_recv.at[n], dev((x + d) % X, z, y, c)
            ).start()
        pending.append(lambda: wait_bytes(buf.at[pl.ds(0, X - 1)], ax_send.at[n]))

    def ax_wait(buf, n):
        wait_bytes(buf.at[pl.ds(0, X - 1)], ax_recv.at[n])

    def own_start(part, buf, k, n):
        to = X * k + x
        mine = to == v

        @pl.when(mine)
        def _():
            pltpu.make_async_copy(part.at[k], buf.at[z], r_recv.at[n]).start()

        @pl.when(jnp.logical_not(mine))
        def _():
            remote(part.at[k], buf.at[z], r_send.at[n, k], r_recv.at[n], (to, t)).start()

    def own_sum(buf, n):
        wait_bytes(buf, r_recv.at[n])
        total = buf[0].astype(F32)
        for k in range(1, Z):
            total = total + buf[k].astype(F32)
        return total

    def own_done(part, n):
        for k in range(Z):
            @pl.when(X * k + x != v)
            def _():
                wait_bytes(part.at[k], r_send.at[n, k])

    def spread_back(left, weights, part, buf, n, seen=None):
        step = 2
        for first in range(0, Z, step):
            total = None
            for xx in range(X):
                term = dot_nt(left(xx), weights(xx, pl.ds(first * B, step * B)))
                total = term if total is None else total + term
            for k in range(first, first + step):
                part[k] = total[:, (k - first) * B : (k - first + 1) * B].astype(BF)
                own_start(part, buf, k, n)
            if seen is not None:
                for k in range(first, first + step):
                    seen(k, part[k].astype(F32))
        pending.append(lambda: own_done(part, n))

    def ar_start(rows, n):
        ar_src[n] = rows
        ar_buf[n, 0] = rows

        def send(d, carry):
            remote(
                ar_src.at[n], ar_buf.at[n, d], s_send.at[n], s_recv.at[n], ((v + d) % V, t)
            ).start()
            return carry

        lax.fori_loop(1, V, send, 0)
        pending.append(lambda: wait_bytes(ar_buf.at[n, pl.ds(1, V - 1)], s_send.at[n]))

    def ar_sum(n):
        wait_bytes(ar_buf.at[n, pl.ds(1, V - 1)], s_recv.at[n])
        return rows_to_square(jnp.sum(ar_buf[n], axis=0))

    for copy in copies[6:]:
        copy.wait()
    hw_buf[x] = jnp.broadcast_to(hw_ref[...].astype(F32), (16, B)).astype(BF)
    ax_start(hw_buf, 3)
    put_hot = jnp.where(place_hot, 1.0, 0.0).astype(BF)
    place_square = row_to_square(place)
    take_hot = jnp.concatenate(
        [
            jnp.where(place_square == (iota((B, B), 1) + first).astype(F32), 1.0, 0.0)
            for first in range(0, R, B)
        ],
        axis=1,
    ).astype(BF)
    segment_f = seg_ref[...].astype(F32)
    same_segment = row_to_square(segment_f) == segment_f
    labels = row_to_square(lab_ref[...].astype(F32))[:, 0:1]
    gain = gain_ref[...].astype(F32)
    head_vector = hw_ref[...].astype(F32)
    x_src[B : B + 16, :] = jnp.broadcast_to(gain, (16, B)).astype(BF)
    tok_wait(ids_src, ids_buf, 0)
    requested = ids_buf[...].reshape(R, B)
    chunk = 512

    def fetch(i, total):
        base = i * chunk
        hot = jnp.concatenate(
            [
                jnp.where(
                    requested == (iota((R, B), 1) + (base + first)).astype(F32), 1.0, 0.0
                ).astype(BF)
                for first in range(0, chunk, B)
            ],
            axis=1,
        )
        return total + dot(hot, emb[pl.ds(pl.multiple_of(base, chunk), chunk), :])

    fetched = lax.fori_loop(0, vocab_rows // chunk, fetch, jnp.zeros((R, B), F32))
    row_src[...] = fetched.astype(BF).reshape(T, cap, B)
    tok_start(row_src, row_buf, 1)
    w2_begin(0)
    for first in range(0, R, B):
        req_out[:, first : first + B] = requested[first : first + B].T[:8]
    w2_forward(0, 0, 1)
    w2_forward(0, 1, 1)
    tok_wait(row_src, row_buf, 1)
    features = dot(take_hot, row_buf[...].reshape(R, B))
    x_src[0:B, :] = features.astype(BF)
    row_start(x_src, x_buf, 0)
    ar_start(
        columns_to_rows(
            [
                jnp.sum(features, axis=1, keepdims=True),
                jnp.sum(features * features, axis=1, keepdims=True),
            ]
        ),
        0,
    )
    w2_forward(0, 0, 2)
    w2_forward(0, 1, 2)
    stats = ar_sum(0)
    row_mean = stats[:, 0:1] / D
    variance = stats[:, 1:2] / D - row_mean * row_mean
    inv_std = lax.rsqrt(variance + epsilon)
    centered = (features - row_mean) * inv_std
    w2_forward(0, 0, 3)
    w2_forward(0, 1, 3)
    row_wait(x_src, x_buf, 0)
    for k in range(Z):
        block = x_buf[k, 0:B, :].astype(F32)
        block_gain = x_buf[k, B : B + 16, :].astype(F32)[0:8]
        gains[k] = block_gain
        normed = ((block - row_mean) * inv_std) * block_gain[0:1]
        cgain[k] = normed
        nrm[:, k * B : (k + 1) * B] = normed.astype(BF)
    w2_begin(1)
    w2_forward(0, 0, 4)
    w2_forward(0, 1, 4)
    w2_ready(0)
    for xx in range(X):
        pq[xx] = dot(nrm[...], Wq[xx]).astype(BF)
    rx_start(pq, pq_buf, 0)
    w2_forward(1, 0, 1)
    w2_forward(1, 1, 1)
    qkv = rx_sum(pq, pq_buf, 0).astype(BF)
    queries, keys, values = qkv[:, :B], qkv[:, B : 2 * B], qkv[:, 2 * B :]
    raw = dot_nt(queries, keys) / math.sqrt(B)
    capped = soft_limit * jnp.tanh(raw / soft_limit)
    exps = jnp.where(same_segment, jnp.exp(capped), 0.0)
    probabilities = exps / jnp.sum(exps, axis=-1, keepdims=True)
    prob_rounded = probabilities.astype(BF)
    h_src[...] = dot(prob_rounded, values).astype(BF)
    row_start(h_src, h_buf, 1)
    for h in (2, 3, 4):
        w2_forward(1, 0, h)
        w2_forward(1, 1, h)
    row_wait(h_src, h_buf, 1)
    w2_ready(1)

    heads_row = jnp.concatenate([h_buf[k] for k in range(Z)], axis=1)
    for xx in range(X):
        po[xx] = dot(heads_row, Wod[xx, :, 0:B]).astype(po.dtype)
    rx_start(po, po_buf, 1)
    hidden = features + rx_sum(po, po_buf, 1)
    d_src[...] = hidden.astype(BF)
    row_start(d_src, d_buf, 2)
    row_wait(d_src, d_buf, 2)

    dense_row = jnp.concatenate([d_buf[k] for k in range(Z)], axis=1)
    for xx in range(X):
        pd[xx] = dot(dense_row, Wod[xx, :, B : 2 * B]).astype(pd.dtype)
    rx_start(pd, pd_buf, 2)
    dense_linear = rx_sum(pd, pd_buf, 2)
    dl_buf[x] = dense_linear
    activated = dense_linear * (0.5 * (1.0 + lax.erf(dense_linear * inv_root_two)))
    ar_start(
        columns_to_rows(
            [
                jnp.sum(activated, axis=1, keepdims=True),
                jnp.sum(activated * activated, axis=1, keepdims=True),
                jnp.sum(activated * head_vector, axis=1, keepdims=True),
                jnp.broadcast_to(jnp.sum(head_vector, axis=1, keepdims=True), (B, 1)),
            ]
        ),
        1,
    )
    ax_start(dl_buf, 0)
    ax_wait(hw_buf, 3)
    ax_wait(dl_buf, 0)
    gelus = []
    for xx in range(X):
        linear = dl_buf[xx]
        phi = 0.5 * (1.0 + lax.erf(linear * inv_root_two))
        slope = phi + linear * jnp.exp(-0.5 * linear * linear) * inv_root_tau
        gelus.append((linear * phi, slope, hw_buf[xx].astype(F32)[0:1]))
    stats = ar_sum(1)
    head_mean = stats[:, 0:1] / D
    head_scale = lax.rsqrt(stats[:, 1:2] / D - head_mean * head_mean + epsilon)
    weight_sum = stats[:, 3:4]
    logits = head_scale * (stats[:, 2:3] - head_mean * weight_sum)
    logit_grads = loss_scale * (jax.nn.sigmoid(logits) - labels)
    mean_grads = logit_grads * weight_sum / D
    mean_product = logit_grads * logits / D
    for xx, (active, slope, vector) in enumerate(gelus):
        head_centered = (active - head_mean) * head_scale
        activated_grads = head_scale * (
            logit_grads * vector - mean_grads - head_centered * mean_product
        )
        pre[xx] = (activated_grads * slope).astype(BF)
    spread_back(lambda xx: pre[xx], lambda xx, rows: Wod[xx, rows, B : 2 * B], b1, b1_buf, 0)
    hidden_grads = own_sum(b1_buf, 0)
    hr_buf[x] = hidden_grads.astype(BF)
    ax_start(hr_buf, 1)
    ax_wait(hr_buf, 1)
    spread_back(lambda xx: hr_buf[xx], lambda xx, rows: Wod[xx, rows, 0:B], b2, b2_buf, 1)
    out_rounded = own_sum(b2_buf, 1).astype(BF)

    prob_grads = dot_nt(out_rounded, values)
    value_grads = dot_tn(prob_rounded, out_rounded)
    capped_grads = probabilities * (
        prob_grads - jnp.sum(probabilities * prob_grads, axis=-1, keepdims=True)
    )
    ratio = capped / soft_limit
    score_rounded = (capped_grads * (1.0 - ratio * ratio) / math.sqrt(B)).astype(BF)
    query_grads = dot(score_rounded, keys)
    key_grads = dot_tn(score_rounded, queries)
    g_buf[x] = jnp.concatenate([query_grads, key_grads, value_grads], axis=1).astype(BF)
    ax_start(g_buf, 2)
    ax_wait(g_buf, 2)
    sums = [jnp.zeros((B, B), F32), jnp.zeros((B, B), F32)]

    def gather_sums(k, block):
        sums[0] = sums[0] + block * gains[k, 0:1]
        sums[1] = sums[1] + block * cgain[k]

    spread_back(lambda xx: g_buf[xx], lambda xx, rows: Wq[xx, rows, :], b3, b3_buf, 2, gather_sums)
    ar_start(columns_to_rows([jnp.sum(total, axis=1, keepdims=True) for total in sums]), 2)
    scaled = own_sum(b3_buf, 2) * gain
    stats = ar_sum(2)
    input_grads = hidden_grads + inv_std * (
        scaled - stats[:, 0:1] / D - centered * (stats[:, 1:2] / D)
    )

    gslot_src[...] = dot(put_hot, input_grads.astype(BF)).astype(BF).reshape(T, cap, B)
    tok_start(gslot_src, gslot_buf, 2)
    tok_wait(gslot_src, gslot_buf, 2)
    grad_out[...] = gslot_buf[...].reshape(R, B)

    finish()


def table_kernel(tile, grad_ref, req_ref, out_ref):
    base = pl.program_id(0) * tile
    hot = jnp.where(
        (iota((tile, req_ref.shape[1]), 0) + base).astype(F32) == req_ref[0:1, :], 1.0, 0.0
    ).astype(BF)
    out_ref[...] = dot(hot, grad_ref[...]).astype(BF)


def local(
    X, Z, Y, C,
    embeddings, norm_gain, query_key_value_weight, out_weight, dense_weight, head_weight,
    token_ids, replace_ids, masked, labels, segments,
):
    vocab_rows = embeddings.shape[0]
    V, T = X * Z, Y * C
    cap = 2 * B // T
    R = T * cap
    vm = pl.BlockSpec(memory_space=pltpu.VMEM)
    dma = pltpu.SemaphoreType.DMA
    rows = query_key_value_weight.shape[0]
    VM = pltpu.VMEM
    right = Y // 2
    grads, requests = pl.pallas_call(
        functools.partial(main_kernel, X, Z, Y, C, vocab_rows),
        out_shape=(
            jax.ShapeDtypeStruct((R, B), BF),
            jax.ShapeDtypeStruct((8, R), F32),
        ),
        in_specs=[pl.BlockSpec(memory_space=pltpu.HBM)] * 11,
        out_specs=(vm, vm),
        scratch_shapes=[
            VM((vocab_rows, B), BF),
            VM((rows, 3 * B), BF),
            VM((rows, 2 * B), BF),
            VM((X, Z * B, 3 * B), BF),
            VM((X, Z * B, 2 * B), BF),
            VM((1, B), jnp.int32), VM((1, B), jnp.int32), VM((1, B), jnp.int32),
            VM((1, B), BF), VM((1, B), BF),
            VM((1, B), jnp.int32), VM((1, B), jnp.int32),
            VM((T, cap, B), F32), VM((T, cap, B), F32),
            VM((T, cap, B), BF), VM((T, cap, B), BF),
            VM((T, cap, B), BF), VM((T, cap, B), BF),
            VM((B + 16, B), BF), VM((Z, B + 16, B), BF),
            VM((B, B), BF), VM((Z, B, B), BF),
            VM((B, B), BF), VM((Z, B, B), BF),
            VM((X, B, 3 * B), BF), VM((X - 1, B, 3 * B), BF),
            VM((X, B, B), BF), VM((X - 1, B, B), BF),
            VM((X, B, B), BF), VM((X - 1, B, B), BF),
            VM((Z, B, B), BF), VM((Z, B, B), BF),
            VM((X, B, B), BF), VM((Z, B, B), BF), VM((Z, B, B), BF),
            VM((X, B, 3 * B), BF), VM((Z, B, B), BF), VM((Z, B, B), BF),
            VM((B, Z * B), BF), VM((Z, B, B), F32), VM((Z, 8, B), F32),
            VM((X, B, B), F32), VM((X, B, B), BF), VM((X, 16, B), BF),
            VM((3, 8, B), F32), VM((3, V, 8, B), F32),
            dma((11,)), dma(()), dma(()), dma((X // C, 2)),
            dma((2, X // C, 2, right)), dma((2, X // C, 2, right)),
            dma((2, X // C, Y)), dma((2, X // C, Y)),
            dma((3,)), dma((3,)), dma((3,)), dma((3,)), dma((3,)),
            dma((3,)), dma((3,)), dma((4,)), dma((4,)),
            dma((3,)), dma((3, Z)), dma((3,)), dma((3,)),
        ],
        compiler_params=pltpu.CompilerParams(
            collective_id=0, has_side_effects=True, vmem_limit_bytes=60 * 1024 * 1024
        ),
    )(
        embeddings,
        norm_gain.reshape(1, B),
        query_key_value_weight.reshape(rows, 3 * B),
        out_weight,
        dense_weight,
        head_weight.reshape(1, B),
        token_ids, replace_ids, masked, labels, segments,
    )
    tile = min(1024, vocab_rows)
    return pl.pallas_call(
        functools.partial(table_kernel, tile),
        grid=(vocab_rows // tile,),
        out_shape=jax.ShapeDtypeStruct((vocab_rows, B), BF),
        in_specs=[
            pl.BlockSpec((R, B), lambda i: (0, 0)),
            pl.BlockSpec((8, R), lambda i: (0, 0)),
        ],
        out_specs=pl.BlockSpec((tile, B), lambda i: (i, 0)),
        compiler_params=pltpu.CompilerParams(vmem_limit_bytes=60 * 1024 * 1024),
    )(grads, requests)


def solution(mesh):
    V, T = mesh.shape["vocab"], mesh.shape["tok"]
    X = 4 if V == 32 else 2
    C = 2
    placed = (
        P("tok", "vocab"),
        P("vocab"),
        P("tok", "vocab", None),
        P("tok", "vocab"),
        P("tok", "vocab"),
        P("vocab"),
        P("tok", None),
        P("tok", None),
        P("tok", None),
        P("tok", None),
        P("tok", None),
    )
    return jax.shard_map(
        functools.partial(local, X, V // X, T // C, C),
        mesh=mesh, in_specs=placed, out_specs=P("tok", "vocab"), check_vma=False,
    )
```

```python
import functools
import math

import jax
import jax.numpy as jnp
from jax import lax
from jax.experimental import pallas as pl
from jax.experimental.pallas import tpu as pltpu
from jax.sharding import PartitionSpec as P

MESH = pl.DeviceIdType.MESH
BF = jnp.bfloat16
F32 = jnp.float32
B = 128

soft_limit = 50.0
loss_scale = 64.0
epsilon = 1e-05
inv_root_two = 0.7071067811865476
inv_root_tau = 0.3989422804014327


def dot(a, b):
    return jnp.dot(a, b, preferred_element_type=F32)


def dot_nt(a, b):
    return lax.dot_general(a, b, (((1,), (1,)), ((), ())), preferred_element_type=F32)


def dot_tn(a, b):
    return lax.dot_general(a, b, (((0,), (0,)), ((), ())), preferred_element_type=F32)


def iota(shape, dim):
    return lax.broadcasted_iota(jnp.int32, shape, dim)


def columns_to_rows(columns):
    lane = iota((B, B), 1)
    total = jnp.zeros((B, B), F32)
    for i, column in enumerate(columns):
        total = jnp.where(lane == i, column, total)
    return total.T[:8]


def rows_to_square(rows):
    return jnp.concatenate([rows, jnp.zeros((B - 8, B), F32)], axis=0).T


def row_to_square(row):
    return jnp.broadcast_to(row, (B, B)).T


def main_kernel(
    X, Z, Y, C, vocab_rows,
    emb_hbm, gain_hbm, wq_hbm, wo_hbm, wd_hbm, hw_hbm,
    tok_hbm, rep_hbm, mask_hbm, lab_hbm, seg_hbm,
    grad_out, req_out,
    emb, wq_ref, wod_src, Wq, Wod,
    tok_ref, rep_ref, mask_ref, gain_ref, hw_ref, lab_ref, seg_ref,
    ids_src, ids_buf, row_src, row_buf, st_src, st_buf, gslot_src, gslot_buf,
    x_src, x_buf, h_src, h_buf, d_src, d_buf,
    pq, pq_buf, po, po_buf, pd, pd_buf,
    b1, b1_buf, hr_buf, b2, b2_buf, g_buf, b3, b3_buf,
    nrm, cgain, gains, dl_buf, pre, hw_buf, ar_src, ar_buf,
    in_sem, w1q_sem, w1o_sem, w1_send, w2_recv, w2_send, sib_recv, sib_send,
    t_recv, t_send, e_recv, e_send, rx_recv, rx_send, ax_recv, ax_send,
    r_recv, r_send, s_recv, s_send,
):
    V, T = X * Z, Y * C
    Xc = X // C
    D = V * B
    K = Z * B
    v, t = lax.axis_index("vocab"), lax.axis_index("tok")
    x, z = v // Z, v % Z
    y, c = t // C, t % C
    cap = 2 * B // T
    R = T * cap

    def dev(xx, zz, yy, cc):
        return (xx * Z + zz, yy * C + cc)

    def remote(src, dst, send, recv, device):
        return pltpu.make_async_remote_copy(
            src_ref=src, dst_ref=dst, send_sem=send, recv_sem=recv,
            device_id=device, device_id_type=MESH,
        )

    pending = []

    def finish():
        for done in pending:
            done()
        pending.clear()

    def wait_bytes(ref, sem):
        pltpu.make_async_copy(ref, ref, sem).wait()

    wanted_here = (
        (tok_hbm, tok_ref), (rep_hbm, rep_ref), (mask_hbm, mask_ref),
        (wq_hbm, wq_ref), (wo_hbm, wod_src.at[:, pl.ds(0, B)]),
        (wd_hbm, wod_src.at[:, pl.ds(B, B)]), (emb_hbm, emb),
        (gain_hbm, gain_ref), (hw_hbm, hw_ref), (lab_hbm, lab_ref), (seg_hbm, seg_ref),
    )
    copies = [
        pltpu.make_async_copy(src, dst, in_sem.at[i]) for i, (src, dst) in enumerate(wanted_here)
    ]
    for copy in copies:
        copy.start()
    barrier = pltpu.get_barrier_semaphore()

    def greet_vocab(d, carry):
        pl.semaphore_signal(barrier, inc=1, device_id=((v + d) % V, t), device_id_type=MESH)
        return carry

    def greet_tok(d, carry):
        pl.semaphore_signal(barrier, inc=1, device_id=(v, (t + d) % T), device_id_type=MESH)
        return carry

    lax.fori_loop(1, V, greet_vocab, 0)
    lax.fori_loop(1, T, greet_tok, 0)
    turn = y // (Z // X)
    same_core = (x // Xc) == c
    from_core = ((x + turn) % X) // Xc
    other_source = from_core != c

    @pl.when(jnp.logical_not(same_core))
    def _():
        for i in range(Xc):
            to = dev((Xc * c + i + X - turn) % X, z, y, x // Xc)
            pl.semaphore_signal(barrier, inc=1, device_id=to, device_id_type=MESH)

    @pl.when(other_source)
    def _():
        for i in range(Xc):
            to = dev(Xc * c + i, z, y, from_core)
            pl.semaphore_signal(barrier, inc=1, device_id=to, device_id_type=MESH)

    for copy in copies[:3]:
        copy.wait()
    chosen = jnp.where(mask_ref[...] == 1, rep_ref[...], tok_ref[...])
    owner = chosen // vocab_rows
    offset = (chosen - owner * vocab_rows).astype(F32)
    owner_f = owner.astype(F32)
    earlier = iota((B, B), 0) < iota((B, B), 1)
    same_owner = row_to_square(owner_f) == owner_f
    slot = jnp.sum(jnp.where(same_owner & earlier, 1.0, 0.0), axis=0, keepdims=True)
    place = owner_f * float(cap) + slot
    place_hot = iota((R, B), 0).astype(F32) == place
    wanted = jnp.sum(jnp.where(place_hot, offset, 0.0), axis=1, keepdims=True)
    ids_src[...] = jnp.broadcast_to(wanted, (R, B)).reshape(T, cap, B)
    for copy in copies[3:6]:
        copy.wait()

    pl.semaphore_wait(
        barrier,
        V - 1 + T - 1
        + Xc * jnp.where(same_core, 0, 1)
        + Xc * jnp.where(other_source, 1, 0),
    )

    def tok_start(src, buf, n):
        buf[t] = src[t]

        def send(d, carry):
            to = (t + d) % T
            remote(src.at[to], buf.at[t], t_send.at[n], t_recv.at[n], (v, to)).start()
            return carry

        lax.fori_loop(1, T, send, 0)
        pending.append(lambda: wait_bytes(src.at[pl.ds(0, T - 1)], t_send.at[n]))

    def tok_wait(src, buf, n):
        wait_bytes(buf.at[pl.ds(0, T - 1)], t_recv.at[n])

    tok_start(ids_src, ids_buf, 0)

    def w1_each(act):
        for i in range(Xc):
            xd, cd = (Xc * c + i + X - turn) % X, x // Xc
            mine = (xd == x) & same_core
            rows = pl.ds(i * B, B)
            dst_rows = pl.ds(pl.multiple_of(y * B, B), B)
            q = (wq_ref.at[rows], Wq.at[x, dst_rows], w1q_sem)
            o = (wod_src.at[rows], Wod.at[x, dst_rows], w1o_sem)
            for a, (src, dst, sem) in enumerate((q, o)):
                act(mine, src, dst, sem, w1_send.at[i, a], dev(xd, z, y, cd))

    def w1_go(mine, src, dst, sem, send, device):
        @pl.when(mine)
        def _():
            pltpu.make_async_copy(src, dst, sem).start()

        @pl.when(jnp.logical_not(mine))
        def _():
            remote(src, dst, send, sem, device).start()

    def w1_end(mine, src, dst, sem, send, device):
        @pl.when(jnp.logical_not(mine))
        def _():
            wait_bytes(src, send)

    w1_each(w1_go)
    pending.append(lambda: w1_each(w1_end))
    pending.append(lambda: w2_done())

    arrays = (Wq, Wod)
    half_up, half_down = Y // 2, Y - 1 - Y // 2

    def block_of(a, i, k):
        return arrays[a].at[Xc * c + i, pl.ds(pl.multiple_of(k * B, B), B)]

    def hops_of(i, way):
        return half_up if way == i % 2 else half_down

    def hop(a, i, h, way):
        step = 1 if way == 0 else Y - 1
        ref = block_of(a, i, (y + (Y - step) * (h - 1)) % Y)
        return remote(
            ref, ref, w2_send.at[a, i], w2_recv.at[a, i, way, h - 1],
            dev(x, z, (y + step) % Y, c),
        )

    def sibling(a, i, k):
        ref = block_of(a, i, k)
        return remote(
            ref, ref, sib_send.at[a, i], sib_recv.at[a, i], dev(x, z, y, (c + 1) % C)
        )

    def w2_begin(a):
        wait_bytes(arrays[a].at[pl.ds(0, Xc), pl.ds(0, B)], (w1q_sem, w1o_sem)[a])
        for i in range(Xc):
            for way in (0, 1):
                if hops_of(i, way) >= 1:
                    hop(a, i, 1, way).start()
        for i in range(Xc):
            sibling(a, i, y).start()

    def w2_forward(a, i, h):
        if i >= Xc:
            return
        for way in (0, 1):
            if h <= hops_of(i, way):
                hop(a, i, h, way).wait_recv()
                if h + 1 <= hops_of(i, way):
                    hop(a, i, h + 1, way).start()
        for way in (0, 1):
            if h <= hops_of(i, way):
                step = 1 if way == 0 else Y - 1
                sibling(a, i, (y + (Y - step) * h) % Y).start()

    def w2_ready(a):
        for i in range(Xc):
            wait_bytes(arrays[a].at[0], sib_recv.at[a, i])

    def w2_done():
        for a in (0, 1):
            for i in range(Xc):
                wait_bytes(arrays[a].at[0, pl.ds(0, (Y - 1) * B)], w2_send.at[a, i])
                wait_bytes(arrays[a].at[0], sib_send.at[a, i])

    row = (z + X - x) % X
    at_home = x == row

    def block_done(ref, sem):
        @pl.when(at_home)
        def _():
            wait_bytes(ref.at[pl.ds(0, Z - 1)], sem)

        @pl.when(jnp.logical_not(at_home))
        def _():
            wait_bytes(ref, sem)

    def row_start(src, buf, n):
        k = v // X
        for j in range(Z):
            zd = (z + x + j) % Z
            mine = at_home & (zd == z)

            @pl.when(mine)
            def _():
                pltpu.make_async_copy(src, buf.at[k], e_recv.at[n]).start()

            @pl.when(jnp.logical_not(mine))
            def _():
                remote(src, buf.at[k], e_send.at[n], e_recv.at[n], dev(row, zd, y, c)).start()

        pending.append(lambda: block_done(buf, e_send.at[n]))

    def row_wait(src, buf, n):
        wait_bytes(buf, e_recv.at[n])

    def rx_start(part, buf, n):
        for d in range(1, X):
            to = (x + d) % X
            remote(
                part.at[to], buf.at[d - 1], rx_send.at[n], rx_recv.at[n], dev(to, z, y, c)
            ).start()
        pending.append(lambda: wait_bytes(buf, rx_send.at[n]))

    def rx_sum(part, buf, n):
        wait_bytes(buf, rx_recv.at[n])
        total = part[x].astype(F32)
        for d in range(1, X):
            total = total + buf[d - 1].astype(F32)
        return total

    def ax_start(buf, n):
        for d in range(1, X):
            remote(
                buf.at[x], buf.at[x], ax_send.at[n], ax_recv.at[n], dev((x + d) % X, z, y, c)
            ).start()
        pending.append(lambda: wait_bytes(buf.at[pl.ds(0, X - 1)], ax_send.at[n]))

    def ax_wait(buf, n):
        wait_bytes(buf.at[pl.ds(0, X - 1)], ax_recv.at[n])

    def own_start(part, buf, n):
        for j in range(Z):
            k = (z + j) % Z
            to = X * k + (x + k // (Z // X)) % X
            mine = to == v

            @pl.when(mine)
            def _():
                pltpu.make_async_copy(part.at[k], buf.at[z], r_recv.at[n]).start()

            @pl.when(jnp.logical_not(mine))
            def _():
                remote(part.at[k], buf.at[z], r_send.at[n], r_recv.at[n], (to, t)).start()

        pending.append(lambda: block_done(part, r_send.at[n]))

    def own_sum(buf, n):
        wait_bytes(buf, r_recv.at[n])
        total = buf[0].astype(F32)
        for k in range(1, Z):
            total = total + buf[k].astype(F32)
        return total

    def spread_back(left, weights, part, buf, n, seen=None):
        step = 2
        for first in range(0, Z, step):
            total = None
            for xx in range(X):
                term = dot_nt(left(xx), weights(xx, pl.ds(first * B, step * B)))
                total = term if total is None else total + term
            for k in range(first, first + step):
                part[k] = total[:, (k - first) * B : (k - first + 1) * B].astype(BF)
        if seen is not None:
            seen()
        own_start(part, buf, n)

    def ar_start(rows, n):
        ar_src[n] = rows
        ar_buf[n, 0] = rows

        def send(d, carry):
            remote(
                ar_src.at[n], ar_buf.at[n, d], s_send.at[n], s_recv.at[n], ((v + d) % V, t)
            ).start()
            return carry

        lax.fori_loop(1, V, send, 0)
        pending.append(lambda: wait_bytes(ar_buf.at[n, pl.ds(1, V - 1)], s_send.at[n]))

    def ar_sum(n):
        wait_bytes(ar_buf.at[n, pl.ds(1, V - 1)], s_recv.at[n])
        return rows_to_square(jnp.sum(ar_buf[n], axis=0))

    for copy in copies[6:]:
        copy.wait()
    hw_buf[x] = jnp.broadcast_to(hw_ref[...].astype(F32), (16, B)).astype(BF)
    ax_start(hw_buf, 3)
    put_hot = jnp.where(place_hot, 1.0, 0.0).astype(BF)
    place_square = row_to_square(place)
    take_hot = jnp.concatenate(
        [
            jnp.where(place_square == (iota((B, B), 1) + first).astype(F32), 1.0, 0.0)
            for first in range(0, R, B)
        ],
        axis=1,
    ).astype(BF)
    segment_f = seg_ref[...].astype(F32)
    same_segment = row_to_square(segment_f) == segment_f
    labels = row_to_square(lab_ref[...].astype(F32))[:, 0:1]
    gain = gain_ref[...].astype(F32)
    head_vector = hw_ref[...].astype(F32)
    x_src[B : B + 16, :] = jnp.broadcast_to(gain, (16, B)).astype(BF)
    tok_wait(ids_src, ids_buf, 0)
    requested = ids_buf[...].reshape(R, B)
    chunk = 512

    w2_begin(0)

    def fetch(i, total):
        base = i * chunk
        hot = jnp.concatenate(
            [
                jnp.where(
                    requested == (iota((R, B), 1) + (base + first)).astype(F32), 1.0, 0.0
                ).astype(BF)
                for first in range(0, chunk, B)
            ],
            axis=1,
        )
        return total + dot(hot, emb[pl.ds(pl.multiple_of(base, chunk), chunk), :])

    fetched = lax.fori_loop(0, vocab_rows // chunk, fetch, jnp.zeros((R, B), F32))
    row_src[...] = fetched.astype(BF).reshape(T, cap, B)
    tok_start(row_src, row_buf, 1)
    row_sums = []
    for first in range(0, R, B):
        piece = fetched[first : first + B]
        row_sums.append(jnp.sum(piece, axis=1, keepdims=True))
        row_sums.append(jnp.sum(piece * piece, axis=1, keepdims=True))
    ar_start(columns_to_rows(row_sums), 0)
    for first in range(0, R, B):
        req_out[:, first : first + B] = requested[first : first + B].T[:8]
    w2_forward(0, 0, 1)
    w2_forward(0, 1, 1)
    tok_wait(row_src, row_buf, 1)
    features = dot(take_hot, row_buf[...].reshape(R, B))
    x_src[0:B, :] = features.astype(BF)
    row_start(x_src, x_buf, 0)
    stats = ar_sum(0)
    lane = iota((B, B), 1)
    for first in range(0, R, B):
        i = 2 * (first // B)
        pair = jnp.where(lane == 0, stats[:, i : i + 1], stats[:, i + 1 : i + 2])
        st_src[first // cap : (first + B) // cap] = pair.reshape(B // cap, cap, B)
    tok_start(st_src, st_buf, 3)
    w2_forward(0, 0, 2)
    w2_forward(0, 1, 2)
    tok_wait(st_src, st_buf, 3)
    stats = jnp.dot(
        take_hot.astype(F32),
        st_buf[...].reshape(R, B),
        preferred_element_type=F32,
        precision=lax.Precision.HIGHEST,
    )
    row_mean = stats[:, 0:1] / D
    variance = stats[:, 1:2] / D - row_mean * row_mean
    inv_std = lax.rsqrt(variance + epsilon)
    centered = (features - row_mean) * inv_std
    w2_forward(0, 0, 3)
    w2_forward(0, 1, 3)
    w2_begin(1)
    row_wait(x_src, x_buf, 0)
    for k in range(Z):
        block = x_buf[k, 0:B, :].astype(F32)
        block_gain = x_buf[k, B : B + 16, :].astype(F32)[0:8]
        gains[k] = block_gain
        normed = ((block - row_mean) * inv_std) * block_gain[0:1]
        cgain[k] = normed
        nrm[:, k * B : (k + 1) * B] = normed.astype(BF)
    w2_forward(0, 0, 4)
    w2_forward(0, 1, 4)
    w2_ready(0)
    for xx in range(X):
        pq[xx] = dot(nrm[...], Wq[xx]).astype(BF)
    rx_start(pq, pq_buf, 0)
    w2_forward(1, 0, 1)
    w2_forward(1, 1, 1)
    qkv = rx_sum(pq, pq_buf, 0).astype(BF)
    queries, keys, values = qkv[:, :B], qkv[:, B : 2 * B], qkv[:, 2 * B :]
    raw = dot_nt(queries, keys) / math.sqrt(B)
    capped = soft_limit * jnp.tanh(raw / soft_limit)
    exps = jnp.where(same_segment, jnp.exp(capped), 0.0)
    probabilities = exps / jnp.sum(exps, axis=-1, keepdims=True)
    prob_rounded = probabilities.astype(BF)
    h_src[...] = dot(prob_rounded, values).astype(BF)
    row_start(h_src, h_buf, 1)
    for h in (2, 3, 4):
        w2_forward(1, 0, h)
        w2_forward(1, 1, h)
    row_wait(h_src, h_buf, 1)
    w2_ready(1)

    heads_row = jnp.concatenate([h_buf[k] for k in range(Z)], axis=1)
    for xx in range(X):
        po[xx] = dot(heads_row, Wod[xx, :, 0:B]).astype(po.dtype)
    rx_start(po, po_buf, 1)
    hidden = features + rx_sum(po, po_buf, 1)
    d_src[...] = hidden.astype(BF)
    row_start(d_src, d_buf, 2)
    row_wait(d_src, d_buf, 2)

    dense_row = jnp.concatenate([d_buf[k] for k in range(Z)], axis=1)
    for xx in range(X):
        pd[xx] = dot(dense_row, Wod[xx, :, B : 2 * B]).astype(pd.dtype)
    rx_start(pd, pd_buf, 2)
    dense_linear = rx_sum(pd, pd_buf, 2)
    dl_buf[x] = dense_linear
    activated = dense_linear * (0.5 * (1.0 + lax.erf(dense_linear * inv_root_two)))
    ar_start(
        columns_to_rows(
            [
                jnp.sum(activated, axis=1, keepdims=True),
                jnp.sum(activated * activated, axis=1, keepdims=True),
                jnp.sum(activated * head_vector, axis=1, keepdims=True),
                jnp.broadcast_to(jnp.sum(head_vector, axis=1, keepdims=True), (B, 1)),
            ]
        ),
        1,
    )
    ax_start(dl_buf, 0)
    ax_wait(hw_buf, 3)
    ax_wait(dl_buf, 0)
    gelus = []
    for xx in range(X):
        linear = dl_buf[xx]
        phi = 0.5 * (1.0 + lax.erf(linear * inv_root_two))
        slope = phi + linear * jnp.exp(-0.5 * linear * linear) * inv_root_tau
        gelus.append((linear * phi, slope, hw_buf[xx].astype(F32)[0:1]))
    stats = ar_sum(1)
    head_mean = stats[:, 0:1] / D
    head_scale = lax.rsqrt(stats[:, 1:2] / D - head_mean * head_mean + epsilon)
    weight_sum = stats[:, 3:4]
    logits = head_scale * (stats[:, 2:3] - head_mean * weight_sum)
    logit_grads = loss_scale * (jax.nn.sigmoid(logits) - labels)
    mean_grads = logit_grads * weight_sum / D
    mean_product = logit_grads * logits / D
    for xx, (active, slope, vector) in enumerate(gelus):
        head_centered = (active - head_mean) * head_scale
        activated_grads = head_scale * (
            logit_grads * vector - mean_grads - head_centered * mean_product
        )
        pre[xx] = (activated_grads * slope).astype(BF)
    spread_back(lambda xx: pre[xx], lambda xx, rows: Wod[xx, rows, B : 2 * B], b1, b1_buf, 0)
    hidden_grads = own_sum(b1_buf, 0)
    hr_buf[x] = hidden_grads.astype(BF)
    ax_start(hr_buf, 1)
    ax_wait(hr_buf, 1)
    spread_back(lambda xx: hr_buf[xx], lambda xx, rows: Wod[xx, rows, 0:B], b2, b2_buf, 1)
    out_rounded = own_sum(b2_buf, 1).astype(BF)

    prob_grads = dot_nt(out_rounded, values)
    value_grads = dot_tn(prob_rounded, out_rounded)
    capped_grads = probabilities * (
        prob_grads - jnp.sum(probabilities * prob_grads, axis=-1, keepdims=True)
    )
    ratio = capped / soft_limit
    score_rounded = (capped_grads * (1.0 - ratio * ratio) / math.sqrt(B)).astype(BF)
    query_grads = dot(score_rounded, keys)
    key_grads = dot_tn(score_rounded, queries)
    g_buf[x] = jnp.concatenate([query_grads, key_grads, value_grads], axis=1).astype(BF)
    ax_start(g_buf, 2)
    ax_wait(g_buf, 2)
    def send_sums():
        plain, weighted = jnp.zeros((B, B), F32), jnp.zeros((B, B), F32)
        for k in range(Z):
            block = b3[k].astype(F32)
            plain = plain + block * gains[k, 0:1]
            weighted = weighted + block * cgain[k]
        columns = [jnp.sum(total, axis=1, keepdims=True) for total in (plain, weighted)]
        ar_start(columns_to_rows(columns), 2)

    old = list(pending)
    pending.clear()

    def finish_old():
        for done in old:
            done()

    spread_back(lambda xx: g_buf[xx], lambda xx, rows: Wq[xx, rows, :], b3, b3_buf, 2, send_sums)
    finish_old()
    scaled = own_sum(b3_buf, 2) * gain
    stats = ar_sum(2)
    input_grads = hidden_grads + inv_std * (
        scaled - stats[:, 0:1] / D - centered * (stats[:, 1:2] / D)
    )

    gslot_src[...] = dot(put_hot, input_grads.astype(BF)).astype(BF).reshape(T, cap, B)
    tok_start(gslot_src, gslot_buf, 2)
    tok_wait(gslot_src, gslot_buf, 2)
    grad_out[...] = gslot_buf[...].reshape(R, B)

    finish()


def table_kernel(tile, grad_ref, req_ref, out_ref):
    wanted = req_ref[0:1, :]
    group = jnp.floor(wanted * (1.0 / B))
    within = jnp.where(iota((B, wanted.shape[1]), 0).astype(F32) == wanted - group * B, 1.0, 0.0)
    within = within.astype(BF)
    grads = grad_ref[...]
    first = pl.program_id(0) * (tile // B)
    for g in range(tile // B):
        here = jnp.where(group == (first + g).astype(F32), 1.0, 0.0).astype(BF)
        out_ref[g * B : (g + 1) * B, :] = dot(within * here, grads).astype(BF)


def local(
    X, Z, Y, C,
    embeddings, norm_gain, query_key_value_weight, out_weight, dense_weight, head_weight,
    token_ids, replace_ids, masked, labels, segments,
):
    vocab_rows = embeddings.shape[0]
    V, T = X * Z, Y * C
    cap = 2 * B // T
    R = T * cap
    vm = pl.BlockSpec(memory_space=pltpu.VMEM)
    dma = pltpu.SemaphoreType.DMA
    rows = query_key_value_weight.shape[0]
    VM = pltpu.VMEM
    right = Y // 2
    grads, requests = pl.pallas_call(
        functools.partial(main_kernel, X, Z, Y, C, vocab_rows),
        out_shape=(
            jax.ShapeDtypeStruct((R, B), BF),
            jax.ShapeDtypeStruct((8, R), F32),
        ),
        in_specs=[pl.BlockSpec(memory_space=pltpu.HBM)] * 11,
        out_specs=(vm, vm),
        scratch_shapes=[
            VM((vocab_rows, B), BF),
            VM((rows, 3 * B), BF),
            VM((rows, 2 * B), BF),
            VM((X, Z * B, 3 * B), BF),
            VM((X, Z * B, 2 * B), BF),
            VM((1, B), jnp.int32), VM((1, B), jnp.int32), VM((1, B), jnp.int32),
            VM((1, B), BF), VM((1, B), BF),
            VM((1, B), jnp.int32), VM((1, B), jnp.int32),
            VM((T, cap, B), F32), VM((T, cap, B), F32),
            VM((T, cap, B), BF), VM((T, cap, B), BF),
            VM((T, cap, B), F32), VM((T, cap, B), F32),
            VM((T, cap, B), BF), VM((T, cap, B), BF),
            VM((B + 16, B), BF), VM((Z, B + 16, B), BF),
            VM((B, B), BF), VM((Z, B, B), BF),
            VM((B, B), BF), VM((Z, B, B), BF),
            VM((X, B, 3 * B), BF), VM((X - 1, B, 3 * B), BF),
            VM((X, B, B), BF), VM((X - 1, B, B), BF),
            VM((X, B, B), BF), VM((X - 1, B, B), BF),
            VM((Z, B, B), BF), VM((Z, B, B), BF),
            VM((X, B, B), BF), VM((Z, B, B), BF), VM((Z, B, B), BF),
            VM((X, B, 3 * B), BF), VM((Z, B, B), BF), VM((Z, B, B), BF),
            VM((B, Z * B), BF), VM((Z, B, B), F32), VM((Z, 8, B), F32),
            VM((X, B, B), F32), VM((X, B, B), BF), VM((X, 16, B), BF),
            VM((3, 8, B), F32), VM((3, V, 8, B), F32),
            dma((11,)), dma(()), dma(()), dma((X // C, 2)),
            dma((2, X // C, 2, right)), dma((2, X // C)),
            dma((2, X // C)), dma((2, X // C)),
            dma((4,)), dma((4,)), dma((3,)), dma((3,)),
            dma((3,)), dma((3,)), dma((4,)), dma((4,)),
            dma((3,)), dma((3,)), dma((3,)), dma((3,)),
        ],
        compiler_params=pltpu.CompilerParams(
            collective_id=0, has_side_effects=True, vmem_limit_bytes=60 * 1024 * 1024
        ),
    )(
        embeddings,
        norm_gain.reshape(1, B),
        query_key_value_weight.reshape(rows, 3 * B),
        out_weight,
        dense_weight,
        head_weight.reshape(1, B),
        token_ids, replace_ids, masked, labels, segments,
    )
    tile = min(1024, vocab_rows)
    return pl.pallas_call(
        functools.partial(table_kernel, tile),
        grid=(vocab_rows // tile,),
        out_shape=jax.ShapeDtypeStruct((vocab_rows, B), BF),
        in_specs=[
            pl.BlockSpec((R, B), lambda i: (0, 0)),
            pl.BlockSpec((8, R), lambda i: (0, 0)),
        ],
        out_specs=pl.BlockSpec((tile, B), lambda i: (i, 0)),
        compiler_params=pltpu.CompilerParams(vmem_limit_bytes=60 * 1024 * 1024),
    )(grads, requests)


def solution(mesh):
    V, T = mesh.shape["vocab"], mesh.shape["tok"]
    X = 4 if V == 32 else 2
    C = 2
    placed = (
        P("tok", "vocab"),
        P("vocab"),
        P("tok", "vocab", None),
        P("tok", "vocab"),
        P("tok", "vocab"),
        P("vocab"),
        P("tok", None),
        P("tok", None),
        P("tok", None),
        P("tok", None),
        P("tok", None),
    )
    return jax.shard_map(
        functools.partial(local, X, V // X, T // C, C),
        mesh=mesh, in_specs=placed, out_specs=P("tok", "vocab"), check_vma=False,
    )
```

```python
import functools
import math

import jax
import jax.numpy as jnp
from jax import lax
from jax.experimental import pallas as pl
from jax.experimental.pallas import tpu as pltpu
from jax.sharding import PartitionSpec as P

MESH = pl.DeviceIdType.MESH
BF = jnp.bfloat16
F32 = jnp.float32
B = 128

soft_limit = 50.0
loss_scale = 64.0
epsilon = 1e-05
inv_root_two = 0.7071067811865476
inv_root_tau = 0.3989422804014327


def dot(a, b):
    return jnp.dot(a, b, preferred_element_type=F32)


def dot_nt(a, b):
    return lax.dot_general(a, b, (((1,), (1,)), ((), ())), preferred_element_type=F32)


def dot_tn(a, b):
    return lax.dot_general(a, b, (((0,), (0,)), ((), ())), preferred_element_type=F32)


def iota(shape, dim):
    return lax.broadcasted_iota(jnp.int32, shape, dim)


def columns_to_rows(columns):
    lane = iota((B, B), 1)
    total = jnp.zeros((B, B), F32)
    for i, column in enumerate(columns):
        total = jnp.where(lane == i, column, total)
    return total.T[:8]


def rows_to_square(rows):
    return jnp.concatenate([rows, jnp.zeros((B - 8, B), F32)], axis=0).T


def row_to_square(row):
    return jnp.broadcast_to(row, (B, B)).T


def main_kernel(
    X, Z, Y, C, vocab_rows,
    emb_hbm, gain_hbm, wq_hbm, wo_hbm, wd_hbm, hw_hbm,
    tok_hbm, rep_hbm, mask_hbm, lab_hbm, seg_hbm,
    grad_out, req_out,
    emb, wq_ref, wod_src, Wq, Wod,
    tok_ref, rep_ref, mask_ref, gain_ref, hw_ref, lab_ref, seg_ref,
    ids_src, ids_buf, row_src, row_buf, st_src, st_buf, gslot_src, gslot_buf,
    x_src, x_buf, h_src, h_buf, d_src, d_buf,
    pq, pq_buf, po, po_buf, pd, pd_buf,
    b1, b1_buf, hr_buf, b2, b2_buf, g_buf, b3, b3_buf,
    nrm, cgain, gains, dl_buf, pre, hw_buf, ar_src, ar_buf,
    in_sem, w1q_sem, w1o_sem, w1_send, w2_recv, w2_send, sib_recv, sib_send,
    t_recv, t_send, e_recv, e_send, rx_recv, rx_send, ax_recv, ax_send,
    r_recv, r_send, s_recv, s_send,
):
    V, T = X * Z, Y * C
    Xc = X // C
    D = V * B
    K = Z * B
    v, t = lax.axis_index("vocab"), lax.axis_index("tok")
    x, z = v // Z, v % Z
    y, c = t // C, t % C
    cap = 2 * B // T
    R = T * cap

    def dev(xx, zz, yy, cc):
        return (xx * Z + zz, yy * C + cc)

    def far_first(i, size):
        return size // 2 + ((i + 1) // 2) * (1 - 2 * (i % 2))

    def remote(src, dst, send, recv, device):
        return pltpu.make_async_remote_copy(
            src_ref=src, dst_ref=dst, send_sem=send, recv_sem=recv,
            device_id=device, device_id_type=MESH,
        )

    pending = []

    def finish():
        for done in pending:
            done()
        pending.clear()

    def wait_bytes(ref, sem):
        pltpu.make_async_copy(ref, ref, sem).wait()

    wanted_here = (
        (tok_hbm, tok_ref), (rep_hbm, rep_ref), (mask_hbm, mask_ref),
        (wq_hbm, wq_ref), (wo_hbm, wod_src.at[:, pl.ds(0, B)]),
        (wd_hbm, wod_src.at[:, pl.ds(B, B)]), (emb_hbm, emb),
        (gain_hbm, gain_ref), (hw_hbm, hw_ref), (lab_hbm, lab_ref), (seg_hbm, seg_ref),
    )
    copies = [
        pltpu.make_async_copy(src, dst, in_sem.at[i]) for i, (src, dst) in enumerate(wanted_here)
    ]
    for copy in copies:
        copy.start()
    barrier = pltpu.get_barrier_semaphore()

    def greet_vocab(d, carry):
        pl.semaphore_signal(barrier, inc=1, device_id=((v + d) % V, t), device_id_type=MESH)
        return carry

    def greet_tok(d, carry):
        pl.semaphore_signal(barrier, inc=1, device_id=(v, (t + d) % T), device_id_type=MESH)
        return carry

    lax.fori_loop(1, V, greet_vocab, 0)
    lax.fori_loop(1, T, greet_tok, 0)
    turn = y // (Z // X)
    same_core = (x // Xc) == c
    from_core = ((x + turn) % X) // Xc
    other_source = from_core != c

    @pl.when(jnp.logical_not(same_core))
    def _():
        for i in range(Xc):
            to = dev((Xc * c + i + X - turn) % X, z, y, x // Xc)
            pl.semaphore_signal(barrier, inc=1, device_id=to, device_id_type=MESH)

    @pl.when(other_source)
    def _():
        for i in range(Xc):
            to = dev(Xc * c + i, z, y, from_core)
            pl.semaphore_signal(barrier, inc=1, device_id=to, device_id_type=MESH)

    for copy in copies[:3]:
        copy.wait()
    chosen = jnp.where(mask_ref[...] == 1, rep_ref[...], tok_ref[...])
    owner = chosen // vocab_rows
    offset = (chosen - owner * vocab_rows).astype(F32)
    owner_f = owner.astype(F32)
    earlier = iota((B, B), 0) < iota((B, B), 1)
    same_owner = row_to_square(owner_f) == owner_f
    slot = jnp.sum(jnp.where(same_owner & earlier, 1.0, 0.0), axis=0, keepdims=True)
    place = owner_f * float(cap) + slot
    place_hot = iota((R, B), 0).astype(F32) == place
    wanted = jnp.sum(jnp.where(place_hot, offset, 0.0), axis=1, keepdims=True)
    ids_src[...] = jnp.broadcast_to(wanted, (R, B)).reshape(T, cap, B)

    pl.semaphore_wait(
        barrier,
        V - 1 + T - 1
        + Xc * jnp.where(same_core, 0, 1)
        + Xc * jnp.where(other_source, 1, 0),
    )

    def tok_start(src, buf, n):
        buf[t] = src[t]

        def send(i, carry):
            cd = (c + C - 1 - i % C) % C
            to = (y + far_first(i // C, Y)) % Y * C + cd
            remote(src.at[to], buf.at[t], t_send.at[n], t_recv.at[n], (v, to)).start()
            return carry

        lax.fori_loop(0, T - 1, send, 0)
        pending.append(lambda: wait_bytes(src.at[pl.ds(0, T - 1)], t_send.at[n]))

    def tok_wait(src, buf, n):
        wait_bytes(buf.at[pl.ds(0, T - 1)], t_recv.at[n])

    tok_start(ids_src, ids_buf, 0)

    def w1_each(act):
        for i in range(Xc):
            xd, cd = (Xc * c + i + X - turn) % X, x // Xc
            mine = (xd == x) & same_core
            rows = pl.ds(i * B, B)
            dst_rows = pl.ds(pl.multiple_of(y * B, B), B)
            q = (wq_ref.at[rows], Wq.at[x, dst_rows], w1q_sem)
            o = (wod_src.at[rows], Wod.at[x, dst_rows], w1o_sem)
            for a, (src, dst, sem) in enumerate((q, o)):
                act(mine, src, dst, sem, w1_send.at[i, a], dev(xd, z, y, cd))

    def w1_go(mine, src, dst, sem, send, device):
        @pl.when(mine)
        def _():
            pltpu.make_async_copy(src, dst, sem).start()

        @pl.when(jnp.logical_not(mine))
        def _():
            remote(src, dst, send, sem, device).start()

    def w1_end(mine, src, dst, sem, send, device):
        @pl.when(jnp.logical_not(mine))
        def _():
            wait_bytes(src, send)

    for copy in copies[3:6]:
        copy.wait()
    w1_each(w1_go)
    pending.append(lambda: w1_each(w1_end))
    pending.append(lambda: w2_done())

    arrays = (Wq, Wod)
    half_up, half_down = Y // 2, Y - 1 - Y // 2

    def block_of(a, i, k):
        return arrays[a].at[Xc * c + i, pl.ds(pl.multiple_of(k * B, B), B)]

    def hops_of(i, way):
        return half_up if way == i % 2 else half_down

    def hop(a, i, h, way):
        step = 1 if way == 0 else Y - 1
        ref = block_of(a, i, (y + (Y - step) * (h - 1)) % Y)
        return remote(
            ref, ref, w2_send.at[a, i], w2_recv.at[a, i, way, h - 1],
            dev(x, z, (y + step) % Y, c),
        )

    def sibling(a, i, k):
        ref = block_of(a, i, k)
        return remote(
            ref, ref, sib_send.at[a, i], sib_recv.at[a, i], dev(x, z, y, (c + 1) % C)
        )

    def w2_begin(a):
        wait_bytes(arrays[a].at[pl.ds(0, Xc), pl.ds(0, B)], (w1q_sem, w1o_sem)[a])
        for i in range(Xc):
            for way in (0, 1):
                if hops_of(i, way) >= 1:
                    hop(a, i, 1, way).start()
        for i in range(Xc):
            sibling(a, i, y).start()

    def w2_forward(a, i, h):
        if i >= Xc:
            return
        for way in (0, 1):
            if h <= hops_of(i, way):
                hop(a, i, h, way).wait_recv()
                if h + 1 <= hops_of(i, way):
                    hop(a, i, h + 1, way).start()
        for way in (0, 1):
            if h <= hops_of(i, way):
                step = 1 if way == 0 else Y - 1
                sibling(a, i, (y + (Y - step) * h) % Y).start()

    def w2_ready(a):
        for i in range(Xc):
            wait_bytes(arrays[a].at[0], sib_recv.at[a, i])

    def w2_done():
        for a in (0, 1):
            for i in range(Xc):
                wait_bytes(arrays[a].at[0, pl.ds(0, (Y - 1) * B)], w2_send.at[a, i])
                wait_bytes(arrays[a].at[0], sib_send.at[a, i])

    row = (z + X - x) % X
    at_home = x == row

    def block_done(ref, sem):
        @pl.when(at_home)
        def _():
            wait_bytes(ref.at[pl.ds(0, Z - 1)], sem)

        @pl.when(jnp.logical_not(at_home))
        def _():
            wait_bytes(ref, sem)

    def row_start(src, buf, n):
        k = v // X
        for j in range(Z):
            zd = (z + far_first(j, Z)) % Z
            mine = at_home & (zd == z)

            @pl.when(mine)
            def _():
                pltpu.make_async_copy(src, buf.at[k], e_recv.at[n]).start()

            @pl.when(jnp.logical_not(mine))
            def _():
                remote(src, buf.at[k], e_send.at[n], e_recv.at[n], dev(row, zd, y, c)).start()

        pending.append(lambda: block_done(buf, e_send.at[n]))

    def row_wait(src, buf, n):
        wait_bytes(buf, e_recv.at[n])

    def rx_start(part, buf, n):
        for d in [far_first(i, X) for i in range(X - 1)]:
            to = (x + d) % X
            remote(
                part.at[to], buf.at[d - 1], rx_send.at[n], rx_recv.at[n], dev(to, z, y, c)
            ).start()
        pending.append(lambda: wait_bytes(buf, rx_send.at[n]))

    def rx_sum(part, buf, n):
        wait_bytes(buf, rx_recv.at[n])
        total = part[x].astype(F32)
        for d in range(1, X):
            total = total + buf[d - 1].astype(F32)
        return total

    def ax_start(buf, n):
        for d in [far_first(i, X) for i in range(X - 1)]:
            remote(
                buf.at[x], buf.at[x], ax_send.at[n], ax_recv.at[n], dev((x + d) % X, z, y, c)
            ).start()
        pending.append(lambda: wait_bytes(buf.at[pl.ds(0, X - 1)], ax_send.at[n]))

    def ax_wait(buf, n):
        wait_bytes(buf.at[pl.ds(0, X - 1)], ax_recv.at[n])

    def own_start(part, buf, n):
        for j in range(Z):
            zd = (z + far_first(j, Z)) % Z
            xd = (zd % X + X - x) % X
            k = xd * (Z // X) + zd // X
            mine = (xd == x) & (zd == z)

            @pl.when(mine)
            def _():
                pltpu.make_async_copy(part.at[k], buf.at[z], r_recv.at[n]).start()

            @pl.when(jnp.logical_not(mine))
            def _():
                to = dev(xd, zd, y, c)
                remote(part.at[k], buf.at[z], r_send.at[n], r_recv.at[n], to).start()

        pending.append(lambda: block_done(part, r_send.at[n]))

    def own_sum(buf, n):
        wait_bytes(buf, r_recv.at[n])
        total = buf[0].astype(F32)
        for k in range(1, Z):
            total = total + buf[k].astype(F32)
        return total

    def spread_back(left, weights, part, buf, n, seen=None):
        step = 2
        for first in range(0, Z, step):
            total = None
            for xx in range(X):
                term = dot_nt(left(xx), weights(xx, pl.ds(first * B, step * B)))
                total = term if total is None else total + term
            for k in range(first, first + step):
                part[k] = total[:, (k - first) * B : (k - first + 1) * B].astype(BF)
        if seen is not None:
            seen()
        own_start(part, buf, n)

    def ar_start(rows, n):
        ar_src[n] = rows
        ar_buf[n, 0] = rows

        def send(i, carry):
            to = dev((x + far_first(i % X, X)) % X, (z + far_first(i // X, Z)) % Z, y, c)
            remote(ar_src.at[n], ar_buf.at[n, i + 1], s_send.at[n], s_recv.at[n], to).start()
            return carry

        lax.fori_loop(0, V - 1, send, 0)
        pending.append(lambda: wait_bytes(ar_buf.at[n, pl.ds(1, V - 1)], s_send.at[n]))

    def ar_sum(n):
        wait_bytes(ar_buf.at[n, pl.ds(1, V - 1)], s_recv.at[n])
        return rows_to_square(jnp.sum(ar_buf[n], axis=0))

    for copy in copies[6:]:
        copy.wait()
    hw_buf[x] = jnp.broadcast_to(hw_ref[...].astype(F32), (16, B)).astype(BF)
    ax_start(hw_buf, 3)
    put_hot = jnp.where(place_hot, 1.0, 0.0).astype(BF)
    place_square = row_to_square(place)
    take_hot = jnp.concatenate(
        [
            jnp.where(place_square == (iota((B, B), 1) + first).astype(F32), 1.0, 0.0)
            for first in range(0, R, B)
        ],
        axis=1,
    ).astype(BF)
    segment_f = seg_ref[...].astype(F32)
    same_segment = row_to_square(segment_f) == segment_f
    labels = row_to_square(lab_ref[...].astype(F32))[:, 0:1]
    gain = gain_ref[...].astype(F32)
    head_vector = hw_ref[...].astype(F32)
    x_src[B : B + 16, :] = jnp.broadcast_to(gain, (16, B)).astype(BF)
    tok_wait(ids_src, ids_buf, 0)
    requested = ids_buf[...].reshape(R, B)
    chunk = 512

    w2_begin(0)

    def fetch(i, total):
        base = i * chunk
        hot = jnp.concatenate(
            [
                jnp.where(
                    requested == (iota((R, B), 1) + (base + first)).astype(F32), 1.0, 0.0
                ).astype(BF)
                for first in range(0, chunk, B)
            ],
            axis=1,
        )
        return total + dot(hot, emb[pl.ds(pl.multiple_of(base, chunk), chunk), :])

    fetched = lax.fori_loop(0, vocab_rows // chunk, fetch, jnp.zeros((R, B), F32))
    row_src[...] = fetched.astype(BF).reshape(T, cap, B)
    tok_start(row_src, row_buf, 1)
    row_sums = []
    for first in range(0, R, B):
        piece = fetched[first : first + B]
        row_sums.append(jnp.sum(piece, axis=1, keepdims=True))
        row_sums.append(jnp.sum(piece * piece, axis=1, keepdims=True))
    ar_start(columns_to_rows(row_sums), 0)
    for first in range(0, R, B):
        req_out[:, first : first + B] = requested[first : first + B].T[:8]
    w2_forward(0, 0, 1)
    w2_forward(0, 1, 1)
    tok_wait(row_src, row_buf, 1)
    features = dot(take_hot, row_buf[...].reshape(R, B))
    x_src[0:B, :] = features.astype(BF)
    row_start(x_src, x_buf, 0)
    stats = ar_sum(0)
    w2_forward(0, 0, 2)
    lane = iota((B, B), 1)
    for first in range(0, R, B):
        i = 2 * (first // B)
        pair = jnp.where(lane == 0, stats[:, i : i + 1], stats[:, i + 1 : i + 2])
        st_src[first // cap : (first + B) // cap] = pair.reshape(B // cap, cap, B)
    tok_start(st_src, st_buf, 3)
    w2_forward(0, 1, 2)
    w2_forward(0, 0, 3)
    w2_forward(0, 1, 3)
    w2_begin(1)
    tok_wait(st_src, st_buf, 3)
    stats = jnp.dot(
        take_hot.astype(F32),
        st_buf[...].reshape(R, B),
        preferred_element_type=F32,
        precision=lax.Precision.HIGHEST,
    )
    row_mean = stats[:, 0:1] / D
    variance = stats[:, 1:2] / D - row_mean * row_mean
    inv_std = lax.rsqrt(variance + epsilon)
    centered = (features - row_mean) * inv_std
    row_wait(x_src, x_buf, 0)
    for k in range(Z):
        block = x_buf[k, 0:B, :].astype(F32)
        block_gain = x_buf[k, B : B + 16, :].astype(F32)[0:8]
        gains[k] = block_gain
        normed = ((block - row_mean) * inv_std) * block_gain[0:1]
        cgain[k] = normed
        nrm[:, k * B : (k + 1) * B] = normed.astype(BF)
    w2_forward(0, 0, 4)
    w2_forward(0, 1, 4)
    w2_forward(1, 0, 1)
    w2_forward(1, 1, 1)
    w2_ready(0)
    for xx in range(X):
        pq[xx] = dot(nrm[...], Wq[xx]).astype(BF)
    rx_start(pq, pq_buf, 0)
    w2_forward(1, 0, 2)
    w2_forward(1, 1, 2)
    qkv = rx_sum(pq, pq_buf, 0).astype(BF)
    queries, keys, values = qkv[:, :B], qkv[:, B : 2 * B], qkv[:, 2 * B :]
    raw = dot_nt(queries, keys) / math.sqrt(B)
    capped = soft_limit * jnp.tanh(raw / soft_limit)
    exps = jnp.where(same_segment, jnp.exp(capped), 0.0)
    probabilities = exps / jnp.sum(exps, axis=-1, keepdims=True)
    prob_rounded = probabilities.astype(BF)
    h_src[...] = dot(prob_rounded, values).astype(BF)
    row_start(h_src, h_buf, 1)
    for h in (3, 4):
        w2_forward(1, 0, h)
        w2_forward(1, 1, h)
    row_wait(h_src, h_buf, 1)
    w2_ready(1)

    heads_row = jnp.concatenate([h_buf[k] for k in range(Z)], axis=1)
    for xx in range(X):
        po[xx] = dot(heads_row, Wod[xx, :, 0:B]).astype(po.dtype)
    rx_start(po, po_buf, 1)
    hidden = features + rx_sum(po, po_buf, 1)
    d_src[...] = hidden.astype(BF)
    row_start(d_src, d_buf, 2)
    row_wait(d_src, d_buf, 2)

    dense_row = jnp.concatenate([d_buf[k] for k in range(Z)], axis=1)
    for xx in range(X):
        pd[xx] = dot(dense_row, Wod[xx, :, B : 2 * B]).astype(pd.dtype)
    rx_start(pd, pd_buf, 2)
    dense_linear = rx_sum(pd, pd_buf, 2)
    dl_buf[x] = dense_linear
    activated = dense_linear * (0.5 * (1.0 + lax.erf(dense_linear * inv_root_two)))
    ar_start(
        columns_to_rows(
            [
                jnp.sum(activated, axis=1, keepdims=True),
                jnp.sum(activated * activated, axis=1, keepdims=True),
                jnp.sum(activated * head_vector, axis=1, keepdims=True),
                jnp.broadcast_to(jnp.sum(head_vector, axis=1, keepdims=True), (B, 1)),
            ]
        ),
        1,
    )
    ax_start(dl_buf, 0)
    ax_wait(hw_buf, 3)
    ax_wait(dl_buf, 0)
    gelus = []
    for xx in range(X):
        linear = dl_buf[xx]
        phi = 0.5 * (1.0 + lax.erf(linear * inv_root_two))
        slope = phi + linear * jnp.exp(-0.5 * linear * linear) * inv_root_tau
        gelus.append((linear * phi, slope, hw_buf[xx].astype(F32)[0:1]))
    stats = ar_sum(1)
    head_mean = stats[:, 0:1] / D
    head_scale = lax.rsqrt(stats[:, 1:2] / D - head_mean * head_mean + epsilon)
    weight_sum = stats[:, 3:4]
    logits = head_scale * (stats[:, 2:3] - head_mean * weight_sum)
    logit_grads = loss_scale * (jax.nn.sigmoid(logits) - labels)
    mean_grads = logit_grads * weight_sum / D
    mean_product = logit_grads * logits / D
    for xx, (active, slope, vector) in enumerate(gelus):
        head_centered = (active - head_mean) * head_scale
        activated_grads = head_scale * (
            logit_grads * vector - mean_grads - head_centered * mean_product
        )
        pre[xx] = (activated_grads * slope).astype(BF)
    spread_back(lambda xx: pre[xx], lambda xx, rows: Wod[xx, rows, B : 2 * B], b1, b1_buf, 0)
    hidden_grads = own_sum(b1_buf, 0)
    hr_buf[x] = hidden_grads.astype(BF)
    ax_start(hr_buf, 1)
    ax_wait(hr_buf, 1)
    spread_back(lambda xx: hr_buf[xx], lambda xx, rows: Wod[xx, rows, 0:B], b2, b2_buf, 1)
    out_rounded = own_sum(b2_buf, 1).astype(BF)

    prob_grads = dot_nt(out_rounded, values)
    value_grads = dot_tn(prob_rounded, out_rounded)
    capped_grads = probabilities * (
        prob_grads - jnp.sum(probabilities * prob_grads, axis=-1, keepdims=True)
    )
    ratio = capped / soft_limit
    score_rounded = (capped_grads * (1.0 - ratio * ratio) / math.sqrt(B)).astype(BF)
    query_grads = dot(score_rounded, keys)
    key_grads = dot_tn(score_rounded, queries)
    g_buf[x] = jnp.concatenate([query_grads, key_grads, value_grads], axis=1).astype(BF)
    ax_start(g_buf, 2)
    ax_wait(g_buf, 2)
    def send_sums():
        plain, weighted = jnp.zeros((B, B), F32), jnp.zeros((B, B), F32)
        for k in range(Z):
            block = b3[k].astype(F32)
            plain = plain + block * gains[k, 0:1]
            weighted = weighted + block * cgain[k]
        columns = [jnp.sum(total, axis=1, keepdims=True) for total in (plain, weighted)]
        ar_start(columns_to_rows(columns), 2)

    old = list(pending)
    pending.clear()

    def finish_old():
        for done in old:
            done()

    spread_back(lambda xx: g_buf[xx], lambda xx, rows: Wq[xx, rows, :], b3, b3_buf, 2, send_sums)
    finish_old()
    scaled = own_sum(b3_buf, 2) * gain
    stats = ar_sum(2)
    input_grads = hidden_grads + inv_std * (
        scaled - stats[:, 0:1] / D - centered * (stats[:, 1:2] / D)
    )

    gslot_src[...] = dot(put_hot, input_grads.astype(BF)).astype(BF).reshape(T, cap, B)
    tok_start(gslot_src, gslot_buf, 2)
    tok_wait(gslot_src, gslot_buf, 2)
    grad_out[...] = gslot_buf[...].reshape(R, B)

    finish()


def table_kernel(tile, grad_ref, req_ref, out_ref):
    wanted = req_ref[0:1, :]
    group = jnp.floor(wanted * (1.0 / B))
    within = jnp.where(iota((B, wanted.shape[1]), 0).astype(F32) == wanted - group * B, 1.0, 0.0)
    within = within.astype(BF)
    grads = grad_ref[...]
    first = pl.program_id(0) * (tile // B)
    for g in range(tile // B):
        here = jnp.where(group == (first + g).astype(F32), 1.0, 0.0).astype(BF)
        out_ref[g * B : (g + 1) * B, :] = dot(within * here, grads).astype(BF)


def local(
    X, Z, Y, C,
    embeddings, norm_gain, query_key_value_weight, out_weight, dense_weight, head_weight,
    token_ids, replace_ids, masked, labels, segments,
):
    vocab_rows = embeddings.shape[0]
    V, T = X * Z, Y * C
    cap = 2 * B // T
    R = T * cap
    vm = pl.BlockSpec(memory_space=pltpu.VMEM)
    dma = pltpu.SemaphoreType.DMA
    rows = query_key_value_weight.shape[0]
    VM = pltpu.VMEM
    right = Y // 2
    grads, requests = pl.pallas_call(
        functools.partial(main_kernel, X, Z, Y, C, vocab_rows),
        out_shape=(
            jax.ShapeDtypeStruct((R, B), BF),
            jax.ShapeDtypeStruct((8, R), F32),
        ),
        in_specs=[pl.BlockSpec(memory_space=pltpu.HBM)] * 11,
        out_specs=(vm, vm),
        scratch_shapes=[
            VM((vocab_rows, B), BF),
            VM((rows, 3 * B), BF),
            VM((rows, 2 * B), BF),
            VM((X, Z * B, 3 * B), BF),
            VM((X, Z * B, 2 * B), BF),
            VM((1, B), jnp.int32), VM((1, B), jnp.int32), VM((1, B), jnp.int32),
            VM((1, B), BF), VM((1, B), BF),
            VM((1, B), jnp.int32), VM((1, B), jnp.int32),
            VM((T, cap, B), F32), VM((T, cap, B), F32),
            VM((T, cap, B), BF), VM((T, cap, B), BF),
            VM((T, cap, B), F32), VM((T, cap, B), F32),
            VM((T, cap, B), BF), VM((T, cap, B), BF),
            VM((B + 16, B), BF), VM((Z, B + 16, B), BF),
            VM((B, B), BF), VM((Z, B, B), BF),
            VM((B, B), BF), VM((Z, B, B), BF),
            VM((X, B, 3 * B), BF), VM((X - 1, B, 3 * B), BF),
            VM((X, B, B), BF), VM((X - 1, B, B), BF),
            VM((X, B, B), BF), VM((X - 1, B, B), BF),
            VM((Z, B, B), BF), VM((Z, B, B), BF),
            VM((X, B, B), BF), VM((Z, B, B), BF), VM((Z, B, B), BF),
            VM((X, B, 3 * B), BF), VM((Z, B, B), BF), VM((Z, B, B), BF),
            VM((B, Z * B), BF), VM((Z, B, B), F32), VM((Z, 8, B), F32),
            VM((X, B, B), F32), VM((X, B, B), BF), VM((X, 16, B), BF),
            VM((3, 8, B), F32), VM((3, V, 8, B), F32),
            dma((11,)), dma(()), dma(()), dma((X // C, 2)),
            dma((2, X // C, 2, right)), dma((2, X // C)),
            dma((2, X // C)), dma((2, X // C)),
            dma((4,)), dma((4,)), dma((3,)), dma((3,)),
            dma((3,)), dma((3,)), dma((4,)), dma((4,)),
            dma((3,)), dma((3,)), dma((3,)), dma((3,)),
        ],
        compiler_params=pltpu.CompilerParams(
            collective_id=0, has_side_effects=True, vmem_limit_bytes=60 * 1024 * 1024
        ),
    )(
        embeddings,
        norm_gain.reshape(1, B),
        query_key_value_weight.reshape(rows, 3 * B),
        out_weight,
        dense_weight,
        head_weight.reshape(1, B),
        token_ids, replace_ids, masked, labels, segments,
    )
    tile = min(4096, vocab_rows)
    return pl.pallas_call(
        functools.partial(table_kernel, tile),
        grid=(vocab_rows // tile,),
        out_shape=jax.ShapeDtypeStruct((vocab_rows, B), BF),
        in_specs=[
            pl.BlockSpec((R, B), lambda i: (0, 0)),
            pl.BlockSpec((8, R), lambda i: (0, 0)),
        ],
        out_specs=pl.BlockSpec((tile, B), lambda i: (i, 0)),
        compiler_params=pltpu.CompilerParams(vmem_limit_bytes=60 * 1024 * 1024),
    )(grads, requests)


def solution(mesh):
    V, T = mesh.shape["vocab"], mesh.shape["tok"]
    X = 4 if V == 32 else 2
    C = 2
    placed = (
        P("tok", "vocab"),
        P("vocab"),
        P("tok", "vocab", None),
        P("tok", "vocab"),
        P("tok", "vocab"),
        P("vocab"),
        P("tok", None),
        P("tok", None),
        P("tok", None),
        P("tok", None),
        P("tok", None),
    )
    return jax.shard_map(
        functools.partial(local, X, V // X, T // C, C),
        mesh=mesh, in_specs=placed, out_specs=P("tok", "vocab"), check_vma=False,
    )
```

```python
import functools
import math

import jax
import jax.numpy as jnp
from jax import lax
from jax.experimental import pallas as pl
from jax.experimental.pallas import tpu as pltpu
from jax.sharding import PartitionSpec as P

MESH = pl.DeviceIdType.MESH
BF = jnp.bfloat16
F32 = jnp.float32
B = 128

soft_limit = 50.0
loss_scale = 64.0
epsilon = 1e-05
inv_root_two = 0.7071067811865476
inv_root_tau = 0.3989422804014327


def dot(a, b):
    return jnp.dot(a, b, preferred_element_type=F32)


def dot_nt(a, b):
    return lax.dot_general(a, b, (((1,), (1,)), ((), ())), preferred_element_type=F32)


def dot_tn(a, b):
    return lax.dot_general(a, b, (((0,), (0,)), ((), ())), preferred_element_type=F32)


def iota(shape, dim):
    return lax.broadcasted_iota(jnp.int32, shape, dim)


def columns_to_rows(columns):
    lane = iota((B, B), 1)
    total = jnp.zeros((B, B), F32)
    for i, column in enumerate(columns):
        total = jnp.where(lane == i, column, total)
    return total.T[:8]


def rows_to_square(rows):
    return jnp.concatenate([rows, jnp.zeros((B - 8, B), F32)], axis=0).T


def row_to_square(row):
    return jnp.broadcast_to(row, (B, B)).T


def main_kernel(
    X, Z, Y, C, vocab_rows,
    emb_hbm, gain_hbm, wq_hbm, wo_hbm, wd_hbm, hw_hbm,
    tok_hbm, rep_hbm, mask_hbm, lab_hbm, seg_hbm,
    grad_out, req_out,
    emb, wq_ref, wod_src, Wq, Wod,
    tok_ref, rep_ref, mask_ref, gain_ref, hw_ref, lab_ref, seg_ref,
    ids_src, ids_buf, row_src, row_buf, st_src, st_buf, gslot_src, gslot_buf,
    g_src, g_all, x_src, x_buf, h_src, h_buf, d_src, d_buf,
    pq, pq_buf, po, po_buf, pd, pd_buf,
    b1, b1_buf, hr_buf, b2, b2_buf, g_buf, b3, b3_buf,
    nrm, cgain, gains, dl_buf, pre, hw_buf, ar_src, ar_buf,
    in_sem, w1q_sem, w1o_sem, w1_send, w2_recv, w2_send, sib_recv, sib_send,
    t_recv, t_send, e_recv, e_send, rx_recv, rx_send, ax_recv, ax_send,
    r_recv, r_send, s_recv, s_send,
):
    V, T = X * Z, Y * C
    Xc = X // C
    D = V * B
    K = Z * B
    v, t = lax.axis_index("vocab"), lax.axis_index("tok")
    x, z = v // Z, v % Z
    y, c = t // C, t % C
    cap = 2 * B // T
    R = T * cap

    def dev(xx, zz, yy, cc):
        return (xx * Z + zz, yy * C + cc)

    def far_first(i, size):
        return size // 2 + ((i + 1) // 2) * (1 - 2 * (i % 2))

    def remote(src, dst, send, recv, device):
        return pltpu.make_async_remote_copy(
            src_ref=src, dst_ref=dst, send_sem=send, recv_sem=recv,
            device_id=device, device_id_type=MESH,
        )

    pending = []

    def finish():
        for done in pending:
            done()
        pending.clear()

    def wait_bytes(ref, sem):
        pltpu.make_async_copy(ref, ref, sem).wait()

    def step_of(way):
        return 1 if way == 0 else Y - 1

    half_up, half_down = Y // 2, Y - 1 - Y // 2

    def hops_of(i, way):
        return half_up if way == i % 2 else half_down

    wanted_here = (
        (tok_hbm, tok_ref), (rep_hbm, rep_ref), (mask_hbm, mask_ref),
        (wq_hbm, wq_ref), (wo_hbm, wod_src.at[:, pl.ds(0, B)]),
        (wd_hbm, wod_src.at[:, pl.ds(B, B)]), (emb_hbm, emb),
        (gain_hbm, gain_ref), (hw_hbm, hw_ref), (lab_hbm, lab_ref), (seg_hbm, seg_ref),
    )
    copies = [
        pltpu.make_async_copy(src, dst, in_sem.at[i]) for i, (src, dst) in enumerate(wanted_here)
    ]
    for copy in copies:
        copy.start()
    barrier = pltpu.get_barrier_semaphore()

    def greet_vocab(d, carry):
        pl.semaphore_signal(barrier, inc=1, device_id=((v + d) % V, t), device_id_type=MESH)
        return carry

    def greet_tok(d, carry):
        pl.semaphore_signal(barrier, inc=1, device_id=(v, (t + d) % T), device_id_type=MESH)
        return carry

    lax.fori_loop(1, V, greet_vocab, 0)
    lax.fori_loop(1, T, greet_tok, 0)
    turn = y // (Z // X)
    same_core = (x // Xc) == c
    from_core = ((x + turn) % X) // Xc
    other_source = from_core != c

    @pl.when(jnp.logical_not(same_core))
    def _():
        for i in range(Xc):
            to = dev((Xc * c + i + X - turn) % X, z, y, x // Xc)
            pl.semaphore_signal(barrier, inc=1, device_id=to, device_id_type=MESH)

    @pl.when(other_source)
    def _():
        for i in range(Xc):
            to = dev(Xc * c + i, z, y, from_core)
            pl.semaphore_signal(barrier, inc=1, device_id=to, device_id_type=MESH)

    ways = [way for way in (0, 1) if hops_of(0, way) >= 1]
    for way in ways:
        ahead, behind = (y + step_of(way)) % Y, (y + Y - step_of(way)) % Y
        sender = ((x + behind // (Z // X)) % X) // Xc
        for i in range(Xc):
            for to in (
                dev((Xc * c + i + X - turn) % X, z, ahead, x // Xc),
                dev(Xc * c + i, z, behind, sender),
            ):
                pl.semaphore_signal(barrier, inc=1, device_id=to, device_id_type=MESH)

    for copy in copies[:3]:
        copy.wait()
    chosen = jnp.where(mask_ref[...] == 1, rep_ref[...], tok_ref[...])
    owner = chosen // vocab_rows
    offset = (chosen - owner * vocab_rows).astype(F32)
    owner_f = owner.astype(F32)
    earlier = iota((B, B), 0) < iota((B, B), 1)
    same_owner = row_to_square(owner_f) == owner_f
    slot = jnp.sum(jnp.where(same_owner & earlier, 1.0, 0.0), axis=0, keepdims=True)
    place = owner_f * float(cap) + slot
    place_hot = iota((R, B), 0).astype(F32) == place
    wanted = jnp.sum(jnp.where(place_hot, offset, 0.0), axis=1, keepdims=True)
    ids_src[...] = jnp.broadcast_to(wanted, (R, B)).reshape(T, cap, B)

    pl.semaphore_wait(
        barrier,
        V - 1 + T - 1 + 2 * Xc * len(ways)
        + Xc * jnp.where(same_core, 0, 1)
        + Xc * jnp.where(other_source, 1, 0),
    )

    def tok_start(src, buf, n):
        buf[t] = src[t]

        def send(i, carry):
            cd = (c + C - 1 - i % C) % C
            to = (y + far_first(i // C, Y)) % Y * C + cd
            remote(src.at[to], buf.at[t], t_send.at[n], t_recv.at[n], (v, to)).start()
            return carry

        lax.fori_loop(0, T - 1, send, 0)
        pending.append(lambda: wait_bytes(src.at[pl.ds(0, T - 1)], t_send.at[n]))

    def tok_wait(src, buf, n):
        wait_bytes(buf.at[pl.ds(0, T - 1)], t_recv.at[n])

    tok_start(ids_src, ids_buf, 0)

    def w1_each(act):
        first, cd = pl.multiple_of(y * B, B), x // Xc
        for a, (src, dst) in enumerate(((wq_ref, Wq), (wod_src, Wod))):
            for i in range(Xc):
                xd = (Xc * c + i + X - turn) % X
                mine = (xd == x) & same_core
                piece, place_ = src.at[pl.ds(i * B, B)], dst.at[x, pl.ds(first, B)]
                for way in ways if a == 0 else ():
                    to = dev(xd, z, (y + step_of(way)) % Y, cd)
                    act(None, piece, place_, w1q_sem.at[1 + way], w1_send.at[i, 2 + way], to)
                sem = w1q_sem.at[0] if a == 0 else w1o_sem
                act(mine, piece, place_, sem, w1_send.at[i, a], dev(xd, z, y, cd))

    def w1_go(mine, src, dst, sem, send, device):
        if mine is None:
            remote(src, dst, send, sem, device).start()
            return

        @pl.when(mine)
        def _():
            pltpu.make_async_copy(src, dst, sem).start()

        @pl.when(jnp.logical_not(mine))
        def _():
            remote(src, dst, send, sem, device).start()

    def w1_end(mine, src, dst, sem, send, device):
        if mine is None:
            wait_bytes(src, send)
            return

        @pl.when(jnp.logical_not(mine))
        def _():
            wait_bytes(src, send)

    for copy in copies[3:6]:
        copy.wait()
    w1_each(w1_go)
    pending.append(lambda: w1_each(w1_end))
    pending.append(lambda: w2_done())

    arrays = (Wq, Wod)
    def block_of(a, i, k):
        return arrays[a].at[Xc * c + i, pl.ds(pl.multiple_of(k * B, B), B)]

    def hop(a, i, h, way):
        step = 1 if way == 0 else Y - 1
        ref = block_of(a, i, (y + (Y - step) * (h - 1)) % Y)
        return remote(
            ref, ref, w2_send.at[a, i], w2_recv.at[a, i, way, h - 1],
            dev(x, z, (y + step) % Y, c),
        )

    def sibling(a, i, k):
        ref = block_of(a, i, k)
        return remote(
            ref, ref, sib_send.at[a, i], sib_recv.at[a, i], dev(x, z, y, (c + 1) % C)
        )

    def w2_first():
        whole = Wq.at[pl.ds(0, Xc), pl.ds(0, B)]
        for way in ways:
            wait_bytes(whole, w1q_sem.at[1 + way])
            for i in range(Xc):
                if hops_of(i, way) >= 2:
                    hop(0, i, 2, way).start()
        wait_bytes(whole, w1q_sem.at[0])
        for i in range(Xc):
            sibling(0, i, y).start()
            for way in ways:
                sibling(0, i, (y + Y - step_of(way)) % Y).start()

    def w2_begin(a):
        wait_bytes(Wod.at[pl.ds(0, Xc), pl.ds(0, B)], w1o_sem)
        for i in range(Xc):
            for way in (0, 1):
                if hops_of(i, way) >= 1:
                    hop(a, i, 1, way).start()
        for i in range(Xc):
            sibling(a, i, y).start()

    def w2_forward(a, i, h):
        if i >= Xc:
            return
        for way in (0, 1):
            if h <= hops_of(i, way):
                hop(a, i, h, way).wait_recv()
                if h + 1 <= hops_of(i, way):
                    hop(a, i, h + 1, way).start()
        for way in (0, 1):
            if h <= hops_of(i, way):
                step = 1 if way == 0 else Y - 1
                sibling(a, i, (y + (Y - step) * h) % Y).start()

    def w2_ready(a):
        for i in range(Xc):
            wait_bytes(arrays[a].at[0], sib_recv.at[a, i])

    def w2_done():
        for a in (0, 1):
            for i in range(Xc):
                sent = Y - 1 - (len(ways) if a == 0 else 0)
                if sent:
                    wait_bytes(arrays[a].at[0, pl.ds(0, sent * B)], w2_send.at[a, i])
                wait_bytes(arrays[a].at[0], sib_send.at[a, i])

    row = (z + X - x) % X
    at_home = x == row

    def block_done(ref, sem):
        @pl.when(at_home)
        def _():
            wait_bytes(ref.at[pl.ds(0, Z - 1)], sem)

        @pl.when(jnp.logical_not(at_home))
        def _():
            wait_bytes(ref, sem)

    def row_start(src, buf, n):
        k = v // X
        for j in range(Z):
            zd = (z + far_first(j, Z)) % Z
            mine = at_home & (zd == z)

            @pl.when(mine)
            def _():
                pltpu.make_async_copy(src, buf.at[k], e_recv.at[n]).start()

            @pl.when(jnp.logical_not(mine))
            def _():
                remote(src, buf.at[k], e_send.at[n], e_recv.at[n], dev(row, zd, y, c)).start()

        pending.append(lambda: block_done(buf, e_send.at[n]))

    def row_wait(src, buf, n):
        wait_bytes(buf, e_recv.at[n])

    def rx_start(part, buf, n):
        for d in [far_first(i, X) for i in range(X - 1)]:
            to = (x + d) % X
            remote(
                part.at[to], buf.at[d - 1], rx_send.at[n], rx_recv.at[n], dev(to, z, y, c)
            ).start()
        pending.append(lambda: wait_bytes(buf, rx_send.at[n]))

    def rx_sum(part, buf, n):
        wait_bytes(buf, rx_recv.at[n])
        total = part[x].astype(F32)
        for d in range(1, X):
            total = total + buf[d - 1].astype(F32)
        return total

    def ax_start(buf, n):
        for d in [far_first(i, X) for i in range(X - 1)]:
            remote(
                buf.at[x], buf.at[x], ax_send.at[n], ax_recv.at[n], dev((x + d) % X, z, y, c)
            ).start()
        pending.append(lambda: wait_bytes(buf.at[pl.ds(0, X - 1)], ax_send.at[n]))

    def ax_wait(buf, n):
        wait_bytes(buf.at[pl.ds(0, X - 1)], ax_recv.at[n])

    def own_start(part, buf, n):
        for j in range(Z):
            zd = (z + far_first(j, Z)) % Z
            xd = (zd % X + X - x) % X
            k = xd * (Z // X) + zd // X
            mine = (xd == x) & (zd == z)

            @pl.when(mine)
            def _():
                pltpu.make_async_copy(part.at[k], buf.at[z], r_recv.at[n]).start()

            @pl.when(jnp.logical_not(mine))
            def _():
                to = dev(xd, zd, y, c)
                remote(part.at[k], buf.at[z], r_send.at[n], r_recv.at[n], to).start()

        pending.append(lambda: block_done(part, r_send.at[n]))

    def own_sum(buf, n):
        wait_bytes(buf, r_recv.at[n])
        total = buf[0].astype(F32)
        for k in range(1, Z):
            total = total + buf[k].astype(F32)
        return total

    def spread_back(left, weights, part, buf, n, seen=None):
        step = 2
        for first in range(0, Z, step):
            total = None
            for xx in range(X):
                term = dot_nt(left(xx), weights(xx, pl.ds(first * B, step * B)))
                total = term if total is None else total + term
            for k in range(first, first + step):
                part[k] = total[:, (k - first) * B : (k - first + 1) * B].astype(BF)
        if seen is not None:
            seen()
        own_start(part, buf, n)

    def ar_start(rows, n):
        ar_src[n] = rows
        ar_buf[n, 0] = rows

        def send(i, carry):
            to = dev((x + far_first(i % X, X)) % X, (z + far_first(i // X, Z)) % Z, y, c)
            remote(ar_src.at[n], ar_buf.at[n, i + 1], s_send.at[n], s_recv.at[n], to).start()
            return carry

        lax.fori_loop(0, V - 1, send, 0)
        pending.append(lambda: wait_bytes(ar_buf.at[n, pl.ds(1, V - 1)], s_send.at[n]))

    def ar_sum(n):
        wait_bytes(ar_buf.at[n, pl.ds(1, V - 1)], s_recv.at[n])
        return rows_to_square(jnp.sum(ar_buf[n], axis=0))

    for copy in copies[6:]:
        copy.wait()
    hw_buf[x] = jnp.broadcast_to(hw_ref[...].astype(F32), (16, B)).astype(BF)
    ax_start(hw_buf, 3)
    put_hot = jnp.where(place_hot, 1.0, 0.0).astype(BF)
    place_square = row_to_square(place)
    take_hot = jnp.concatenate(
        [
            jnp.where(place_square == (iota((B, B), 1) + first).astype(F32), 1.0, 0.0)
            for first in range(0, R, B)
        ],
        axis=1,
    ).astype(BF)
    segment_f = seg_ref[...].astype(F32)
    same_segment = row_to_square(segment_f) == segment_f
    labels = row_to_square(lab_ref[...].astype(F32))[:, 0:1]
    gain = gain_ref[...].astype(F32)
    head_vector = hw_ref[...].astype(F32)
    g_src[...] = jnp.broadcast_to(gain, (16, B)).astype(BF)
    row_start(g_src, g_all, 3)
    tok_wait(ids_src, ids_buf, 0)
    requested = ids_buf[...].reshape(R, B)
    chunk = 512


    def fetch(i, total):
        base = i * chunk
        hot = jnp.concatenate(
            [
                jnp.where(
                    requested == (iota((R, B), 1) + (base + first)).astype(F32), 1.0, 0.0
                ).astype(BF)
                for first in range(0, chunk, B)
            ],
            axis=1,
        )
        return total + dot(hot, emb[pl.ds(pl.multiple_of(base, chunk), chunk), :])

    fetched = lax.fori_loop(0, vocab_rows // chunk, fetch, jnp.zeros((R, B), F32))
    row_src[...] = fetched.astype(BF).reshape(T, cap, B)
    tok_start(row_src, row_buf, 1)
    row_sums = []
    for first in range(0, R, B):
        piece = fetched[first : first + B]
        row_sums.append(jnp.sum(piece, axis=1, keepdims=True))
        row_sums.append(jnp.sum(piece * piece, axis=1, keepdims=True))
    ar_start(columns_to_rows(row_sums), 0)
    w2_first()
    tok_wait(row_src, row_buf, 1)
    features = dot(take_hot, row_buf[...].reshape(R, B))
    x_src[...] = features.astype(BF)
    row_start(x_src, x_buf, 0)
    w2_forward(0, 0, 2)
    w2_forward(0, 1, 2)
    stats = ar_sum(0)
    lane = iota((B, B), 1)
    for first in range(0, R, B):
        i = 2 * (first // B)
        pair = jnp.where(lane == 0, stats[:, i : i + 1], stats[:, i + 1 : i + 2])
        st_src[first // cap : (first + B) // cap] = pair.reshape(B // cap, cap, B)
    tok_start(st_src, st_buf, 3)
    for first in range(0, R, B):
        req_out[:, first : first + B] = requested[first : first + B].T[:8]
    w2_forward(0, 0, 3)
    w2_forward(0, 1, 3)
    w2_begin(1)
    tok_wait(st_src, st_buf, 3)
    stats = jnp.dot(
        take_hot.astype(F32),
        st_buf[...].reshape(R, B),
        preferred_element_type=F32,
        precision=lax.Precision.HIGHEST,
    )
    row_mean = stats[:, 0:1] / D
    variance = stats[:, 1:2] / D - row_mean * row_mean
    inv_std = lax.rsqrt(variance + epsilon)
    centered = (features - row_mean) * inv_std
    row_wait(g_src, g_all, 3)
    row_wait(x_src, x_buf, 0)
    for k in range(Z):
        block = x_buf[k].astype(F32)
        block_gain = g_all[k].astype(F32)[0:8]
        gains[k] = block_gain
        normed = ((block - row_mean) * inv_std) * block_gain[0:1]
        cgain[k] = normed
        nrm[:, k * B : (k + 1) * B] = normed.astype(BF)
    w2_forward(0, 0, 4)
    w2_forward(0, 1, 4)
    w2_forward(1, 0, 1)
    w2_forward(1, 1, 1)
    w2_ready(0)
    for xx in range(X):
        pq[xx] = dot(nrm[...], Wq[xx]).astype(BF)
    rx_start(pq, pq_buf, 0)
    w2_forward(1, 0, 2)
    w2_forward(1, 1, 2)
    qkv = rx_sum(pq, pq_buf, 0).astype(BF)
    queries, keys, values = qkv[:, :B], qkv[:, B : 2 * B], qkv[:, 2 * B :]
    raw = dot_nt(queries, keys) / math.sqrt(B)
    capped = soft_limit * jnp.tanh(raw / soft_limit)
    exps = jnp.where(same_segment, jnp.exp(capped), 0.0)
    probabilities = exps / jnp.sum(exps, axis=-1, keepdims=True)
    prob_rounded = probabilities.astype(BF)
    h_src[...] = dot(prob_rounded, values).astype(BF)
    row_start(h_src, h_buf, 1)
    for h in (3, 4):
        w2_forward(1, 0, h)
        w2_forward(1, 1, h)
    row_wait(h_src, h_buf, 1)
    w2_ready(1)

    heads_row = jnp.concatenate([h_buf[k] for k in range(Z)], axis=1)
    for xx in range(X):
        po[xx] = dot(heads_row, Wod[xx, :, 0:B]).astype(po.dtype)
    rx_start(po, po_buf, 1)
    hidden = features + rx_sum(po, po_buf, 1)
    d_src[...] = hidden.astype(BF)
    row_start(d_src, d_buf, 2)
    row_wait(d_src, d_buf, 2)

    dense_row = jnp.concatenate([d_buf[k] for k in range(Z)], axis=1)
    for xx in range(X):
        pd[xx] = dot(dense_row, Wod[xx, :, B : 2 * B]).astype(pd.dtype)
    rx_start(pd, pd_buf, 2)
    dense_linear = rx_sum(pd, pd_buf, 2)
    dl_buf[x] = dense_linear
    activated = dense_linear * (0.5 * (1.0 + lax.erf(dense_linear * inv_root_two)))
    ar_start(
        columns_to_rows(
            [
                jnp.sum(activated, axis=1, keepdims=True),
                jnp.sum(activated * activated, axis=1, keepdims=True),
                jnp.sum(activated * head_vector, axis=1, keepdims=True),
                jnp.broadcast_to(jnp.sum(head_vector, axis=1, keepdims=True), (B, 1)),
            ]
        ),
        1,
    )
    ax_start(dl_buf, 0)
    ax_wait(hw_buf, 3)
    ax_wait(dl_buf, 0)
    gelus = []
    for xx in range(X):
        linear = dl_buf[xx]
        phi = 0.5 * (1.0 + lax.erf(linear * inv_root_two))
        slope = phi + linear * jnp.exp(-0.5 * linear * linear) * inv_root_tau
        gelus.append((linear * phi, slope, hw_buf[xx].astype(F32)[0:1]))
    stats = ar_sum(1)
    head_mean = stats[:, 0:1] / D
    head_scale = lax.rsqrt(stats[:, 1:2] / D - head_mean * head_mean + epsilon)
    weight_sum = stats[:, 3:4]
    logits = head_scale * (stats[:, 2:3] - head_mean * weight_sum)
    logit_grads = loss_scale * (jax.nn.sigmoid(logits) - labels)
    mean_grads = logit_grads * weight_sum / D
    mean_product = logit_grads * logits / D
    for xx, (active, slope, vector) in enumerate(gelus):
        head_centered = (active - head_mean) * head_scale
        activated_grads = head_scale * (
            logit_grads * vector - mean_grads - head_centered * mean_product
        )
        pre[xx] = (activated_grads * slope).astype(BF)
    spread_back(lambda xx: pre[xx], lambda xx, rows: Wod[xx, rows, B : 2 * B], b1, b1_buf, 0)
    hidden_grads = own_sum(b1_buf, 0)
    hr_buf[x] = hidden_grads.astype(BF)
    ax_start(hr_buf, 1)
    ax_wait(hr_buf, 1)
    spread_back(lambda xx: hr_buf[xx], lambda xx, rows: Wod[xx, rows, 0:B], b2, b2_buf, 1)
    out_rounded = own_sum(b2_buf, 1).astype(BF)

    prob_grads = dot_nt(out_rounded, values)
    value_grads = dot_tn(prob_rounded, out_rounded)
    capped_grads = probabilities * (
        prob_grads - jnp.sum(probabilities * prob_grads, axis=-1, keepdims=True)
    )
    ratio = capped / soft_limit
    score_rounded = (capped_grads * (1.0 - ratio * ratio) / math.sqrt(B)).astype(BF)
    query_grads = dot(score_rounded, keys)
    key_grads = dot_tn(score_rounded, queries)
    g_buf[x] = jnp.concatenate([query_grads, key_grads, value_grads], axis=1).astype(BF)
    ax_start(g_buf, 2)
    ax_wait(g_buf, 2)
    def send_sums():
        plain, weighted = jnp.zeros((B, B), F32), jnp.zeros((B, B), F32)
        for k in range(Z):
            block = b3[k].astype(F32)
            plain = plain + block * gains[k, 0:1]
            weighted = weighted + block * cgain[k]
        columns = [jnp.sum(total, axis=1, keepdims=True) for total in (plain, weighted)]
        ar_start(columns_to_rows(columns), 2)

    old = list(pending)
    pending.clear()

    def finish_old():
        for done in old:
            done()

    spread_back(lambda xx: g_buf[xx], lambda xx, rows: Wq[xx, rows, :], b3, b3_buf, 2, send_sums)
    finish_old()
    scaled = own_sum(b3_buf, 2) * gain
    stats = ar_sum(2)
    input_grads = hidden_grads + inv_std * (
        scaled - stats[:, 0:1] / D - centered * (stats[:, 1:2] / D)
    )

    gslot_src[...] = dot(put_hot, input_grads.astype(BF)).astype(BF).reshape(T, cap, B)
    tok_start(gslot_src, gslot_buf, 2)
    tok_wait(gslot_src, gslot_buf, 2)
    grad_out[...] = gslot_buf[...].reshape(R, B)

    finish()


def table_kernel(tile, grad_ref, req_ref, out_ref):
    wanted = req_ref[0:1, :]
    group = jnp.floor(wanted * (1.0 / B))
    within = jnp.where(iota((B, wanted.shape[1]), 0).astype(F32) == wanted - group * B, 1.0, 0.0)
    within = within.astype(BF)
    grads = grad_ref[...]
    first = pl.program_id(0) * (tile // B)
    for g in range(tile // B):
        here = jnp.where(group == (first + g).astype(F32), 1.0, 0.0).astype(BF)
        out_ref[g * B : (g + 1) * B, :] = dot(within * here, grads).astype(BF)


def local(
    X, Z, Y, C,
    embeddings, norm_gain, query_key_value_weight, out_weight, dense_weight, head_weight,
    token_ids, replace_ids, masked, labels, segments,
):
    vocab_rows = embeddings.shape[0]
    V, T = X * Z, Y * C
    cap = 2 * B // T
    R = T * cap
    vm = pl.BlockSpec(memory_space=pltpu.VMEM)
    dma = pltpu.SemaphoreType.DMA
    rows = query_key_value_weight.shape[0]
    VM = pltpu.VMEM
    right = Y // 2
    grads, requests = pl.pallas_call(
        functools.partial(main_kernel, X, Z, Y, C, vocab_rows),
        out_shape=(
            jax.ShapeDtypeStruct((R, B), BF),
            jax.ShapeDtypeStruct((8, R), F32),
        ),
        in_specs=[pl.BlockSpec(memory_space=pltpu.HBM)] * 11,
        out_specs=(vm, vm),
        scratch_shapes=[
            VM((vocab_rows, B), BF),
            VM((rows, 3 * B), BF),
            VM((rows, 2 * B), BF),
            VM((X, Z * B, 3 * B), BF),
            VM((X, Z * B, 2 * B), BF),
            VM((1, B), jnp.int32), VM((1, B), jnp.int32), VM((1, B), jnp.int32),
            VM((1, B), BF), VM((1, B), BF),
            VM((1, B), jnp.int32), VM((1, B), jnp.int32),
            VM((T, cap, B), F32), VM((T, cap, B), F32),
            VM((T, cap, B), BF), VM((T, cap, B), BF),
            VM((T, cap, B), F32), VM((T, cap, B), F32),
            VM((T, cap, B), BF), VM((T, cap, B), BF),
            VM((16, B), BF), VM((Z, 16, B), BF),
            VM((B, B), BF), VM((Z, B, B), BF),
            VM((B, B), BF), VM((Z, B, B), BF),
            VM((B, B), BF), VM((Z, B, B), BF),
            VM((X, B, 3 * B), BF), VM((X - 1, B, 3 * B), BF),
            VM((X, B, B), BF), VM((X - 1, B, B), BF),
            VM((X, B, B), BF), VM((X - 1, B, B), BF),
            VM((Z, B, B), BF), VM((Z, B, B), BF),
            VM((X, B, B), BF), VM((Z, B, B), BF), VM((Z, B, B), BF),
            VM((X, B, 3 * B), BF), VM((Z, B, B), BF), VM((Z, B, B), BF),
            VM((B, Z * B), BF), VM((Z, B, B), F32), VM((Z, 8, B), F32),
            VM((X, B, B), F32), VM((X, B, B), BF), VM((X, 16, B), BF),
            VM((3, 8, B), F32), VM((3, V, 8, B), F32),
            dma((11,)), dma((3,)), dma(()), dma((X // C, 4)),
            dma((2, X // C, 2, right)), dma((2, X // C)),
            dma((2, X // C)), dma((2, X // C)),
            dma((4,)), dma((4,)), dma((4,)), dma((4,)),
            dma((3,)), dma((3,)), dma((4,)), dma((4,)),
            dma((3,)), dma((3,)), dma((3,)), dma((3,)),
        ],
        compiler_params=pltpu.CompilerParams(
            collective_id=0, has_side_effects=True, vmem_limit_bytes=60 * 1024 * 1024
        ),
    )(
        embeddings,
        norm_gain.reshape(1, B),
        query_key_value_weight.reshape(rows, 3 * B),
        out_weight,
        dense_weight,
        head_weight.reshape(1, B),
        token_ids, replace_ids, masked, labels, segments,
    )
    tile = min(4096, vocab_rows)
    return pl.pallas_call(
        functools.partial(table_kernel, tile),
        grid=(vocab_rows // tile,),
        out_shape=jax.ShapeDtypeStruct((vocab_rows, B), BF),
        in_specs=[
            pl.BlockSpec((R, B), lambda i: (0, 0)),
            pl.BlockSpec((8, R), lambda i: (0, 0)),
        ],
        out_specs=pl.BlockSpec((tile, B), lambda i: (i, 0)),
        compiler_params=pltpu.CompilerParams(vmem_limit_bytes=60 * 1024 * 1024),
    )(grads, requests)


def solution(mesh):
    V, T = mesh.shape["vocab"], mesh.shape["tok"]
    X = 4 if V == 32 else 2
    C = 2
    placed = (
        P("tok", "vocab"),
        P("vocab"),
        P("tok", "vocab", None),
        P("tok", "vocab"),
        P("tok", "vocab"),
        P("vocab"),
        P("tok", None),
        P("tok", None),
        P("tok", None),
        P("tok", None),
        P("tok", None),
    )
    return jax.shard_map(
        functools.partial(local, X, V // X, T // C, C),
        mesh=mesh, in_specs=placed, out_specs=P("tok", "vocab"), check_vma=False,
    )
```

```python
import functools
import math

import jax
import jax.numpy as jnp
from jax import lax
from jax.experimental import pallas as pl
from jax.experimental.pallas import tpu as pltpu
from jax.sharding import PartitionSpec as P

MESH = pl.DeviceIdType.MESH
BF = jnp.bfloat16
F32 = jnp.float32
B = 128

soft_limit = 50.0
loss_scale = 64.0
epsilon = 1e-05
inv_root_two = 0.7071067811865476
inv_root_tau = 0.3989422804014327


def dot(a, b):
    return jnp.dot(a, b, preferred_element_type=F32)


def dot_nt(a, b):
    return lax.dot_general(a, b, (((1,), (1,)), ((), ())), preferred_element_type=F32)


def dot_tn(a, b):
    return lax.dot_general(a, b, (((0,), (0,)), ((), ())), preferred_element_type=F32)


def iota(shape, dim):
    return lax.broadcasted_iota(jnp.int32, shape, dim)


def columns_to_rows(columns):
    lane = iota((B, B), 1)
    total = jnp.zeros((B, B), F32)
    for i, column in enumerate(columns):
        total = jnp.where(lane == i, column, total)
    return total.T[:8]


def rows_to_square(rows):
    return jnp.concatenate([rows, jnp.zeros((B - 8, B), F32)], axis=0).T


def row_to_square(row):
    return jnp.broadcast_to(row, (B, B)).T


def main_kernel(
    X, Z, Y, C, vocab_rows,
    emb_hbm, gain_hbm, wq_hbm, wo_hbm, wd_hbm, hw_hbm,
    tok_hbm, rep_hbm, mask_hbm, lab_hbm, seg_hbm,
    grad_out, req_out,
    emb, wq_ref, wod_src, Wq, Wod,
    tok_ref, rep_ref, mask_ref, gain_ref, hw_ref, lab_ref, seg_ref,
    ids_src, ids_buf, row_src, row_buf, st_src, st_buf, gslot_src, gslot_buf,
    g_src, g_all, x_src, x_buf, h_src, h_buf, d_src, d_buf,
    pq, pq_buf, po, po_buf, pd, pd_buf,
    b1, b1_buf, hr_buf, b2, b2_buf, g_buf, b3, b3_buf,
    nrm, cgain, gains, dl_buf, pre, hw_buf, ar_src, ar_buf,
    in_sem, w1q_sem, w1o_sem, w1_send, w2_recv, w2_send, sib_recv, sib_send,
    t_recv, t_send, e_recv, e_send, rx_recv, rx_send, ax_recv, ax_send,
    r_recv, r_send, s_recv, s_send,
):
    V, T = X * Z, Y * C
    Xc = X // C
    D = V * B
    K = Z * B
    v, t = lax.axis_index("vocab"), lax.axis_index("tok")
    x, z = v // Z, v % Z
    y, c = t // C, t % C
    cap = 2 * B // T
    R = T * cap

    def dev(xx, zz, yy, cc):
        return (xx * Z + zz, yy * C + cc)

    def far_first(i, size):
        return size // 2 + ((i + 1) // 2) * (1 - 2 * (i % 2))

    def remote(src, dst, send, recv, device):
        return pltpu.make_async_remote_copy(
            src_ref=src, dst_ref=dst, send_sem=send, recv_sem=recv,
            device_id=device, device_id_type=MESH,
        )

    pending = []

    def finish():
        for done in pending:
            done()
        pending.clear()

    def wait_bytes(ref, sem):
        pltpu.make_async_copy(ref, ref, sem).wait()

    def step_of(way):
        return 1 if way == 0 else Y - 1

    half_up, half_down = Y // 2, Y - 1 - Y // 2

    def hops_of(i, way):
        return half_up if way == i % 2 else half_down

    wanted_here = (
        (tok_hbm, tok_ref), (rep_hbm, rep_ref), (mask_hbm, mask_ref),
        (wq_hbm, wq_ref), (wo_hbm, wod_src.at[:, pl.ds(0, B)]),
        (wd_hbm, wod_src.at[:, pl.ds(B, B)]), (emb_hbm, emb),
        (gain_hbm, gain_ref), (hw_hbm, hw_ref), (lab_hbm, lab_ref), (seg_hbm, seg_ref),
    )
    copies = [
        pltpu.make_async_copy(src, dst, in_sem.at[i]) for i, (src, dst) in enumerate(wanted_here)
    ]
    for copy in copies:
        copy.start()
    barrier = pltpu.get_barrier_semaphore()

    def greet_vocab(d, carry):
        pl.semaphore_signal(barrier, inc=1, device_id=((v + d) % V, t), device_id_type=MESH)
        return carry

    def greet_tok(d, carry):
        pl.semaphore_signal(barrier, inc=1, device_id=(v, (t + d) % T), device_id_type=MESH)
        return carry

    lax.fori_loop(1, V, greet_vocab, 0)
    lax.fori_loop(1, T, greet_tok, 0)
    turn = y // (Z // X)
    same_core = (x // Xc) == c
    from_core = ((x + turn) % X) // Xc
    other_source = from_core != c

    @pl.when(jnp.logical_not(same_core))
    def _():
        for i in range(Xc):
            to = dev((Xc * c + i + X - turn) % X, z, y, x // Xc)
            pl.semaphore_signal(barrier, inc=1, device_id=to, device_id_type=MESH)

    @pl.when(other_source)
    def _():
        for i in range(Xc):
            to = dev(Xc * c + i, z, y, from_core)
            pl.semaphore_signal(barrier, inc=1, device_id=to, device_id_type=MESH)

    ways = [way for way in (0, 1) if hops_of(0, way) >= 1]
    for way in ways:
        ahead, behind = (y + step_of(way)) % Y, (y + Y - step_of(way)) % Y
        sender = ((x + behind // (Z // X)) % X) // Xc
        for i in range(Xc):
            for to in (
                dev((Xc * c + i + X - turn) % X, z, ahead, x // Xc),
                dev(Xc * c + i, z, behind, sender),
            ):
                pl.semaphore_signal(barrier, inc=1, device_id=to, device_id_type=MESH)

    for copy in copies[:3]:
        copy.wait()
    chosen = jnp.where(mask_ref[...] == 1, rep_ref[...], tok_ref[...])
    owner = chosen // vocab_rows
    offset = (chosen - owner * vocab_rows).astype(F32)
    owner_f = owner.astype(F32)
    earlier = iota((B, B), 0) < iota((B, B), 1)
    same_owner = row_to_square(owner_f) == owner_f
    slot = jnp.sum(jnp.where(same_owner & earlier, 1.0, 0.0), axis=0, keepdims=True)
    place = owner_f * float(cap) + slot
    place_hot = iota((R, B), 0).astype(F32) == place
    wanted = jnp.sum(jnp.where(place_hot, offset, 0.0), axis=1, keepdims=True)
    ids_src[...] = jnp.broadcast_to(wanted, (R, B)).reshape(T, cap, B)

    pl.semaphore_wait(
        barrier,
        V - 1 + T - 1 + 2 * Xc * len(ways)
        + Xc * jnp.where(same_core, 0, 1)
        + Xc * jnp.where(other_source, 1, 0),
    )

    def tok_start(src, buf, n):
        buf[t] = src[t]

        def send(i, carry):
            cd = (c + C - 1 - i % C) % C
            to = (y + far_first(i // C, Y)) % Y * C + cd
            remote(src.at[to], buf.at[t], t_send.at[n], t_recv.at[n], (v, to)).start()
            return carry

        lax.fori_loop(0, T - 1, send, 0)
        pending.append(lambda: wait_bytes(src.at[pl.ds(0, T - 1)], t_send.at[n]))

    def tok_wait(src, buf, n):
        wait_bytes(buf.at[pl.ds(0, T - 1)], t_recv.at[n])

    tok_start(ids_src, ids_buf, 0)

    def w1_each(act):
        first, cd = pl.multiple_of(y * B, B), x // Xc
        for a, (src, dst) in enumerate(((wq_ref, Wq), (wod_src, Wod))):
            for i in range(Xc):
                xd = (Xc * c + i + X - turn) % X
                mine = (xd == x) & same_core
                piece, place_ = src.at[pl.ds(i * B, B)], dst.at[x, pl.ds(first, B)]
                for way in ways if a == 0 else ():
                    to = dev(xd, z, (y + step_of(way)) % Y, cd)
                    act(None, piece, place_, w1q_sem.at[1 + way], w1_send.at[i, 2 + way], to)
                sem = w1q_sem.at[0] if a == 0 else w1o_sem
                act(mine, piece, place_, sem, w1_send.at[i, a], dev(xd, z, y, cd))

    def w1_go(mine, src, dst, sem, send, device):
        if mine is None:
            remote(src, dst, send, sem, device).start()
            return

        @pl.when(mine)
        def _():
            pltpu.make_async_copy(src, dst, sem).start()

        @pl.when(jnp.logical_not(mine))
        def _():
            remote(src, dst, send, sem, device).start()

    def w1_end(mine, src, dst, sem, send, device):
        if mine is None:
            wait_bytes(src, send)
            return

        @pl.when(jnp.logical_not(mine))
        def _():
            wait_bytes(src, send)

    for copy in copies[3:6]:
        copy.wait()
    w1_each(w1_go)
    pending.append(lambda: w1_each(w1_end))
    pending.append(lambda: w2_done())

    arrays = (Wq, Wod)
    def block_of(a, i, k):
        return arrays[a].at[Xc * c + i, pl.ds(pl.multiple_of(k * B, B), B)]

    def hop(a, i, h, way):
        step = 1 if way == 0 else Y - 1
        ref = block_of(a, i, (y + (Y - step) * (h - 1)) % Y)
        return remote(
            ref, ref, w2_send.at[a, i], w2_recv.at[a, i, way, h - 1],
            dev(x, z, (y + step) % Y, c),
        )

    def sibling(a, i, k):
        ref = block_of(a, i, k)
        return remote(
            ref, ref, sib_send.at[a, i], sib_recv.at[a, i], dev(x, z, y, (c + 1) % C)
        )

    def w2_first():
        whole = Wq.at[pl.ds(0, Xc), pl.ds(0, B)]
        for way in ways:
            wait_bytes(whole, w1q_sem.at[1 + way])
            for i in range(Xc):
                if hops_of(i, way) >= 2:
                    hop(0, i, 2, way).start()
        wait_bytes(whole, w1q_sem.at[0])
        for i in range(Xc):
            sibling(0, i, y).start()
            for way in ways:
                sibling(0, i, (y + Y - step_of(way)) % Y).start()

    def w2_begin(a):
        wait_bytes(Wod.at[pl.ds(0, Xc), pl.ds(0, B)], w1o_sem)
        for i in range(Xc):
            for way in (0, 1):
                if hops_of(i, way) >= 1:
                    hop(a, i, 1, way).start()
        for i in range(Xc):
            sibling(a, i, y).start()

    def w2_forward(a, i, h):
        if i >= Xc:
            return
        for way in (0, 1):
            if h <= hops_of(i, way):
                hop(a, i, h, way).wait_recv()
                if h + 1 <= hops_of(i, way):
                    hop(a, i, h + 1, way).start()
        for way in (0, 1):
            if h <= hops_of(i, way):
                step = 1 if way == 0 else Y - 1
                sibling(a, i, (y + (Y - step) * h) % Y).start()

    def w2_ready(a):
        for i in range(Xc):
            wait_bytes(arrays[a].at[0], sib_recv.at[a, i])

    def w2_done():
        for a in (0, 1):
            for i in range(Xc):
                sent = Y - 1 - (len(ways) if a == 0 else 0)
                if sent:
                    wait_bytes(arrays[a].at[0, pl.ds(0, sent * B)], w2_send.at[a, i])
                wait_bytes(arrays[a].at[0], sib_send.at[a, i])

    row = (z + X - x) % X
    at_home = x == row

    whole_rows, H = pl.ds(0, B), B // 2
    halves = [(0, pl.ds(0, H)), (1, pl.ds(H, H))]

    def block_done(ref, sem, rows):
        @pl.when(at_home)
        def _():
            wait_bytes(ref.at[pl.ds(0, Z - 1), rows], sem)

        @pl.when(jnp.logical_not(at_home))
        def _():
            wait_bytes(ref.at[pl.ds(0, Z), rows], sem)

    def row_start(src, buf, n, rows=whole_rows):
        k = v // X
        for j in range(Z):
            zd = (z + far_first(j, Z)) % Z
            mine = at_home & (zd == z)

            @pl.when(mine)
            def _():
                pltpu.make_async_copy(src.at[rows], buf.at[k, rows], e_recv.at[n]).start()

            @pl.when(jnp.logical_not(mine))
            def _():
                to = dev(row, zd, y, c)
                remote(src.at[rows], buf.at[k, rows], e_send.at[n], e_recv.at[n], to).start()

        pending.append(lambda: block_done(buf, e_send.at[n], rows))

    def row_wait(buf, n, rows=whole_rows):
        wait_bytes(buf.at[pl.ds(0, Z), rows], e_recv.at[n])

    def rx_start(part, buf, n, rows=whole_rows):
        for d in [far_first(i, X) for i in range(X - 1)]:
            to = (x + d) % X
            remote(
                part.at[to, rows], buf.at[d - 1, rows], rx_send.at[n], rx_recv.at[n],
                dev(to, z, y, c),
            ).start()
        pending.append(lambda: wait_bytes(buf.at[pl.ds(0, X - 1), rows], rx_send.at[n]))

    def rx_sum(part, buf, n, rows=whole_rows):
        wait_bytes(buf.at[pl.ds(0, X - 1), rows], rx_recv.at[n])
        total = part[x, rows].astype(F32)
        for d in range(1, X):
            total = total + buf[d - 1, rows].astype(F32)
        return total

    def ax_start(buf, n, rows=whole_rows):
        for d in [far_first(i, X) for i in range(X - 1)]:
            remote(
                buf.at[x, rows], buf.at[x, rows], ax_send.at[n], ax_recv.at[n],
                dev((x + d) % X, z, y, c),
            ).start()
        pending.append(lambda: wait_bytes(buf.at[pl.ds(0, X - 1), rows], ax_send.at[n]))

    def ax_wait(buf, n, rows=whole_rows):
        wait_bytes(buf.at[pl.ds(0, X - 1), rows], ax_recv.at[n])

    def own_start(part, buf, n, rows):
        for j in range(Z):
            zd = (z + far_first(j, Z)) % Z
            xd = (zd % X + X - x) % X
            k = xd * (Z // X) + zd // X
            mine = (xd == x) & (zd == z)

            @pl.when(mine)
            def _():
                pltpu.make_async_copy(part.at[k, rows], buf.at[z, rows], r_recv.at[n]).start()

            @pl.when(jnp.logical_not(mine))
            def _():
                to = dev(xd, zd, y, c)
                remote(
                    part.at[k, rows], buf.at[z, rows], r_send.at[n], r_recv.at[n], to
                ).start()

        pending.append(lambda: block_done(part, r_send.at[n], rows))

    def own_sum(buf, n, rows=whole_rows):
        wait_bytes(buf.at[pl.ds(0, Z), rows], r_recv.at[n])
        total = buf[0, rows].astype(F32)
        for k in range(1, Z):
            total = total + buf[k, rows].astype(F32)
        return total

    def spread_back(left, weights, part, buf, n, rows=whole_rows, seen=None):
        step = 2
        for first in range(0, Z, step):
            total = None
            for xx in range(X):
                term = dot_nt(left(xx), weights(xx, pl.ds(first * B, step * B)))
                total = term if total is None else total + term
            for k in range(first, first + step):
                part[k, rows] = total[:, (k - first) * B : (k - first + 1) * B].astype(BF)
        if seen is not None:
            seen()
        own_start(part, buf, n, rows)

    def ar_start(rows, n):
        ar_src[n] = rows
        ar_buf[n, 0] = rows

        def send(i, carry):
            to = dev((x + far_first(i % X, X)) % X, (z + far_first(i // X, Z)) % Z, y, c)
            remote(ar_src.at[n], ar_buf.at[n, i + 1], s_send.at[n], s_recv.at[n], to).start()
            return carry

        lax.fori_loop(0, V - 1, send, 0)
        pending.append(lambda: wait_bytes(ar_buf.at[n, pl.ds(1, V - 1)], s_send.at[n]))

    def ar_sum(n):
        wait_bytes(ar_buf.at[n, pl.ds(1, V - 1)], s_recv.at[n])
        return rows_to_square(jnp.sum(ar_buf[n], axis=0))

    for copy in copies[6:]:
        copy.wait()
    hw_buf[x] = jnp.broadcast_to(hw_ref[...].astype(F32), (16, B)).astype(BF)
    ax_start(hw_buf, 3, pl.ds(0, 16))
    put_hot = jnp.where(place_hot, 1.0, 0.0).astype(BF)
    place_square = row_to_square(place)
    take_hot = jnp.concatenate(
        [
            jnp.where(place_square == (iota((B, B), 1) + first).astype(F32), 1.0, 0.0)
            for first in range(0, R, B)
        ],
        axis=1,
    ).astype(BF)
    segment_f = seg_ref[...].astype(F32)
    same_segment = row_to_square(segment_f) == segment_f
    labels = row_to_square(lab_ref[...].astype(F32))[:, 0:1]
    gain = gain_ref[...].astype(F32)
    head_vector = hw_ref[...].astype(F32)
    g_src[...] = jnp.broadcast_to(gain, (16, B)).astype(BF)
    row_start(g_src, g_all, 3, pl.ds(0, 16))
    tok_wait(ids_src, ids_buf, 0)
    requested = ids_buf[...].reshape(R, B)
    chunk = 512


    def fetch(i, total):
        base = i * chunk
        hot = jnp.concatenate(
            [
                jnp.where(
                    requested == (iota((R, B), 1) + (base + first)).astype(F32), 1.0, 0.0
                ).astype(BF)
                for first in range(0, chunk, B)
            ],
            axis=1,
        )
        return total + dot(hot, emb[pl.ds(pl.multiple_of(base, chunk), chunk), :])

    fetched = lax.fori_loop(0, vocab_rows // chunk, fetch, jnp.zeros((R, B), F32))
    row_src[...] = fetched.astype(BF).reshape(T, cap, B)
    tok_start(row_src, row_buf, 1)
    row_sums = []
    for first in range(0, R, B):
        piece = fetched[first : first + B]
        row_sums.append(jnp.sum(piece, axis=1, keepdims=True))
        row_sums.append(jnp.sum(piece * piece, axis=1, keepdims=True))
    ar_start(columns_to_rows(row_sums), 0)
    w2_first()
    tok_wait(row_src, row_buf, 1)
    features = dot(take_hot, row_buf[...].reshape(R, B))
    x_src[...] = features.astype(BF)
    row_start(x_src, x_buf, 0)
    w2_forward(0, 0, 2)
    w2_forward(0, 1, 2)
    stats = ar_sum(0)
    lane = iota((B, B), 1)
    for first in range(0, R, B):
        i = 2 * (first // B)
        pair = jnp.where(lane == 0, stats[:, i : i + 1], stats[:, i + 1 : i + 2])
        st_src[first // cap : (first + B) // cap] = pair.reshape(B // cap, cap, B)
    tok_start(st_src, st_buf, 3)
    for first in range(0, R, B):
        req_out[:, first : first + B] = requested[first : first + B].T[:8]
    w2_forward(0, 0, 3)
    w2_forward(0, 1, 3)
    w2_begin(1)
    tok_wait(st_src, st_buf, 3)
    stats = jnp.dot(
        take_hot.astype(F32),
        st_buf[...].reshape(R, B),
        preferred_element_type=F32,
        precision=lax.Precision.HIGHEST,
    )
    row_mean = stats[:, 0:1] / D
    variance = stats[:, 1:2] / D - row_mean * row_mean
    inv_std = lax.rsqrt(variance + epsilon)
    centered = (features - row_mean) * inv_std
    row_wait(g_all, 3, pl.ds(0, 16))
    row_wait(x_buf, 0)
    for k in range(Z):
        block = x_buf[k].astype(F32)
        block_gain = g_all[k].astype(F32)[0:8]
        gains[k] = block_gain
        normed = ((block - row_mean) * inv_std) * block_gain[0:1]
        cgain[k] = normed
        nrm[:, k * B : (k + 1) * B] = normed.astype(BF)
    w2_forward(0, 0, 4)
    w2_forward(0, 1, 4)
    w2_forward(1, 0, 1)
    w2_forward(1, 1, 1)
    w2_ready(0)
    for xx in range(X):
        pq[xx] = dot(nrm[...], Wq[xx]).astype(BF)
    rx_start(pq, pq_buf, 0)
    w2_forward(1, 0, 2)
    w2_forward(1, 1, 2)
    qkv = rx_sum(pq, pq_buf, 0).astype(BF)
    queries, keys, values = qkv[:, :B], qkv[:, B : 2 * B], qkv[:, 2 * B :]
    raw = dot_nt(queries, keys) / math.sqrt(B)
    capped = soft_limit * jnp.tanh(raw / soft_limit)
    exps = jnp.where(same_segment, jnp.exp(capped), 0.0)
    probabilities = exps / jnp.sum(exps, axis=-1, keepdims=True)
    prob_rounded = probabilities.astype(BF)
    h_src[...] = dot(prob_rounded, values).astype(BF)
    for n, rows in halves:
        row_start(h_src, h_buf, 1 + 3 * n, rows)
    for h in (3, 4):
        w2_forward(1, 0, h)
        w2_forward(1, 1, h)
    w2_ready(1)

    for n, rows in halves:
        row_wait(h_buf, 1 + 3 * n, rows)
        heads_row = jnp.concatenate([h_buf[k, rows] for k in range(Z)], axis=1)
        for xx in range(X):
            po[xx, rows] = dot(heads_row, Wod[xx, :, 0:B]).astype(po.dtype)
        rx_start(po, po_buf, 1 + 2 * n, rows)
    for n, rows in halves:
        hidden = features[n * H : (n + 1) * H] + rx_sum(po, po_buf, 1 + 2 * n, rows)
        d_src[rows] = hidden.astype(BF)
        row_start(d_src, d_buf, 2 + 3 * n, rows)

    for n, rows in halves:
        row_wait(d_buf, 2 + 3 * n, rows)
        dense_row = jnp.concatenate([d_buf[k, rows] for k in range(Z)], axis=1)
        for xx in range(X):
            pd[xx, rows] = dot(dense_row, Wod[xx, :, B : 2 * B]).astype(pd.dtype)
        rx_start(pd, pd_buf, 2 + 2 * n, rows)
    dense_linear = jnp.concatenate(
        [rx_sum(pd, pd_buf, 2 + 2 * n, rows) for n, rows in halves], axis=0
    )
    dl_buf[x] = dense_linear
    activated = dense_linear * (0.5 * (1.0 + lax.erf(dense_linear * inv_root_two)))
    ar_start(
        columns_to_rows(
            [
                jnp.sum(activated, axis=1, keepdims=True),
                jnp.sum(activated * activated, axis=1, keepdims=True),
                jnp.sum(activated * head_vector, axis=1, keepdims=True),
                jnp.broadcast_to(jnp.sum(head_vector, axis=1, keepdims=True), (B, 1)),
            ]
        ),
        1,
    )
    ax_start(dl_buf, 0)
    ax_wait(hw_buf, 3, pl.ds(0, 16))
    ax_wait(dl_buf, 0)
    gelus = []
    for xx in range(X):
        linear = dl_buf[xx]
        phi = 0.5 * (1.0 + lax.erf(linear * inv_root_two))
        slope = phi + linear * jnp.exp(-0.5 * linear * linear) * inv_root_tau
        gelus.append((linear * phi, slope, hw_buf[xx].astype(F32)[0:1]))
    stats = ar_sum(1)
    head_mean = stats[:, 0:1] / D
    head_scale = lax.rsqrt(stats[:, 1:2] / D - head_mean * head_mean + epsilon)
    weight_sum = stats[:, 3:4]
    logits = head_scale * (stats[:, 2:3] - head_mean * weight_sum)
    logit_grads = loss_scale * (jax.nn.sigmoid(logits) - labels)
    mean_grads = logit_grads * weight_sum / D
    mean_product = logit_grads * logits / D
    for xx, (active, slope, vector) in enumerate(gelus):
        head_centered = (active - head_mean) * head_scale
        activated_grads = head_scale * (
            logit_grads * vector - mean_grads - head_centered * mean_product
        )
        pre[xx] = (activated_grads * slope).astype(BF)
    for n, rows in halves:
        spread_back(
            lambda xx: pre[xx, rows],
            lambda xx, part: Wod[xx, part, B : 2 * B],
            b1, b1_buf, 3 * n, rows,
        )
    pieces = []
    for n, rows in halves:
        pieces.append(own_sum(b1_buf, 3 * n, rows))
        hr_buf[x, rows] = pieces[n].astype(BF)
        ax_start(hr_buf, 1 + 3 * n, rows)
    for n, rows in halves:
        ax_wait(hr_buf, 1 + 3 * n, rows)
        spread_back(
            lambda xx: hr_buf[xx, rows],
            lambda xx, part: Wod[xx, part, 0:B],
            b2, b2_buf, 1 + 3 * n, rows,
        )
    hidden_grads = jnp.concatenate(pieces, axis=0)
    out_rounded = jnp.concatenate(
        [own_sum(b2_buf, 1 + 3 * n, rows) for n, rows in halves], axis=0
    ).astype(BF)

    prob_grads = dot_nt(out_rounded, values)
    value_grads = dot_tn(prob_rounded, out_rounded)
    capped_grads = probabilities * (
        prob_grads - jnp.sum(probabilities * prob_grads, axis=-1, keepdims=True)
    )
    ratio = capped / soft_limit
    score_rounded = (capped_grads * (1.0 - ratio * ratio) / math.sqrt(B)).astype(BF)
    query_grads = dot(score_rounded, keys)
    key_grads = dot_tn(score_rounded, queries)
    g_buf[x] = jnp.concatenate([query_grads, key_grads, value_grads], axis=1).astype(BF)
    ax_start(g_buf, 2)
    ax_wait(g_buf, 2)
    def send_sums():
        plain, weighted = jnp.zeros((B, B), F32), jnp.zeros((B, B), F32)
        for k in range(Z):
            block = b3[k].astype(F32)
            plain = plain + block * gains[k, 0:1]
            weighted = weighted + block * cgain[k]
        columns = [jnp.sum(total, axis=1, keepdims=True) for total in (plain, weighted)]
        ar_start(columns_to_rows(columns), 2)

    old = list(pending)
    pending.clear()

    def finish_old():
        for done in old:
            done()

    spread_back(lambda xx: g_buf[xx], lambda xx, rows: Wq[xx, rows, :], b3, b3_buf, 2, seen=send_sums)
    finish_old()
    scaled = own_sum(b3_buf, 2) * gain
    stats = ar_sum(2)
    input_grads = hidden_grads + inv_std * (
        scaled - stats[:, 0:1] / D - centered * (stats[:, 1:2] / D)
    )

    gslot_src[...] = dot(put_hot, input_grads.astype(BF)).astype(BF).reshape(T, cap, B)
    tok_start(gslot_src, gslot_buf, 2)
    tok_wait(gslot_src, gslot_buf, 2)
    grad_out[...] = gslot_buf[...].reshape(R, B)

    finish()


def table_kernel(tile, grad_ref, req_ref, out_ref):
    wanted = req_ref[0:1, :]
    group = jnp.floor(wanted * (1.0 / B))
    within = jnp.where(iota((B, wanted.shape[1]), 0).astype(F32) == wanted - group * B, 1.0, 0.0)
    within = within.astype(BF)
    grads = grad_ref[...]
    first = pl.program_id(0) * (tile // B)
    for g in range(tile // B):
        here = jnp.where(group == (first + g).astype(F32), 1.0, 0.0).astype(BF)
        out_ref[g * B : (g + 1) * B, :] = dot(within * here, grads).astype(BF)


def local(
    X, Z, Y, C,
    embeddings, norm_gain, query_key_value_weight, out_weight, dense_weight, head_weight,
    token_ids, replace_ids, masked, labels, segments,
):
    vocab_rows = embeddings.shape[0]
    V, T = X * Z, Y * C
    cap = 2 * B // T
    R = T * cap
    vm = pl.BlockSpec(memory_space=pltpu.VMEM)
    dma = pltpu.SemaphoreType.DMA
    rows = query_key_value_weight.shape[0]
    VM = pltpu.VMEM
    right = Y // 2
    grads, requests = pl.pallas_call(
        functools.partial(main_kernel, X, Z, Y, C, vocab_rows),
        out_shape=(
            jax.ShapeDtypeStruct((R, B), BF),
            jax.ShapeDtypeStruct((8, R), F32),
        ),
        in_specs=[pl.BlockSpec(memory_space=pltpu.HBM)] * 11,
        out_specs=(vm, vm),
        scratch_shapes=[
            VM((vocab_rows, B), BF),
            VM((rows, 3 * B), BF),
            VM((rows, 2 * B), BF),
            VM((X, Z * B, 3 * B), BF),
            VM((X, Z * B, 2 * B), BF),
            VM((1, B), jnp.int32), VM((1, B), jnp.int32), VM((1, B), jnp.int32),
            VM((1, B), BF), VM((1, B), BF),
            VM((1, B), jnp.int32), VM((1, B), jnp.int32),
            VM((T, cap, B), F32), VM((T, cap, B), F32),
            VM((T, cap, B), BF), VM((T, cap, B), BF),
            VM((T, cap, B), F32), VM((T, cap, B), F32),
            VM((T, cap, B), BF), VM((T, cap, B), BF),
            VM((16, B), BF), VM((Z, 16, B), BF),
            VM((B, B), BF), VM((Z, B, B), BF),
            VM((B, B), BF), VM((Z, B, B), BF),
            VM((B, B), BF), VM((Z, B, B), BF),
            VM((X, B, 3 * B), BF), VM((X - 1, B, 3 * B), BF),
            VM((X, B, B), BF), VM((X - 1, B, B), BF),
            VM((X, B, B), BF), VM((X - 1, B, B), BF),
            VM((Z, B, B), BF), VM((Z, B, B), BF),
            VM((X, B, B), BF), VM((Z, B, B), BF), VM((Z, B, B), BF),
            VM((X, B, 3 * B), BF), VM((Z, B, B), BF), VM((Z, B, B), BF),
            VM((B, Z * B), BF), VM((Z, B, B), F32), VM((Z, 8, B), F32),
            VM((X, B, B), F32), VM((X, B, B), BF), VM((X, 16, B), BF),
            VM((3, 8, B), F32), VM((3, V, 8, B), F32),
            dma((11,)), dma((3,)), dma(()), dma((X // C, 4)),
            dma((2, X // C, 2, right)), dma((2, X // C)),
            dma((2, X // C)), dma((2, X // C)),
            dma((4,)), dma((4,)), dma((6,)), dma((6,)),
            dma((5,)), dma((5,)), dma((5,)), dma((5,)),
            dma((5,)), dma((5,)), dma((3,)), dma((3,)),
        ],
        compiler_params=pltpu.CompilerParams(
            collective_id=0, has_side_effects=True, vmem_limit_bytes=60 * 1024 * 1024
        ),
    )(
        embeddings,
        norm_gain.reshape(1, B),
        query_key_value_weight.reshape(rows, 3 * B),
        out_weight,
        dense_weight,
        head_weight.reshape(1, B),
        token_ids, replace_ids, masked, labels, segments,
    )
    tile = min(4096, vocab_rows)
    return pl.pallas_call(
        functools.partial(table_kernel, tile),
        grid=(vocab_rows // tile,),
        out_shape=jax.ShapeDtypeStruct((vocab_rows, B), BF),
        in_specs=[
            pl.BlockSpec((R, B), lambda i: (0, 0)),
            pl.BlockSpec((8, R), lambda i: (0, 0)),
        ],
        out_specs=pl.BlockSpec((tile, B), lambda i: (i, 0)),
        compiler_params=pltpu.CompilerParams(vmem_limit_bytes=60 * 1024 * 1024),
    )(grads, requests)


def solution(mesh):
    V, T = mesh.shape["vocab"], mesh.shape["tok"]
    X = 4 if V == 32 else 2
    C = 2
    placed = (
        P("tok", "vocab"),
        P("vocab"),
        P("tok", "vocab", None),
        P("tok", "vocab"),
        P("tok", "vocab"),
        P("vocab"),
        P("tok", None),
        P("tok", None),
        P("tok", None),
        P("tok", None),
        P("tok", None),
    )
    return jax.shard_map(
        functools.partial(local, X, V // X, T // C, C),
        mesh=mesh, in_specs=placed, out_specs=P("tok", "vocab"), check_vma=False,
    )
```

```python
import functools
import math

import jax
import jax.numpy as jnp
from jax import lax
from jax.experimental import pallas as pl
from jax.experimental.pallas import tpu as pltpu
from jax.sharding import PartitionSpec as P

MESH = pl.DeviceIdType.MESH
BF = jnp.bfloat16
F32 = jnp.float32
B = 128

soft_limit = 50.0
loss_scale = 64.0
epsilon = 1e-05
inv_root_two = 0.7071067811865476
inv_root_tau = 0.3989422804014327


def dot(a, b):
    return jnp.dot(a, b, preferred_element_type=F32)


def dot_nt(a, b):
    return lax.dot_general(a, b, (((1,), (1,)), ((), ())), preferred_element_type=F32)


def dot_tn(a, b):
    return lax.dot_general(a, b, (((0,), (0,)), ((), ())), preferred_element_type=F32)


def iota(shape, dim):
    return lax.broadcasted_iota(jnp.int32, shape, dim)


def columns_to_rows(columns):
    lane = iota((B, B), 1)
    total = jnp.zeros((B, B), F32)
    for i, column in enumerate(columns):
        total = jnp.where(lane == i, column, total)
    return total.T[:8]


def rows_to_square(rows):
    return jnp.concatenate([rows, jnp.zeros((B - 8, B), F32)], axis=0).T


def row_to_square(row):
    return jnp.broadcast_to(row, (B, B)).T


def main_kernel(
    X, Z, Y, C, vocab_rows,
    emb_hbm, gain_hbm, wq_hbm, wo_hbm, wd_hbm, hw_hbm,
    tok_hbm, rep_hbm, mask_hbm, lab_hbm, seg_hbm,
    grad_out, req_out,
    emb, wq_ref, wod_src, Wq, Wod,
    tok_ref, rep_ref, mask_ref, gain_ref, hw_ref, lab_ref, seg_ref,
    ids_src, ids_buf, row_src, row_buf, st_src, st_buf, gslot_src, gslot_buf,
    g_src, g_all, x_src, x_buf, h_src, h_buf, d_src, d_buf,
    pq, pq_buf, po, po_buf, pd, pd_buf,
    b1, b1_buf, hr_buf, b2, b2_buf, g_buf, b3, b3_buf,
    nrm, cgain, gains, dl_buf, pre, hw_buf, ar_src, ar_buf,
    in_sem, w1q_sem, w1o_sem, w1_send, w2_recv, w2_send, sib_recv, sib_send,
    t_recv, t_send, e_recv, e_send, rx_recv, rx_send, ax_recv, ax_send,
    r_recv, r_send, s_recv, s_send,
):
    V, T = X * Z, Y * C
    Xc = X // C
    D = V * B
    K = Z * B
    v, t = lax.axis_index("vocab"), lax.axis_index("tok")
    x, z = v // Z, v % Z
    y, c = t // C, t % C
    cap = 2 * B // T
    R = T * cap

    def dev(xx, zz, yy, cc):
        return (xx * Z + zz, yy * C + cc)

    def far_first(i, size):
        return size // 2 + ((i + 1) // 2) * (1 - 2 * (i % 2))

    def remote(src, dst, send, recv, device):
        return pltpu.make_async_remote_copy(
            src_ref=src, dst_ref=dst, send_sem=send, recv_sem=recv,
            device_id=device, device_id_type=MESH,
        )

    pending = []

    def finish():
        for done in pending:
            done()
        pending.clear()

    def wait_bytes(ref, sem):
        pltpu.make_async_copy(ref, ref, sem).wait()

    def step_of(way):
        return 1 if way == 0 else Y - 1

    half_up, half_down = Y // 2, Y - 1 - Y // 2

    def hops_of(i, way):
        return half_up if way == i % 2 else half_down

    wanted_here = (
        (tok_hbm, tok_ref), (rep_hbm, rep_ref), (mask_hbm, mask_ref),
        (wq_hbm, wq_ref), (wo_hbm, wod_src.at[:, pl.ds(0, B)]),
        (wd_hbm, wod_src.at[:, pl.ds(B, B)]), (emb_hbm, emb),
        (gain_hbm, gain_ref), (hw_hbm, hw_ref), (lab_hbm, lab_ref), (seg_hbm, seg_ref),
    )
    copies = [
        pltpu.make_async_copy(src, dst, in_sem.at[i]) for i, (src, dst) in enumerate(wanted_here)
    ]
    for copy in copies:
        copy.start()
    barrier = pltpu.get_barrier_semaphore()

    def greet_vocab(d, carry):
        pl.semaphore_signal(barrier, inc=1, device_id=((v + d) % V, t), device_id_type=MESH)
        return carry

    def greet_tok(d, carry):
        pl.semaphore_signal(barrier, inc=1, device_id=(v, (t + d) % T), device_id_type=MESH)
        return carry

    lax.fori_loop(1, V, greet_vocab, 0)
    lax.fori_loop(1, T, greet_tok, 0)
    turn = y // (Z // X)
    same_core = (x // Xc) == c
    from_core = ((x + turn) % X) // Xc
    other_source = from_core != c

    @pl.when(jnp.logical_not(same_core))
    def _():
        for i in range(Xc):
            to = dev((Xc * c + i + X - turn) % X, z, y, x // Xc)
            pl.semaphore_signal(barrier, inc=1, device_id=to, device_id_type=MESH)

    @pl.when(other_source)
    def _():
        for i in range(Xc):
            to = dev(Xc * c + i, z, y, from_core)
            pl.semaphore_signal(barrier, inc=1, device_id=to, device_id_type=MESH)

    ways = [way for way in (0, 1) if hops_of(0, way) >= 1]
    for way in ways:
        ahead, behind = (y + step_of(way)) % Y, (y + Y - step_of(way)) % Y
        sender = ((x + behind // (Z // X)) % X) // Xc
        for i in range(Xc):
            for to in (
                dev((Xc * c + i + X - turn) % X, z, ahead, x // Xc),
                dev(Xc * c + i, z, behind, sender),
            ):
                pl.semaphore_signal(barrier, inc=1, device_id=to, device_id_type=MESH)

    for copy in copies[:3]:
        copy.wait()
    chosen = jnp.where(mask_ref[...] == 1, rep_ref[...], tok_ref[...])
    owner = chosen // vocab_rows
    offset = (chosen - owner * vocab_rows).astype(F32)
    owner_f = owner.astype(F32)
    earlier = iota((B, B), 0) < iota((B, B), 1)
    same_owner = row_to_square(owner_f) == owner_f
    slot = jnp.sum(jnp.where(same_owner & earlier, 1.0, 0.0), axis=0, keepdims=True)
    place = owner_f * float(cap) + slot
    place_hot = iota((R, B), 0).astype(F32) == place
    wanted = jnp.sum(jnp.where(place_hot, offset, 0.0), axis=1, keepdims=True)
    ids_src[...] = jnp.broadcast_to(wanted, (R, B)).reshape(T, cap, B)

    pl.semaphore_wait(
        barrier,
        V - 1 + T - 1 + 2 * Xc * len(ways)
        + Xc * jnp.where(same_core, 0, 1)
        + Xc * jnp.where(other_source, 1, 0),
    )

    def tok_start(src, buf, n):
        buf[t] = src[t]

        def send(i, carry):
            cd = (c + C - 1 - i % C) % C
            to = (y + far_first(i // C, Y)) % Y * C + cd
            remote(src.at[to], buf.at[t], t_send.at[n], t_recv.at[n], (v, to)).start()
            return carry

        lax.fori_loop(0, T - 1, send, 0)
        pending.append(lambda: wait_bytes(src.at[pl.ds(0, T - 1)], t_send.at[n]))

    def tok_wait(src, buf, n):
        wait_bytes(buf.at[pl.ds(0, T - 1)], t_recv.at[n])

    tok_start(ids_src, ids_buf, 0)

    def w1_each(act):
        first, cd = pl.multiple_of(y * B, B), x // Xc
        for a, (src, dst) in enumerate(((wq_ref, Wq), (wod_src, Wod))):
            for i in range(Xc):
                xd = (Xc * c + i + X - turn) % X
                mine = (xd == x) & same_core
                piece, place_ = src.at[pl.ds(i * B, B)], dst.at[x, pl.ds(first, B)]
                for way in ways if a == 0 else ():
                    to = dev(xd, z, (y + step_of(way)) % Y, cd)
                    act(None, piece, place_, w1q_sem.at[1 + way], w1_send.at[i, 2 + way], to)
                sem = w1q_sem.at[0] if a == 0 else w1o_sem
                act(mine, piece, place_, sem, w1_send.at[i, a], dev(xd, z, y, cd))

    def w1_go(mine, src, dst, sem, send, device):
        if mine is None:
            remote(src, dst, send, sem, device).start()
            return

        @pl.when(mine)
        def _():
            pltpu.make_async_copy(src, dst, sem).start()

        @pl.when(jnp.logical_not(mine))
        def _():
            remote(src, dst, send, sem, device).start()

    def w1_end(mine, src, dst, sem, send, device):
        if mine is None:
            wait_bytes(src, send)
            return

        @pl.when(jnp.logical_not(mine))
        def _():
            wait_bytes(src, send)

    for copy in copies[3:6]:
        copy.wait()
    w1_each(w1_go)
    pending.append(lambda: w1_each(w1_end))
    pending.append(lambda: w2_done())

    arrays = (Wq, Wod)
    def block_of(a, i, k):
        return arrays[a].at[Xc * c + i, pl.ds(pl.multiple_of(k * B, B), B)]

    def hop(a, i, h, way):
        step = 1 if way == 0 else Y - 1
        ref = block_of(a, i, (y + (Y - step) * (h - 1)) % Y)
        return remote(
            ref, ref, w2_send.at[a, i], w2_recv.at[a, i, way, h - 1],
            dev(x, z, (y + step) % Y, c),
        )

    def sibling(a, i, k):
        ref = block_of(a, i, k)
        return remote(
            ref, ref, sib_send.at[a, i], sib_recv.at[a, i], dev(x, z, y, (c + 1) % C)
        )

    def w2_first():
        whole = Wq.at[pl.ds(0, Xc), pl.ds(0, B)]
        for way in ways:
            wait_bytes(whole, w1q_sem.at[1 + way])
            for i in range(Xc):
                if hops_of(i, way) >= 2:
                    hop(0, i, 2, way).start()
        wait_bytes(whole, w1q_sem.at[0])
        for i in range(Xc):
            sibling(0, i, y).start()
            for way in ways:
                sibling(0, i, (y + Y - step_of(way)) % Y).start()

    def w2_begin(a):
        wait_bytes(Wod.at[pl.ds(0, Xc), pl.ds(0, B)], w1o_sem)
        for i in range(Xc):
            for way in (0, 1):
                if hops_of(i, way) >= 1:
                    hop(a, i, 1, way).start()
        for i in range(Xc):
            sibling(a, i, y).start()

    def w2_forward(a, i, h):
        if i >= Xc:
            return
        for way in (0, 1):
            if h <= hops_of(i, way):
                hop(a, i, h, way).wait_recv()
                if h + 1 <= hops_of(i, way):
                    hop(a, i, h + 1, way).start()
        for way in (0, 1):
            if h <= hops_of(i, way):
                step = 1 if way == 0 else Y - 1
                sibling(a, i, (y + (Y - step) * h) % Y).start()

    def w2_ready(a):
        for i in range(Xc):
            wait_bytes(arrays[a].at[0], sib_recv.at[a, i])

    def w2_done():
        for a in (0, 1):
            for i in range(Xc):
                sent = Y - 1 - (len(ways) if a == 0 else 0)
                if sent:
                    wait_bytes(arrays[a].at[0, pl.ds(0, sent * B)], w2_send.at[a, i])
                wait_bytes(arrays[a].at[0], sib_send.at[a, i])

    row = (z + X - x) % X
    at_home = x == row

    whole_rows, H = pl.ds(0, B), B // 2
    halves = [(0, pl.ds(0, H)), (1, pl.ds(H, H))]

    def block_done(ref, sem, rows):
        @pl.when(at_home)
        def _():
            wait_bytes(ref.at[pl.ds(0, Z - 1), rows], sem)

        @pl.when(jnp.logical_not(at_home))
        def _():
            wait_bytes(ref.at[pl.ds(0, Z), rows], sem)

    def row_start(src, buf, n, rows=whole_rows):
        k = v // X
        for j in range(Z):
            zd = (z + far_first(j, Z)) % Z
            mine = at_home & (zd == z)

            @pl.when(mine)
            def _():
                pltpu.make_async_copy(src.at[rows], buf.at[k, rows], e_recv.at[n]).start()

            @pl.when(jnp.logical_not(mine))
            def _():
                to = dev(row, zd, y, c)
                remote(src.at[rows], buf.at[k, rows], e_send.at[n], e_recv.at[n], to).start()

        pending.append(lambda: block_done(buf, e_send.at[n], rows))

    def row_wait(buf, n, rows=whole_rows):
        wait_bytes(buf.at[pl.ds(0, Z), rows], e_recv.at[n])

    def rx_start(left, weights, part, buf, n, rows=whole_rows):
        for d in [far_first(i, X) for i in range(X)]:
            to = (x + d) % X
            part[to, rows] = dot(left, weights(to)).astype(BF)
            if d:
                remote(
                    part.at[to, rows], buf.at[d - 1, rows], rx_send.at[n], rx_recv.at[n],
                    dev(to, z, y, c),
                ).start()
        pending.append(lambda: wait_bytes(buf.at[pl.ds(0, X - 1), rows], rx_send.at[n]))

    def rx_sum(part, buf, n, rows=whole_rows):
        wait_bytes(buf.at[pl.ds(0, X - 1), rows], rx_recv.at[n])
        total = part[x, rows].astype(F32)
        for d in range(1, X):
            total = total + buf[d - 1, rows].astype(F32)
        return total

    def ax_start(buf, n, rows=whole_rows):
        for d in [far_first(i, X) for i in range(X - 1)]:
            remote(
                buf.at[x, rows], buf.at[x, rows], ax_send.at[n], ax_recv.at[n],
                dev((x + d) % X, z, y, c),
            ).start()
        pending.append(lambda: wait_bytes(buf.at[pl.ds(0, X - 1), rows], ax_send.at[n]))

    def ax_wait(buf, n, rows=whole_rows):
        wait_bytes(buf.at[pl.ds(0, X - 1), rows], ax_recv.at[n])

    def own_start(part, buf, n, rows):
        for j in range(Z):
            zd = (z + far_first(j, Z)) % Z
            xd = (zd % X + X - x) % X
            k = xd * (Z // X) + zd // X
            mine = (xd == x) & (zd == z)

            @pl.when(mine)
            def _():
                pltpu.make_async_copy(part.at[k, rows], buf.at[z, rows], r_recv.at[n]).start()

            @pl.when(jnp.logical_not(mine))
            def _():
                to = dev(xd, zd, y, c)
                remote(
                    part.at[k, rows], buf.at[z, rows], r_send.at[n], r_recv.at[n], to
                ).start()

        pending.append(lambda: block_done(part, r_send.at[n], rows))

    def own_sum(buf, n, rows=whole_rows):
        wait_bytes(buf.at[pl.ds(0, Z), rows], r_recv.at[n])
        total = buf[0, rows].astype(F32)
        for k in range(1, Z):
            total = total + buf[k, rows].astype(F32)
        return total

    def spread_back(left, weights, part, buf, n, rows=whole_rows, seen=None):
        step = 2
        for first in range(0, Z, step):
            total = None
            for xx in range(X):
                term = dot_nt(left(xx), weights(xx, pl.ds(first * B, step * B)))
                total = term if total is None else total + term
            for k in range(first, first + step):
                part[k, rows] = total[:, (k - first) * B : (k - first + 1) * B].astype(BF)
        if seen is not None:
            seen()
        own_start(part, buf, n, rows)

    def ar_start(rows, n):
        ar_src[n] = rows
        ar_buf[n, 0] = rows

        def send(i, carry):
            to = dev((x + far_first(i % X, X)) % X, (z + far_first(i // X, Z)) % Z, y, c)
            remote(ar_src.at[n], ar_buf.at[n, i + 1], s_send.at[n], s_recv.at[n], to).start()
            return carry

        lax.fori_loop(0, V - 1, send, 0)
        pending.append(lambda: wait_bytes(ar_buf.at[n, pl.ds(1, V - 1)], s_send.at[n]))

    def ar_sum(n):
        wait_bytes(ar_buf.at[n, pl.ds(1, V - 1)], s_recv.at[n])
        return rows_to_square(jnp.sum(ar_buf[n], axis=0))

    for copy in copies[6:]:
        copy.wait()
    hw_buf[x] = jnp.broadcast_to(hw_ref[...].astype(F32), (16, B)).astype(BF)
    ax_start(hw_buf, 3, pl.ds(0, 16))
    put_hot = jnp.where(place_hot, 1.0, 0.0).astype(BF)
    place_square = row_to_square(place)
    take_hot = jnp.concatenate(
        [
            jnp.where(place_square == (iota((B, B), 1) + first).astype(F32), 1.0, 0.0)
            for first in range(0, R, B)
        ],
        axis=1,
    ).astype(BF)
    segment_f = seg_ref[...].astype(F32)
    same_segment = row_to_square(segment_f) == segment_f
    labels = row_to_square(lab_ref[...].astype(F32))[:, 0:1]
    gain = gain_ref[...].astype(F32)
    head_vector = hw_ref[...].astype(F32)
    g_src[...] = jnp.broadcast_to(gain, (16, B)).astype(BF)
    row_start(g_src, g_all, 3, pl.ds(0, 16))
    tok_wait(ids_src, ids_buf, 0)
    requested = ids_buf[...].reshape(R, B)
    chunk = 512


    def fetch(i, total):
        base = i * chunk
        hot = jnp.concatenate(
            [
                jnp.where(
                    requested == (iota((R, B), 1) + (base + first)).astype(F32), 1.0, 0.0
                ).astype(BF)
                for first in range(0, chunk, B)
            ],
            axis=1,
        )
        return total + dot(hot, emb[pl.ds(pl.multiple_of(base, chunk), chunk), :])

    fetched = lax.fori_loop(0, vocab_rows // chunk, fetch, jnp.zeros((R, B), F32))
    row_src[...] = fetched.astype(BF).reshape(T, cap, B)
    tok_start(row_src, row_buf, 1)
    row_sums = []
    for first in range(0, R, B):
        piece = fetched[first : first + B]
        row_sums.append(jnp.sum(piece, axis=1, keepdims=True))
        row_sums.append(jnp.sum(piece * piece, axis=1, keepdims=True))
    ar_start(columns_to_rows(row_sums), 0)
    w2_first()
    tok_wait(row_src, row_buf, 1)
    features = dot(take_hot, row_buf[...].reshape(R, B))
    x_src[...] = features.astype(BF)
    row_start(x_src, x_buf, 0)
    w2_forward(0, 0, 2)
    w2_forward(0, 1, 2)
    stats = ar_sum(0)
    lane = iota((B, B), 1)
    for first in range(0, R, B):
        i = 2 * (first // B)
        pair = jnp.where(lane == 0, stats[:, i : i + 1], stats[:, i + 1 : i + 2])
        st_src[first // cap : (first + B) // cap] = pair.reshape(B // cap, cap, B)
    tok_start(st_src, st_buf, 3)
    for first in range(0, R, B):
        req_out[:, first : first + B] = requested[first : first + B].T[:8]
    w2_forward(0, 0, 3)
    w2_forward(0, 1, 3)
    w2_begin(1)
    tok_wait(st_src, st_buf, 3)
    stats = jnp.dot(
        take_hot.astype(F32),
        st_buf[...].reshape(R, B),
        preferred_element_type=F32,
        precision=lax.Precision.HIGHEST,
    )
    row_mean = stats[:, 0:1] / D
    variance = stats[:, 1:2] / D - row_mean * row_mean
    inv_std = lax.rsqrt(variance + epsilon)
    centered = (features - row_mean) * inv_std
    row_wait(g_all, 3, pl.ds(0, 16))
    row_wait(x_buf, 0)
    for k in range(Z):
        block = x_buf[k].astype(F32)
        block_gain = g_all[k].astype(F32)[0:8]
        gains[k] = block_gain
        normed = ((block - row_mean) * inv_std) * block_gain[0:1]
        cgain[k] = normed
        nrm[:, k * B : (k + 1) * B] = normed.astype(BF)
    w2_forward(0, 0, 4)
    w2_forward(0, 1, 4)
    w2_forward(1, 0, 1)
    w2_forward(1, 1, 1)
    w2_ready(0)
    rx_start(nrm[...], lambda to: Wq[to], pq, pq_buf, 0)
    w2_forward(1, 0, 2)
    w2_forward(1, 1, 2)
    qkv = rx_sum(pq, pq_buf, 0).astype(BF)
    queries, keys, values = qkv[:, :B], qkv[:, B : 2 * B], qkv[:, 2 * B :]
    raw = dot_nt(queries, keys) / math.sqrt(B)
    capped = soft_limit * jnp.tanh(raw / soft_limit)
    exps = jnp.where(same_segment, jnp.exp(capped), 0.0)
    probabilities = exps / jnp.sum(exps, axis=-1, keepdims=True)
    prob_rounded = probabilities.astype(BF)
    h_src[...] = dot(prob_rounded, values).astype(BF)
    for n, rows in halves:
        row_start(h_src, h_buf, 1 + 3 * n, rows)
    for h in (3, 4):
        w2_forward(1, 0, h)
        w2_forward(1, 1, h)
    w2_ready(1)

    for n, rows in halves:
        row_wait(h_buf, 1 + 3 * n, rows)
        heads_row = jnp.concatenate([h_buf[k, rows] for k in range(Z)], axis=1)
        rx_start(heads_row, lambda to: Wod[to, :, 0:B], po, po_buf, 1 + 2 * n, rows)
    for n, rows in halves:
        hidden = features[n * H : (n + 1) * H] + rx_sum(po, po_buf, 1 + 2 * n, rows)
        d_src[rows] = hidden.astype(BF)
        row_start(d_src, d_buf, 2 + 3 * n, rows)

    for n, rows in halves:
        row_wait(d_buf, 2 + 3 * n, rows)
        dense_row = jnp.concatenate([d_buf[k, rows] for k in range(Z)], axis=1)
        rx_start(dense_row, lambda to: Wod[to, :, B : 2 * B], pd, pd_buf, 2 + 2 * n, rows)
    dense_linear = jnp.concatenate(
        [rx_sum(pd, pd_buf, 2 + 2 * n, rows) for n, rows in halves], axis=0
    )
    dl_buf[x] = dense_linear
    activated = dense_linear * (0.5 * (1.0 + lax.erf(dense_linear * inv_root_two)))
    ar_start(
        columns_to_rows(
            [
                jnp.sum(activated, axis=1, keepdims=True),
                jnp.sum(activated * activated, axis=1, keepdims=True),
                jnp.sum(activated * head_vector, axis=1, keepdims=True),
                jnp.broadcast_to(jnp.sum(head_vector, axis=1, keepdims=True), (B, 1)),
            ]
        ),
        1,
    )
    ax_start(dl_buf, 0)
    ax_wait(hw_buf, 3, pl.ds(0, 16))
    ax_wait(dl_buf, 0)
    gelus = []
    for xx in range(X):
        linear = dl_buf[xx]
        phi = 0.5 * (1.0 + lax.erf(linear * inv_root_two))
        slope = phi + linear * jnp.exp(-0.5 * linear * linear) * inv_root_tau
        gelus.append((linear * phi, slope, hw_buf[xx].astype(F32)[0:1]))
    stats = ar_sum(1)
    head_mean = stats[:, 0:1] / D
    head_scale = lax.rsqrt(stats[:, 1:2] / D - head_mean * head_mean + epsilon)
    weight_sum = stats[:, 3:4]
    logits = head_scale * (stats[:, 2:3] - head_mean * weight_sum)
    logit_grads = loss_scale * (jax.nn.sigmoid(logits) - labels)
    mean_grads = logit_grads * weight_sum / D
    mean_product = logit_grads * logits / D
    for xx, (active, slope, vector) in enumerate(gelus):
        head_centered = (active - head_mean) * head_scale
        activated_grads = head_scale * (
            logit_grads * vector - mean_grads - head_centered * mean_product
        )
        pre[xx] = (activated_grads * slope).astype(BF)
    for n, rows in halves:
        spread_back(
            lambda xx: pre[xx, rows],
            lambda xx, part: Wod[xx, part, B : 2 * B],
            b1, b1_buf, 3 * n, rows,
        )
    pieces = []
    for n, rows in halves:
        pieces.append(own_sum(b1_buf, 3 * n, rows))
        hr_buf[x, rows] = pieces[n].astype(BF)
        ax_start(hr_buf, 1 + 3 * n, rows)
    for n, rows in halves:
        ax_wait(hr_buf, 1 + 3 * n, rows)
        spread_back(
            lambda xx: hr_buf[xx, rows],
            lambda xx, part: Wod[xx, part, 0:B],
            b2, b2_buf, 1 + 3 * n, rows,
        )
    hidden_grads = jnp.concatenate(pieces, axis=0)
    out_rounded = jnp.concatenate(
        [own_sum(b2_buf, 1 + 3 * n, rows) for n, rows in halves], axis=0
    ).astype(BF)

    prob_grads = dot_nt(out_rounded, values)
    value_grads = dot_tn(prob_rounded, out_rounded)
    capped_grads = probabilities * (
        prob_grads - jnp.sum(probabilities * prob_grads, axis=-1, keepdims=True)
    )
    ratio = capped / soft_limit
    score_rounded = (capped_grads * (1.0 - ratio * ratio) / math.sqrt(B)).astype(BF)
    query_grads = dot(score_rounded, keys)
    key_grads = dot_tn(score_rounded, queries)
    g_buf[x] = jnp.concatenate([query_grads, key_grads, value_grads], axis=1).astype(BF)
    ax_start(g_buf, 2)
    ax_wait(g_buf, 2)
    def send_sums():
        plain, weighted = jnp.zeros((B, B), F32), jnp.zeros((B, B), F32)
        for k in range(Z):
            block = b3[k].astype(F32)
            plain = plain + block * gains[k, 0:1]
            weighted = weighted + block * cgain[k]
        columns = [jnp.sum(total, axis=1, keepdims=True) for total in (plain, weighted)]
        ar_start(columns_to_rows(columns), 2)

    old = list(pending)
    pending.clear()

    def finish_old():
        for done in old:
            done()

    spread_back(lambda xx: g_buf[xx], lambda xx, rows: Wq[xx, rows, :], b3, b3_buf, 2, seen=send_sums)
    finish_old()
    scaled = own_sum(b3_buf, 2) * gain
    stats = ar_sum(2)
    input_grads = hidden_grads + inv_std * (
        scaled - stats[:, 0:1] / D - centered * (stats[:, 1:2] / D)
    )

    gslot_src[...] = dot(put_hot, input_grads.astype(BF)).astype(BF).reshape(T, cap, B)
    tok_start(gslot_src, gslot_buf, 2)
    tok_wait(gslot_src, gslot_buf, 2)
    grad_out[...] = gslot_buf[...].reshape(R, B)

    finish()


def table_kernel(tile, grad_ref, req_ref, out_ref):
    wanted = req_ref[0:1, :]
    group = jnp.floor(wanted * (1.0 / B))
    within = jnp.where(iota((B, wanted.shape[1]), 0).astype(F32) == wanted - group * B, 1.0, 0.0)
    within = within.astype(BF)
    grads = grad_ref[...]
    first = pl.program_id(0) * (tile // B)
    for g in range(tile // B):
        here = jnp.where(group == (first + g).astype(F32), 1.0, 0.0).astype(BF)
        out_ref[g * B : (g + 1) * B, :] = dot(within * here, grads).astype(BF)


def local(
    X, Z, Y, C,
    embeddings, norm_gain, query_key_value_weight, out_weight, dense_weight, head_weight,
    token_ids, replace_ids, masked, labels, segments,
):
    vocab_rows = embeddings.shape[0]
    V, T = X * Z, Y * C
    cap = 2 * B // T
    R = T * cap
    vm = pl.BlockSpec(memory_space=pltpu.VMEM)
    dma = pltpu.SemaphoreType.DMA
    rows = query_key_value_weight.shape[0]
    VM = pltpu.VMEM
    right = Y // 2
    grads, requests = pl.pallas_call(
        functools.partial(main_kernel, X, Z, Y, C, vocab_rows),
        out_shape=(
            jax.ShapeDtypeStruct((R, B), BF),
            jax.ShapeDtypeStruct((8, R), F32),
        ),
        in_specs=[pl.BlockSpec(memory_space=pltpu.HBM)] * 11,
        out_specs=(vm, vm),
        scratch_shapes=[
            VM((vocab_rows, B), BF),
            VM((rows, 3 * B), BF),
            VM((rows, 2 * B), BF),
            VM((X, Z * B, 3 * B), BF),
            VM((X, Z * B, 2 * B), BF),
            VM((1, B), jnp.int32), VM((1, B), jnp.int32), VM((1, B), jnp.int32),
            VM((1, B), BF), VM((1, B), BF),
            VM((1, B), jnp.int32), VM((1, B), jnp.int32),
            VM((T, cap, B), F32), VM((T, cap, B), F32),
            VM((T, cap, B), BF), VM((T, cap, B), BF),
            VM((T, cap, B), F32), VM((T, cap, B), F32),
            VM((T, cap, B), BF), VM((T, cap, B), BF),
            VM((16, B), BF), VM((Z, 16, B), BF),
            VM((B, B), BF), VM((Z, B, B), BF),
            VM((B, B), BF), VM((Z, B, B), BF),
            VM((B, B), BF), VM((Z, B, B), BF),
            VM((X, B, 3 * B), BF), VM((X - 1, B, 3 * B), BF),
            VM((X, B, B), BF), VM((X - 1, B, B), BF),
            VM((X, B, B), BF), VM((X - 1, B, B), BF),
            VM((Z, B, B), BF), VM((Z, B, B), BF),
            VM((X, B, B), BF), VM((Z, B, B), BF), VM((Z, B, B), BF),
            VM((X, B, 3 * B), BF), VM((Z, B, B), BF), VM((Z, B, B), BF),
            VM((B, Z * B), BF), VM((Z, B, B), F32), VM((Z, 8, B), F32),
            VM((X, B, B), F32), VM((X, B, B), BF), VM((X, 16, B), BF),
            VM((3, 8, B), F32), VM((3, V, 8, B), F32),
            dma((11,)), dma((3,)), dma(()), dma((X // C, 4)),
            dma((2, X // C, 2, right)), dma((2, X // C)),
            dma((2, X // C)), dma((2, X // C)),
            dma((4,)), dma((4,)), dma((6,)), dma((6,)),
            dma((5,)), dma((5,)), dma((5,)), dma((5,)),
            dma((5,)), dma((5,)), dma((3,)), dma((3,)),
        ],
        compiler_params=pltpu.CompilerParams(
            collective_id=0, has_side_effects=True, vmem_limit_bytes=60 * 1024 * 1024
        ),
    )(
        embeddings,
        norm_gain.reshape(1, B),
        query_key_value_weight.reshape(rows, 3 * B),
        out_weight,
        dense_weight,
        head_weight.reshape(1, B),
        token_ids, replace_ids, masked, labels, segments,
    )
    tile = min(4096, vocab_rows)
    return pl.pallas_call(
        functools.partial(table_kernel, tile),
        grid=(vocab_rows // tile,),
        out_shape=jax.ShapeDtypeStruct((vocab_rows, B), BF),
        in_specs=[
            pl.BlockSpec((R, B), lambda i: (0, 0)),
            pl.BlockSpec((8, R), lambda i: (0, 0)),
        ],
        out_specs=pl.BlockSpec((tile, B), lambda i: (i, 0)),
        compiler_params=pltpu.CompilerParams(vmem_limit_bytes=60 * 1024 * 1024),
    )(grads, requests)


def solution(mesh):
    V, T = mesh.shape["vocab"], mesh.shape["tok"]
    X = 4 if V == 32 else 2
    C = 2
    placed = (
        P("tok", "vocab"),
        P("vocab"),
        P("tok", "vocab", None),
        P("tok", "vocab"),
        P("tok", "vocab"),
        P("vocab"),
        P("tok", None),
        P("tok", None),
        P("tok", None),
        P("tok", None),
        P("tok", None),
    )
    return jax.shard_map(
        functools.partial(local, X, V // X, T // C, C),
        mesh=mesh, in_specs=placed, out_specs=P("tok", "vocab"), check_vma=False,
    )
```
